32 devices in a mesh: dp: 8 (over z, x), tensor: 4 (over y, core).
Axes of the slice: x: 2, y: 2, z: 4, core: 2. Of those that a mesh axis runs over, the one named last changes fastest.
Arguments:
- block_input: bfloat16 [8192, 1152], P('dp'), may hold values from -24 to 24
- conditions: float32 [32, 1152], replicated, may hold values from -6 to 6
- segment_ids: int32 [8, 1024], P('dp'), may hold values from 0 to 7, never falling along the last dimension, each value on 1 to 256 neighbouring positions
- segment_cond: int32 [8, 8], P('dp'), may hold values from 0 to 31
- cotangent: bfloat16 [8192, 1152], P('dp'), may hold values from -6 to 6
- qkv_weight: float32 [1152, 3, 1152], P('dp', None, 'tensor'), may hold values from -0.1875 to 0.1875
- proj_weight: float32 [1152, 1152], P(('tensor', 'dp')), may hold values from -1.5 to 1.5
- inner_weight: float32 [1152, 4608], P('dp', 'tensor'), may hold values from -0.1875 to 0.1875
- outer_weight: float32 [4608, 1152], P(('tensor', 'dp')), may hold values from -0.1875 to 0.1875
- ada_weight: float32 [6, 1152, 1152], P(None, 'tensor'), may hold values from -0.1875 to 0.1875
- head_biases: float32 [9, 1152], P(None, 'tensor'), may hold values from -1.8 to 1.8
- inner_bias: float32 [4608], P('tensor'), may hold values from -1.8 to 1.8
- shared_biases: float32 [2, 1152], replicated, may hold values from -1.8 to 1.8
- qkv_first: float32 [1152, 3, 1152], P('dp', None, 'tensor'), may hold values from -160 to 160
- proj_first: float32 [1152, 1152], P(('tensor', 'dp')), may hold values from -32 to 32
- inner_first: float32 [1152, 4608], P('dp', 'tensor'), may hold values from -256 to 256
- outer_first: float32 [4608, 1152], P(('tensor', 'dp')), may hold values from -192 to 192
- ada_first: float32 [6, 1152, 1152], P(None, 'tensor'), may hold values from -320 to 320
- head_biases_first: float32 [9, 1152], P(None, 'tensor'), may hold values from -384 to 384
- inner_bias_first: float32 [4608], P('tensor'), may hold values from -256 to 256
- shared_biases_first: float32 [2, 1152], replicated, may hold values from -384 to 384
- qkv_second: float32 [1152, 3, 1152], P('dp', None, 'tensor'), may hold values from 522.88 to 2092.8
- proj_second: float32 [1152, 1152], P(('tensor', 'dp')), may hold values from 20.928 to 83.648
- inner_second: float32 [1152, 4608], P('dp', 'tensor'), may hold values from 1105.92 to 4423.68
- outer_second: float32 [4608, 1152], P(('tensor', 'dp')), may hold values from 707.7888 to 2831.1553
- ada_second: float32 [6, 1152, 1152], P(None, 'tensor'), may hold values from 1966.08 to 7864.32
- head_biases_second: float32 [9, 1152], P(None, 'tensor'), may hold values from 2678.784 to 10706.944
- inner_bias_second: float32 [4608], P('tensor'), may hold values from 1105.92 to 4423.68
- shared_biases_second: float32 [2, 1152], replicated, may hold values from 2678.784 to 10706.944
Outputs:
- block_output: bfloat16 [8192, 1152], P(('dp', 'tensor'))
- input_grad: float32 [8192, 1152], P(('dp', 'tensor'))
- cond_grad: float32 [32, 1152], replicated
- qkv_updated: float32 [1152, 3, 1152], P('dp', None, 'tensor')
- proj_updated: float32 [1152, 1152], P(('tensor', 'dp'))
- inner_updated: float32 [1152, 4608], P('dp', 'tensor')
- outer_updated: float32 [4608, 1152], P(('tensor', 'dp'))
- ada_updated: float32 [6, 1152, 1152], P(None, 'tensor')
- head_biases_updated: float32 [9, 1152], P(None, 'tensor')
- inner_bias_updated: float32 [4608], P('tensor')
- shared_biases_updated: float32 [2, 1152], replicated
- qkv_first_new: float32 [1152, 3, 1152], P('dp', None, 'tensor')
- proj_first_new: float32 [1152, 1152], P(('tensor', 'dp'))
- inner_first_new: float32 [1152, 4608], P('dp', 'tensor')
- outer_first_new: float32 [4608, 1152], P(('tensor', 'dp'))
- ada_first_new: float32 [6, 1152, 1152], P(None, 'tensor')
- head_biases_first_new: float32 [9, 1152], P(None, 'tensor')
- inner_bias_first_new: float32 [4608], P('tensor')
- shared_biases_first_new: float32 [2, 1152], replicated
- qkv_second_new: float32 [1152, 3, 1152], P('dp', None, 'tensor')
- proj_second_new: float32 [1152, 1152], P(('tensor', 'dp'))
- inner_second_new: float32 [1152, 4608], P('dp', 'tensor')
- outer_second_new: float32 [4608, 1152], P(('tensor', 'dp'))
- ada_second_new: float32 [6, 1152, 1152], P(None, 'tensor')
- head_biases_second_new: float32 [9, 1152], P(None, 'tensor')
- inner_bias_second_new: float32 [4608], P('tensor')
- shared_biases_second_new: float32 [2, 1152], replicated
- qkv_copy: bfloat16 [1152, 3, 1152], P('dp', None, 'tensor')
- projection_bfloat_copy: bfloat16 [1152, 1152], P(('tensor', 'dp'))
- inner_copy: bfloat16 [1152, 4608], P('dp', 'tensor')
- outer_copy: bfloat16 [4608, 1152], P(('tensor', 'dp'))
The draws below stay inside these ranges and needn't reach their ends.
Inputs may be any that keep to these rules, and one draw needn't show every extreme that they name: `segment_ids`: in each row segment numbers start at 0 and never fall; each of the 8 images holds at most 256 positions.
All inputs are finite; a program needn't handle non-finite values.
Results may differ from the reference program's by a relative error of at most 0.018.
The reference program's roundings to bfloat16 on the way count: a program that leaves them out, or rounds other values in their place, can miss the bound.
Values may be sent and summed in bfloat16 or wider, within the bound.
A program may use at most 256 MiB of HBM per device.

```python
import math
import jax
import jax.numpy as jnp
import numpy as np
from jax import lax

D = 1152
H = 16
HD = 72
FF = 4608
ROW = 1024
SEG_ROW = 8
SEG_MOST = 256
CONDS = 32
STEP = 10
ROWS = 8
TOKENS = 8192


def draw_block_input(key, part):
    key_values, key_rows, key_columns = jax.random.split(key, 3)
    values = jnp.clip(jax.random.normal(key_values, (TOKENS, D), jnp.float32), -4.0, 4.0)
    row_scale = jnp.exp(jax.random.uniform(key_rows, (TOKENS, 1), jnp.float32, math.log(0.3), math.log(3.0)))
    column_scale = jnp.exp(jax.random.uniform(key_columns, (1, D), jnp.float32, math.log(0.5), math.log(2.0)))
    return (values * row_scale * column_scale).astype(jnp.bfloat16)


def place_ends(entries, own_key, smallest, largest):
    place = [jax.random.randint(jax.random.fold_in(own_key, axis), (), 0, length) for axis, length in enumerate(entries.shape)]
    longest = entries.shape.index(max(entries.shape))
    neighbour = place[:longest] + [(place[longest] + 1) % entries.shape[longest]] + place[longest + 1:]
    return entries.at[tuple(place)].set(smallest).at[tuple(neighbour)].set(largest)


def steps_of(own_key, shape, cuts, smallest, largest):
    level, own = 1.0, jax.random.fold_in(own_key, 6)
    for position, shards_of in cuts:
        heights = jnp.exp(jax.random.uniform(jax.random.fold_in(own, position), (shards_of,), jnp.float32, smallest / len(cuts), largest / len(cuts)))
        level = level * jnp.repeat(heights, shape[position] // shards_of).reshape([-1 if axis == position else 1 for axis in range(len(shape))])
    return level


def length_profile(count, total, reach, slope):
    portions = [(1 << 20) // math.isqrt(standing ** slope) + 1 for standing in range(2, count + 1)]
    spare, given = total - reach - (count - 1), [1] * (count - 1)
    while spare > 0:
        candidates = [i for i in range(count - 1) if given[i] < reach]
        whole, budget = sum([portions[i] for i in candidates]), spare
        for i in candidates:
            more = min(reach - given[i], max(1, budget * portions[i] // whole), spare)
            given[i] = given[i] + more
            spare = spare - more
    return np.array([reach] + given)


def uneven_parts(rng, number_of, total, reach, slope):
    if number_of == 2:
        one = jax.random.randint(rng, (), max(1, total - reach), min(reach, total - 1) + 1)
        return jnp.stack([one, total - one])
    lengths = jnp.asarray(length_profile(number_of, total, reach, slope), jnp.int32)
    pairs = (number_of - 1) // 2
    source_of, receiver = lengths[1:1 + 2 * pairs:2], lengths[2:2 + 2 * pairs:2]
    margin = jnp.minimum(source_of - 1, reach - receiver)
    passed = jax.random.randint(jax.random.fold_in(rng, 1), (pairs,), 0, 1 << 20) % (margin + 1)
    lengths = lengths.at[1:1 + 2 * pairs:2].set(source_of - passed).at[2:2 + 2 * pairs:2].set(receiver + passed)
    return lengths[jax.random.permutation(jax.random.fold_in(rng, 2), number_of)]


def bell_draw(own_key, extent, spread, reach, cuts=(), dtype=jnp.bfloat16):
    factor_of = steps_of(own_key, extent, cuts, -0.22, 0.18) if cuts else 1.0
    drawn = jax.random.normal(own_key, extent, jnp.float32) * spread * factor_of
    return jnp.minimum(jnp.maximum(drawn, -reach), reach).astype(dtype)


def setup_inputs(seed: int = 0) -> dict:
    seeds = jax.random.split(jax.random.key(seed), 30)
    return {
        "block_input": draw_block_input(jax.random.fold_in(seeds[29], 71), 0),
        "conditions": bell_draw(seeds[1], (CONDS, D), 1.0, 6.0, (), jnp.float32),
        "segment_ids": jax.vmap(lambda own: jnp.searchsorted(jnp.cumsum(uneven_parts(own, SEG_ROW, ROW, SEG_MOST, 1)), jnp.arange(ROW), side="right"))(jax.random.split(seeds[2], ROWS)).reshape((ROWS, ROW)).astype(jnp.int32),
        "segment_cond": place_ends(jax.random.randint(seeds[3], (ROWS, SEG_ROW), 0, CONDS), jax.random.fold_in(seeds[3], 1), 0, CONDS - 1).astype(jnp.int32),
        "cotangent": bell_draw(seeds[4], (TOKENS, D), 1.0, 6.0, ((0, 8),)),
        "qkv_weight": bell_draw(seeds[5], (D, 3, D), D ** -0.5, 0.1875, ((0, 8), (2, 4)), jnp.float32),
        "proj_weight": bell_draw(seeds[6], (D, D), (D // 64) ** -0.5, 1.5, ((0, 32),), jnp.float32),
        "inner_weight": bell_draw(seeds[7], (D, FF), D ** -0.5, 0.1875, ((0, 8), (1, 4)), jnp.float32),
        "outer_weight": bell_draw(seeds[8], (FF, D), (FF // 4) ** -0.5, 0.1875, ((0, 32),), jnp.float32),
        "ada_weight": bell_draw(seeds[9], (6, D, D), D ** -0.5, 0.1875, ((1, 4),), jnp.float32),
        "head_biases": bell_draw(seeds[10], (9, D), 0.3, 1.8, ((1, 4),), jnp.float32),
        "inner_bias": bell_draw(seeds[11], (FF,), 0.3, 1.8, ((0, 4),), jnp.float32),
        "shared_biases": bell_draw(seeds[12], (2, D), 0.3, 1.8, (), jnp.float32),
        "qkv_first": bell_draw(seeds[13], (D, 3, D), (3.5 * (SEG_ROW * TOKENS / ROW) ** 0.5), 160.0, ((0, 8), (2, 4)), jnp.float32),
        "proj_first": bell_draw(seeds[14], (D, D), (0.7 * (SEG_ROW * TOKENS / ROW) ** 0.5), 32.0, ((0, 32),), jnp.float32),
        "inner_first": bell_draw(seeds[15], (D, FF), (0.45 * TOKENS ** 0.5), 256.0, ((0, 8), (1, 4)), jnp.float32),
        "outer_first": bell_draw(seeds[16], (FF, D), (0.36 * TOKENS ** 0.5), 192.0, ((0, 32),), jnp.float32),
        "ada_first": bell_draw(seeds[17], (6, D, D), (0.6 * TOKENS ** 0.5), 320.0, ((1, 4),), jnp.float32),
        "head_biases_first": bell_draw(seeds[18], (9, D), (0.7 * TOKENS ** 0.5), 384.0, ((1, 4),), jnp.float32),
        "inner_bias_first": bell_draw(seeds[19], (FF,), (0.45 * TOKENS ** 0.5), 256.0, ((0, 4),), jnp.float32),
        "shared_biases_first": bell_draw(seeds[20], (2, D), (0.7 * TOKENS ** 0.5), 384.0, (), jnp.float32),
        "qkv_second": jnp.clip(jnp.exp(math.log(2092.8) - 1.3869062 * jax.random.uniform(seeds[21], (D, 3, D), jnp.float32) ** steps_of(seeds[21], (D, 3, D), ((0, 8), (2, 4)), -0.2, 0.2)), 522.88, 2092.8),
        "proj_second": jnp.clip(jnp.exp(math.log(83.648) - 1.3855296 * jax.random.uniform(seeds[22], (D, D), jnp.float32) ** steps_of(seeds[22], (D, D), ((0, 32),), -0.2, 0.2)), 20.928, 83.648),
        "inner_second": jnp.clip(jnp.exp(math.log(4423.68) - 1.3862944 * jax.random.uniform(seeds[23], (D, FF), jnp.float32) ** steps_of(seeds[23], (D, FF), ((0, 8), (1, 4)), -0.2, 0.2)), 1105.92, 4423.68),
        "outer_second": jnp.clip(jnp.exp(math.log(2831.1553) - 1.3862944 * jax.random.uniform(seeds[24], (FF, D), jnp.float32) ** steps_of(seeds[24], (FF, D), ((0, 32),), -0.2, 0.2)), 707.7888, 2831.1553),
        "ada_second": jnp.clip(jnp.exp(math.log(7864.32) - 1.3862944 * jax.random.uniform(seeds[25], (6, D, D), jnp.float32) ** steps_of(seeds[25], (6, D, D), ((1, 4),), -0.2, 0.2)), 1966.08, 7864.32),
        "head_biases_second": jnp.clip(jnp.exp(math.log(10706.944) - 1.3855296 * jax.random.uniform(seeds[26], (9, D), jnp.float32) ** steps_of(seeds[26], (9, D), ((1, 4),), -0.2, 0.2)), 2678.784, 10706.944),
        "inner_bias_second": jnp.clip(jnp.exp(math.log(4423.68) - 1.3862944 * jax.random.uniform(seeds[27], (FF,), jnp.float32) ** steps_of(seeds[27], (FF,), ((0, 4),), -0.2, 0.2)), 1105.92, 4423.68),
        "shared_biases_second": jnp.clip(jnp.exp(jax.random.uniform(seeds[28], (2, D), jnp.float32, math.log(2678.784), math.log(10706.944))), 2678.784, 10706.944),
    }


BETA_ONE = 0.5
BETA_TWO = 0.6
ADAM_EPS = 1e-08
DECAY = 0.01
NORM_EPSILON = 1e-06
RATES = (0.04, 0.3, 0.04, 0.04, 0.04, 0.4, 0.4, 0.4)
PRECISION_MAX = lax.Precision.HIGHEST

@jax.custom_vjp
def low(v):
    return lax.optimization_barrier(v.astype(jnp.bfloat16)).astype(jnp.float32)

@jax.custom_vjp
def low_back(v):
    return v

def low_keep(v):
    return (low(v), None)

def low_pass(kept, grad):
    return (grad,)

def back_keep(v):
    return (v, None)

def back_low(kept, grad):
    return (low(grad),)
low.defvjp(low_keep, low_pass)
low_back.defvjp(back_keep, back_low)

def silu(values):
    return values / (1.0 + jnp.exp(-values))

def gelu_tanh(values):
    inner = math.sqrt(2.0 / math.pi) * (values + 0.044715 * values * values * values)
    return 0.5 * values * (1.0 + jnp.tanh(inner))

def normalize(values):
    centered = values - lax.optimization_barrier(jnp.mean(values, axis=-1, keepdims=True))
    inv_std = lax.rsqrt(lax.optimization_barrier(jnp.mean(centered * centered, axis=-1, keepdims=True)) + NORM_EPSILON)
    return centered * inv_std

def attend_row(pieces):
    row_qkv, row_segments = pieces
    queries = row_qkv[:, 0]
    keys = row_qkv[:, 1]
    values = row_qkv[:, 2]
    scores = jnp.einsum('qhe,khe->hqk', queries, keys, precision=PRECISION_MAX) * (1.0 / math.sqrt(HD))
    scores = low_back(scores)
    same = row_segments[:, None] == row_segments[None, :]
    scores = jnp.where(same[None], scores, -1e+30)
    top = lax.optimization_barrier(jnp.max(scores, axis=-1, keepdims=True))
    expo = jnp.exp(scores - top)
    probs = low(expo / lax.optimization_barrier(jnp.sum(expo, axis=-1, keepdims=True)))
    return jnp.einsum('hqk,khe->qhe', probs, values, precision=PRECISION_MAX)

def forward(inputs, conditions, qkv_weight, proj_weight, inner_weight, outer_weight, ada_weight, head_biases, inner_bias, shared_biases, segment_ids, segment_cond):
    row_count = segment_ids.shape[0]
    row_length = segment_ids.shape[1]
    token_count = inputs.shape[0]
    width = inputs.shape[1]
    condition_row_block = conditions[segment_cond]
    modulation = jnp.einsum('rsd,kcd->rskc', silu(condition_row_block), ada_weight, precision=PRECISION_MAX) + head_biases[3:][None, None]
    per_token = modulation[jnp.arange(row_count)[:, None], segment_ids].reshape(token_count, 6, width)
    hidden_one = low(normalize(inputs) * (1.0 + per_token[:, 1]) + per_token[:, 0])
    qkv = jnp.einsum('nd,dkc->nkc', hidden_one, low(qkv_weight), precision=PRECISION_MAX) + head_biases[:3][None]
    qkv = low_back(low(qkv))
    heads = qkv.reshape(row_count, row_length, 3, H, HD)
    attended = lax.map(jax.checkpoint(attend_row), (heads, segment_ids))
    attended = low_back(low(attended.reshape(token_count, width)))
    branch_one = low_back(jnp.dot(attended, low(proj_weight), precision=PRECISION_MAX) + shared_biases[0])
    middle = inputs + per_token[:, 2] * branch_one
    hidden_two = low(normalize(middle) * (1.0 + per_token[:, 4]) + per_token[:, 3])
    pre_act = low_back(jnp.dot(hidden_two, low(inner_weight), precision=PRECISION_MAX) + inner_bias)
    act_values = low(gelu_tanh(pre_act))
    branch_two = low_back(jnp.dot(act_values, low(outer_weight), precision=PRECISION_MAX) + shared_biases[1])
    return middle + per_token[:, 5] * branch_two

def adam_update(weight, grad, first, second, rate):
    first_new = BETA_ONE * first + (1.0 - BETA_ONE) * grad
    second_new = BETA_TWO * second + (1.0 - BETA_TWO) * grad * grad
    fix_one = 1.0 - BETA_ONE ** STEP
    fix_two = 1.0 - BETA_TWO ** STEP
    update = first_new / fix_one / (jnp.sqrt(second_new / fix_two) + ADAM_EPS)
    return (weight - rate * (update + DECAY * weight), first_new, second_new)

def reference(block_input, conditions, segment_ids, segment_cond, cotangent, qkv_weight, proj_weight, inner_weight, outer_weight, ada_weight, head_biases, inner_bias, shared_biases, qkv_first, proj_first, inner_first, outer_first, ada_first, head_biases_first, inner_bias_first, shared_biases_first, qkv_second, proj_second, inner_second, outer_second, ada_second, head_biases_second, inner_bias_second, shared_biases_second):

    def wrapped(inputs, conds, weight_a, weight_b, weight_c, weight_d, weight_e, bias_a, bias_b, bias_c):
        return forward(inputs, conds, weight_a, weight_b, weight_c, weight_d, weight_e, bias_a, bias_b, bias_c, segment_ids, segment_cond)
    output, pullback = jax.vjp(wrapped, block_input.astype(jnp.float32), conditions, qkv_weight, proj_weight, inner_weight, outer_weight, ada_weight, head_biases, inner_bias, shared_biases)
    grads = pullback(cotangent.astype(jnp.float32))
    qkv_new = adam_update(qkv_weight, grads[2], qkv_first, qkv_second, RATES[0])
    proj_new = adam_update(proj_weight, grads[3], proj_first, proj_second, RATES[1])
    inner_new = adam_update(inner_weight, grads[4], inner_first, inner_second, RATES[2])
    outer_new = adam_update(outer_weight, grads[5], outer_first, outer_second, RATES[3])
    ada_new = adam_update(ada_weight, grads[6], ada_first, ada_second, RATES[4])
    head_new = adam_update(head_biases, grads[7], head_biases_first, head_biases_second, RATES[5])
    inner_bias_new = adam_update(inner_bias, grads[8], inner_bias_first, inner_bias_second, RATES[6])
    shared_new = adam_update(shared_biases, grads[9], shared_biases_first, shared_biases_second, RATES[7])
    return (output.astype(jnp.bfloat16), grads[0], grads[1], qkv_new[0], proj_new[0], inner_new[0], outer_new[0], ada_new[0], head_new[0], inner_bias_new[0], shared_new[0], qkv_new[1], proj_new[1], inner_new[1], outer_new[1], ada_new[1], head_new[1], inner_bias_new[1], shared_new[1], qkv_new[2], proj_new[2], inner_new[2], outer_new[2], ada_new[2], head_new[2], inner_bias_new[2], shared_new[2], qkv_new[0].astype(jnp.bfloat16), proj_new[0].astype(jnp.bfloat16), inner_new[0].astype(jnp.bfloat16), outer_new[0].astype(jnp.bfloat16))
```

```python
import functools
import math

import jax
import jax.numpy as jnp
from jax import lax
from jax.experimental import pallas as pl
from jax.experimental.pallas import tpu as pltpu
from jax.sharding import PartitionSpec as P

HD = 72
STEP = 10


BETA_ONE = 0.5
BETA_TWO = 0.6
ADAM_EPS = 1e-08
DECAY = 0.01
NORM_EPSILON = 1e-06
RATES = (0.04, 0.3, 0.04, 0.04, 0.04, 0.4, 0.4, 0.4)
PRECISION_MAX = lax.Precision.HIGHEST
FLOAT = jnp.float32
HALF = jnp.bfloat16


def silu(values):
    return values / (1.0 + jnp.exp(-values))


def gelu_tanh(values):
    inner = math.sqrt(2.0 / math.pi) * (values + 0.044715 * values * values * values)
    return 0.5 * values * (1.0 + jnp.tanh(inner))


def normalize(values):
    centered = values - jnp.mean(values, axis=-1, keepdims=True)
    inv_std = lax.rsqrt(jnp.mean(centered * centered, axis=-1, keepdims=True) + NORM_EPSILON)
    return (centered * inv_std, inv_std)


def norm_back(grad_normed, normed, inv_std):
    first_mean = jnp.mean(grad_normed, axis=-1, keepdims=True)
    second_mean = jnp.mean(grad_normed * normed, axis=-1, keepdims=True)
    return inv_std * (grad_normed - first_mean - normed * second_mean)


def block_scores(query_block, keys, query_segs, key_segs):
    scores = jnp.einsum("qhe,khe->hqk", query_block, keys, preferred_element_type=FLOAT) * (
        1.0 / math.sqrt(HD)
    )
    same = query_segs[:, None] == key_segs[None, :]
    return jnp.where(same[None], scores, -1e30)


def attend_forward(row_qkv, row_segs):
    queries = row_qkv[:, 0]
    keys = row_qkv[:, 1]
    values = row_qkv[:, 2]
    length = queries.shape[0]
    heads_local = queries.shape[1]
    block = min(512, length)
    blocks = length // block

    def one_block(pieces):
        query_block, query_segs = pieces
        scores = block_scores(query_block, keys, query_segs, row_segs)
        top = jnp.max(scores, axis=-1, keepdims=True)
        expo = jnp.exp(scores - top)
        total = jnp.sum(expo, axis=-1, keepdims=True)
        probs = (expo / total).astype(HALF)
        attended = jnp.einsum("hqk,khe->qhe", probs, values, preferred_element_type=FLOAT)
        return (attended, (top + jnp.log(total))[:, :, 0])

    attended, log_totals = lax.map(
        one_block,
        (queries.reshape(blocks, block, heads_local, HD), row_segs.reshape(blocks, block)),
    )
    return (attended.reshape(length, heads_local, HD), log_totals)


def attend_backward(row_qkv, row_segs, grad_row, log_totals):
    queries = row_qkv[:, 0]
    keys = row_qkv[:, 1]
    values = row_qkv[:, 2]
    length = queries.shape[0]
    heads_local = queries.shape[1]
    block = min(512, length)
    blocks = length // block
    scale = 1.0 / math.sqrt(HD)

    def one_block(carry, pieces):
        key_sum, value_sum = carry
        query_block, query_segs, grad_block, block_total = pieces
        scores = block_scores(query_block, keys, query_segs, row_segs)
        probs = jnp.exp(scores - block_total[:, :, None])
        grad_probs = jnp.einsum("qhe,khe->hqk", grad_block, values, preferred_element_type=FLOAT)
        center = jnp.sum(probs * grad_probs, axis=-1, keepdims=True)
        grad_scores = (probs * (grad_probs - center)).astype(HALF)
        grad_query = (
            jnp.einsum("hqk,khe->qhe", grad_scores, keys, preferred_element_type=FLOAT) * scale
        )
        key_sum = (
            key_sum
            + jnp.einsum("hqk,qhe->khe", grad_scores, query_block, preferred_element_type=FLOAT)
            * scale
        )
        value_sum = value_sum + jnp.einsum(
            "hqk,qhe->khe", probs.astype(HALF), grad_block, preferred_element_type=FLOAT
        )
        return ((key_sum, value_sum), grad_query)

    zeros = jnp.zeros((length, heads_local, HD), FLOAT)
    sums, grad_queries = lax.scan(
        one_block,
        (zeros, zeros),
        (
            queries.reshape(blocks, block, heads_local, HD),
            row_segs.reshape(blocks, block),
            grad_row.reshape(blocks, block, heads_local, HD),
            log_totals,
        ),
    )
    return jnp.stack([grad_queries.reshape(length, heads_local, HD), sums[0], sums[1]], axis=1)


def adam_update(weight, grad, first, second, rate):
    first_new = BETA_ONE * first + (1.0 - BETA_ONE) * grad
    second_new = BETA_TWO * second + (1.0 - BETA_TWO) * grad * grad
    fix_one = 1.0 - BETA_ONE**STEP
    fix_two = 1.0 - BETA_TWO**STEP
    update = first_new / fix_one / (jnp.sqrt(second_new / fix_two) + ADAM_EPS)
    return (weight - rate * (update + DECAY * weight), first_new, second_new)


def sum_to_shares(partial):
    return lax.psum_scatter(
        partial.astype(HALF), "tensor", scatter_dimension=0, tiled=True
    ).astype(FLOAT)


def sum_to_owners(partial):
    return lax.psum_scatter(
        partial.astype(HALF), "dp", scatter_dimension=0, tiled=True
    ).astype(FLOAT)


SEG_MOST = 256
CORES = 2
MESH = pl.DeviceIdType.MESH
NT_DIMS = (((1,), (1,)), ((), ()))
TN_DIMS = (((0,), (0,)), ((), ()))
VMEM_BYTES = 60 * 1024 * 1024


def line_length(count):
    length = 1
    while (2 * length) ** 2 <= count:
        length *= 2
    return length


def mm(left, right):
    return jnp.dot(left, right, preferred_element_type=FLOAT)


def mm_nt(left, right):
    return lax.dot_general(left, right, NT_DIMS, preferred_element_type=FLOAT)


def mm_tn(left, right):
    return lax.dot_general(left, right, TN_DIMS, preferred_element_type=FLOAT)


def split_two(values):
    high = values.astype(HALF)
    return high, (values - high.astype(FLOAT)).astype(HALF)


class Place:
    def __init__(self, dp_count, tensor_count):
        self.dp_count, self.tensor_count = dp_count, tensor_count
        self.xs = line_length(dp_count)
        self.zs = dp_count // self.xs
        self.ys = tensor_count // CORES
        self.dp, self.tensor = lax.axis_index("dp"), lax.axis_index("tensor")
        self.z, self.x = lax.div(self.dp, self.xs), lax.rem(self.dp, self.xs)
        self.y, self.core = lax.div(self.tensor, CORES), lax.rem(self.tensor, CORES)

    def z_of(self, step):
        return lax.rem(self.z + step + self.zs, self.zs)

    def x_of(self, step):
        return lax.rem(self.x + step + self.xs, self.xs)

    def z_peer(self, step):
        return (self.z_of(step) * self.xs + self.x, self.tensor)

    def x_peer(self, step):
        return (self.z * self.xs + self.x_of(step), self.tensor)

    def tensor_peer(self, step):
        return (self.dp, lax.rem(self.tensor + step, self.tensor_count))

    def core_peer(self):
        return (self.dp, self.y * CORES + 1 - self.core)

    def y_peer(self):
        return (self.dp, (1 - self.y) * CORES + self.core)

    def share_of(self, other_y, other_core):
        y = 1 - self.y if other_y else self.y
        core = 1 - self.core if other_core else self.core
        return y * CORES + core


def greet(peers):
    barrier = pltpu.get_barrier_semaphore()
    for peer in peers:
        pl.semaphore_signal(barrier, inc=1, device_id=peer, device_id_type=MESH)
    pl.semaphore_wait(barrier, len(peers))


def remote(src, dst, sends, recvs, peer):
    return pltpu.make_async_remote_copy(
        src_ref=src, dst_ref=dst, send_sem=sends, recv_sem=recvs, device_id=peer, device_id_type=MESH
    )


def rows_at(start, count):
    return pl.ds(pl.multiple_of(start, 16), count)


class Gather:
    def __init__(self, place, pieces, z_sems, x_sems):
        self.place, self.pieces = place, pieces
        self.z_send, self.z_recv = z_sems
        self.x_send, self.x_recv = x_sems
        self.pending = []

    def slot(self, piece, z, x):
        own, full, shard_rows, first, count = self.pieces[piece]
        return full.at[rows_at((z * self.place.xs + x) * shard_rows + first, count)]

    def z_copy(self, piece, step):
        own, full, shard_rows, first, count = self.pieces[piece]
        at = self.place
        return remote(
            own.at[pl.ds(first, count)], self.slot(piece, at.z, at.x),
            self.z_send.at[piece, step - 1], self.z_recv.at[piece, step - 1], at.z_peer(step),
        )

    def z_landing(self, piece, step):
        at = self.place
        landed = self.slot(piece, at.z_of(-step), at.x)
        return remote(
            landed, landed, self.z_send.at[piece, step - 1], self.z_recv.at[piece, step - 1], at.z_peer(step)
        )

    def x_copy(self, piece, back, step):
        at = self.place
        chunk = self.slot(piece, at.z_of(-back), at.x)
        source = chunk
        if back == 0:
            own, full, shard_rows, first, count = self.pieces[piece]
            source = own.at[pl.ds(first, count)]
        return remote(
            source, chunk, self.x_send.at[piece, back, step - 1], self.x_recv.at[piece, back, step - 1],
            at.x_peer(step),
        )

    def x_landing(self, piece, back, step):
        at = self.place
        landed = self.slot(piece, at.z_of(-back), at.x_of(-step))
        return remote(
            landed, landed, self.x_send.at[piece, back, step - 1], self.x_recv.at[piece, back, step - 1],
            at.x_peer(step),
        )

    def start(self, piece):
        at = self.place
        for step in sorted(range(1, at.zs), key=lambda s: -min(s, at.zs - s)):
            self.z_copy(piece, step).start()
        for step in range(1, at.xs):
            self.x_copy(piece, 0, step).start()

    def sent(self, piece):
        for step in range(1, self.place.zs):
            self.z_copy(piece, step).wait_send()

    def forward(self, piece):
        at = self.place
        for back in range(1, at.zs):
            self.z_landing(piece, back).wait_recv()
            for step in range(1, at.xs):
                self.x_copy(piece, back, step).start()

    def arrive(self, piece):
        at = self.place
        for back in range(at.zs):
            for step in range(1, at.xs):
                self.x_landing(piece, back, step).wait_recv()

    def finish(self, piece):
        at = self.place
        for back in range(at.zs):
            for step in range(1, at.xs):
                self.x_copy(piece, back, step).wait_send()


def layer_norm(values):
    mean = jnp.mean(values, axis=-1, keepdims=True)
    centered = values - mean
    inv_std = lax.rsqrt(jnp.mean(centered * centered, axis=-1, keepdims=True) + NORM_EPSILON)
    return centered * inv_std, inv_std


def forward_kernel(
    sizes,
    x_ref, seg_col, seg_row, cond_ref, ada_ref, mod_bias, qkv_bias, inner_bias, shared_bias,
    proj_place, wq, wp, wi, wo,
    wq_out, wp_out, wi_out, wo_out, hid_a_out, heads_out, lse_out, att_out, hid_b_out, act_out,
    slope_out, part_out, branch_out, middle_out, modk_out,
    wq_full, wp_full, wp_tight, wi_full, wo_full, hid_a, heads, lse, att_heads, att, part, core_in,
    y_out, y_in, hid_b, act, slope, ff_part, branch, middle, modk, mods, ada_tile,
    z_send, z_recv, x_send, x_recv, mod_send, mod_recv, sum_send, sum_recv, gat_send, gat_recv,
    ada_sem, save_sem,
):
    at = Place(sizes["dp"], sizes["tensor"])
    tokens, width, columns, share = sizes["tokens"], sizes["width"], sizes["columns"], sizes["share"]
    nheads, segs = columns // HD, cond_ref.shape[0]
    window = min(tokens, share + 2 * SEG_MOST)
    greet(
        [at.z_peer(s) for s in range(1, at.zs)]
        + [at.x_peer(s) for s in range(1, at.xs)]
        + [at.tensor_peer(s) for s in range(1, at.tensor_count)]
    )
    pieces = []
    for own, full in ((wq, wq_full), (wp, wp_full), (wi, wi_full), (wo, wo_full)):
        shard = own.shape[0]
        unit = 48 if shard % 48 == 0 else shard
        pieces += [(own, full, shard, first, unit) for first in range(0, shard, unit)]
    gather = Gather(at, pieces, (z_send, z_recv), (x_send, x_recv))
    n_q, n_p, n_i = (wq.shape[0] // 48 if wq.shape[0] % 48 == 0 else 1), 1, (wi.shape[0] // 48 if wi.shape[0] % 48 == 0 else 1)
    list_q, list_p = list(range(n_q)), [n_q]
    list_i = list(range(n_q + n_p, n_q + n_p + n_i))
    list_o = list(range(n_q + n_p + n_i, len(pieces)))
    last = len(pieces)
    started = [0]

    def push():
        piece = started[0]
        if piece < last:
            if piece >= 2:
                gather.sent(piece - 2)
            gather.start(piece)
            started[0] += 1

    push()
    push()

    for own, full in ((wq, wq_full), (wp, wp_full), (wi, wi_full), (wo, wo_full)):
        full[rows_at(at.dp * own.shape[0], own.shape[0]), :] = own[...]

    def ada_copy(group):
        return pltpu.make_async_copy(ada_ref.at[group], ada_tile.at[group % 2], ada_sem.at[group % 2])

    ada_copy(0).start()
    cond_high, cond_low = split_two(cond_ref[...])
    cond_both = jnp.concatenate([cond_high, cond_low], axis=0)
    for group in range(6):
        if group < 5:
            ada_copy(group + 1).start()
        ada_copy(group).wait()
        weight_high, weight_low = split_two(ada_tile[group % 2])
        both = mm_nt(cond_both, weight_high)
        mods[at.tensor, group] = (
            both[:segs] + both[segs:] + mm_nt(cond_high, weight_low) + mod_bias[group]
        )

    def mod_copy(step):
        own = mods.at[at.tensor]
        return remote(own, own, mod_send.at[step - 1], mod_recv.at[step - 1], at.tensor_peer(step))

    def mod_landing(step):
        landed = mods.at[lax.rem(at.tensor + at.tensor_count - step, at.tensor_count)]
        return remote(landed, landed, mod_send.at[step - 1], mod_recv.at[step - 1], at.tensor_peer(step))

    for step in range(1, at.tensor_count):
        mod_copy(step).start()
    for step in range(1, at.tensor_count):
        mod_landing(step).wait_recv()
    for group in range(6):
        whole = jnp.concatenate([mods[t, group] for t in range(at.tensor_count)], axis=1)
        high, low = split_two(whole)
        modk[group] = jnp.concatenate([high, low], axis=0)

    def pick(rows):
        ids = seg_col[rows, :]
        lanes = lax.broadcasted_iota(jnp.int32, (1, 2 * segs), 1)
        return (ids == lax.rem(lanes, segs)).astype(FLOAT).astype(HALF)

    gather.forward(0)
    push()

    def hidden_block(index, carry):
        rows = rows_at(index * share, share)
        normed, _ = layer_norm(x_ref[rows, :].astype(FLOAT))
        chosen = pick(rows)
        hid_a[rows, :] = (normed * (1.0 + mm(chosen, modk[1])) + mm(chosen, modk[0])).astype(HALF)
        return carry

    lax.fori_loop(0, tokens // share, hidden_block, 0)
    for piece in list_q[1:]:
        gather.forward(piece)
        push()
    for piece in list_q:
        gather.arrive(piece)
    gather.forward(list_p[0])
    push()

    def qkv_block(index, carry):
        rows = rows_at(index * share, share)
        values = mm(hid_a[rows, :], wq_full[...]) + qkv_bias[...]
        for head in range(3 * nheads):
            heads[head, rows, :] = values[:, head * HD:(head + 1) * HD].astype(HALF)
        return carry

    lax.fori_loop(0, tokens // share, qkv_block, 0)

    def attend(block):
        start = block * share
        rows = rows_at(start, share)
        first = pl.multiple_of(jnp.clip(start - SEG_MOST, 0, tokens - window), 128)
        keys = pl.ds(first, window)

        def one_head(head, carry):
            same = seg_col[rows, :] == seg_row[:, keys]
            scores = mm_nt(heads[head, rows, :], heads[nheads + head, keys, :]) * (1.0 / math.sqrt(HD))
            scores = jnp.where(same, scores, -1e30)
            top = jnp.max(scores, axis=-1, keepdims=True)
            expo = jnp.exp(scores - top)
            total = jnp.sum(expo, axis=-1, keepdims=True)
            probs = (expo * (1.0 / total)).astype(HALF)
            att_heads[head, :, :] = mm(probs, heads[2 * nheads + head, keys, :])
            lse[head, rows, :] = top + jnp.log(total)
            return carry

        lax.fori_loop(0, nheads, one_head, 0)
        joined = jnp.concatenate([att_heads[head] for head in range(nheads)], axis=1).astype(HALF)
        att[rows, :] = joined
        return joined

    def core_copy(slot, src):
        return remote(src, core_in.at[slot], sum_send.at[slot], sum_recv.at[slot], at.core_peer())

    y_copy = remote(y_out, y_in, sum_send.at[2], sum_recv.at[2], at.y_peer())

    joined = attend(at.share_of(True, True))
    gather.arrive(list_p[0])
    wp_tight[...] = mm(proj_place[...], wp_full[...]).astype(HALF)
    part[0] = mm(joined, wp_tight[...]).astype(HALF)
    core_copy(0, part.at[0]).start()
    gather.forward(list_i[0])
    push()
    joined = attend(at.share_of(False, True))
    part[1] = mm(joined, wp_tight[...]).astype(HALF)
    core_copy(1, part.at[1]).start()
    joined = attend(at.share_of(True, False))
    summed = mm(joined, wp_tight[...])
    core_copy(0, part.at[0]).wait_recv()
    y_out[...] = (summed + core_in[0].astype(FLOAT)).astype(HALF)
    y_copy.start()
    joined = attend(at.share_of(False, False))
    summed = mm(joined, wp_tight[...])
    core_copy(1, part.at[1]).wait_recv()
    summed = summed + core_in[1].astype(FLOAT)
    if len(list_i) > 1:
        gather.forward(list_i[1])
        push()
    y_copy.wait_recv()
    branch[...] = summed + y_in[...].astype(FLOAT) + shared_bias[0:1, :]

    own_rows = rows_at(at.tensor * share, share)
    chosen = pick(own_rows)
    middle[...] = x_ref[own_rows, :].astype(FLOAT) + mm(chosen, modk[2]) * branch[...]
    normed, _ = layer_norm(middle[...])
    hid_b[own_rows, :] = (normed * (1.0 + mm(chosen, modk[4])) + mm(chosen, modk[3])).astype(HALF)

    def hid_rows(other_y, other_core):
        return hid_b.at[rows_at(at.share_of(other_y, other_core) * share, share)]

    own_hid = hid_rows(False, False)
    to_core = remote(own_hid, own_hid, gat_send.at[0], gat_recv.at[0], at.core_peer())
    to_y = remote(own_hid, own_hid, gat_send.at[1], gat_recv.at[1], at.y_peer())
    to_y.start()
    to_core.start()
    across = hid_rows(True, False)
    onward = remote(across, across, gat_send.at[2], gat_recv.at[2], at.core_peer())
    for piece in list_i[2:]:
        gather.forward(piece)
        push()
    remote(across, across, gat_send.at[1], gat_recv.at[1], at.y_peer()).wait_recv()
    onward.start()
    for piece in list_i:
        gather.arrive(piece)
    beside = hid_rows(False, True)
    remote(beside, beside, gat_send.at[0], gat_recv.at[0], at.core_peer()).wait_recv()
    far = hid_rows(True, True)
    remote(far, far, gat_send.at[2], gat_recv.at[2], at.core_peer()).wait_recv()
    gather.forward(list_o[0])
    push()

    def inner_block(index, carry):
        rows = rows_at(index * share, share)
        pre = mm(hid_b[rows, :], wi_full[...]) + inner_bias[...]
        factor = math.sqrt(2.0 / math.pi)
        squared = pre * pre
        bend = jnp.tanh(factor * (pre + 0.044715 * squared * pre))
        act[rows, :] = (0.5 * pre * (1.0 + bend)).astype(HALF)
        slope[rows, :] = (
            0.5 * (1.0 + bend)
            + 0.5 * pre * (1.0 - bend * bend) * (factor * (1.0 + (3 * 0.044715) * squared))
        ).astype(HALF)
        return carry

    lax.fori_loop(0, tokens // share, inner_block, 0)

    saves = []

    def save(src, dst):
        copy = pltpu.make_async_copy(src, dst, save_sem.at[len(saves)])
        copy.start()
        saves.append(copy)

    for src, dst in (
        (wq_full, wq_out), (wp_tight, wp_out), (wi_full, wi_out), (hid_a, hid_a_out), (heads, heads_out),
        (lse, lse_out), (att, att_out), (hid_b, hid_b_out), (act, act_out), (slope, slope_out),
        (branch, branch_out), (middle, middle_out), (modk, modk_out),
    ):
        save(src, dst)
    for piece in list_o[1:]:
        gather.forward(piece)
        push()
    for piece in list_o:
        gather.arrive(piece)
    save(wo_full, wo_out)

    def outer_block(index, carry):
        rows = rows_at(index * share, share)
        ff_part[rows, :] = mm(act[rows, :], wo_full[...]).astype(HALF)
        return carry

    lax.fori_loop(0, tokens // share, outer_block, 0)
    save(ff_part, part_out)

    for step in range(1, at.tensor_count):
        mod_copy(step).wait_send()
    core_copy(0, part.at[0]).wait_send()
    core_copy(1, part.at[1]).wait_send()
    y_copy.wait_send()
    to_core.wait_send()
    to_y.wait_send()
    onward.wait_send()
    for piece in range(max(0, last - 2), last):
        gather.sent(piece)
    for piece in range(last):
        gather.finish(piece)
    for copy in saves:
        copy.wait()


def any_spec():
    return pl.BlockSpec(memory_space=pl.ANY)


def vmem_spec():
    return pl.BlockSpec(memory_space=pltpu.VMEM)


def sizes_of(block_input, segment_ids, qkv_weight, inner_weight):
    dp_count, tensor_count = lax.axis_size("dp"), lax.axis_size("tensor")
    tokens, width = block_input.shape
    return {
        "dp": dp_count,
        "tensor": tensor_count,
        "tokens": tokens,
        "rows": segment_ids.shape[0],
        "width": width,
        "columns": qkv_weight.shape[2],
        "hidden": inner_weight.shape[1],
        "shard": qkv_weight.shape[0],
        "share": tokens // tensor_count,
    }


def kernels_fit(sizes):
    return (
        sizes["tensor"] == 2 * CORES
        and sizes["rows"] == 1
        and sizes["share"] % 128 == 0
        and sizes["width"] % 128 == 0
        and sizes["hidden"] % 128 == 0
        and sizes["shard"] % 16 == 0
        and sizes["columns"] % 32 == 0
    )


def run_forward(sizes, block_input, segment_ids, cond_act, ada_weight, head_biases, inner_bias,
                shared_biases, wq, wp, wi, wo):
    tokens, width, columns, share = (sizes[k] for k in ("tokens", "width", "columns", "share"))
    hidden, dp_count, tensor_count = sizes["hidden"], sizes["dp"], sizes["tensor"]
    nheads, segs = columns // HD, cond_act.shape[0]
    own_rows = columns // dp_count
    pad_rows = wp.shape[0]
    xs = line_length(dp_count)
    zs = dp_count // xs
    units = sum(w.shape[0] // 48 if w.shape[0] % 48 == 0 else 1 for w in (wq, wp, wi, wo))
    tight = jnp.arange(columns)
    place = (tight // own_rows * pad_rows + tight % own_rows)[:, None] == jnp.arange(dp_count * pad_rows)
    shapes = [
        ((width, 3 * columns), HALF), ((columns, width), HALF), ((width, hidden), HALF),
        ((hidden, width), HALF), ((tokens, width), HALF), ((3 * nheads, tokens, HD), HALF),
        ((nheads, tokens, 1), FLOAT), ((tokens, columns), HALF), ((tokens, width), HALF),
        ((tokens, hidden), HALF), ((tokens, hidden), HALF), ((tokens, width), HALF),
        ((share, width), FLOAT), ((share, width), FLOAT), ((6, 2 * segs, width), HALF),
    ]
    vmem = pltpu.VMEM
    dma = pltpu.SemaphoreType.DMA
    scratch = [
        vmem((width, 3 * columns), HALF), vmem((dp_count * pad_rows, width), HALF),
        vmem((columns, width), HALF), vmem((width, hidden), HALF), vmem((hidden, width), HALF),
        vmem((tokens, width), HALF), vmem((3 * nheads, tokens, HD), HALF),
        vmem((nheads, tokens, 1), FLOAT), vmem((nheads, share, HD), FLOAT),
        vmem((tokens, columns), HALF), vmem((2, share, width), HALF), vmem((2, share, width), HALF),
        vmem((share, width), HALF), vmem((share, width), HALF), vmem((tokens, width), HALF),
        vmem((tokens, hidden), HALF), vmem((tokens, hidden), HALF), vmem((tokens, width), HALF),
        vmem((share, width), FLOAT), vmem((share, width), FLOAT), vmem((6, 2 * segs, width), HALF),
        vmem((tensor_count, 6, segs, columns), FLOAT), vmem((2, columns, width), FLOAT),
        dma((units, zs - 1)), dma((units, zs - 1)), dma((units, zs, xs - 1)), dma((units, zs, xs - 1)),
        dma((tensor_count - 1,)), dma((tensor_count - 1,)), dma((3,)), dma((3,)), dma((3,)), dma((3,)),
        dma((2,)), dma((15,)),
    ]
    return pl.pallas_call(
        functools.partial(forward_kernel, sizes),
        out_shape=[jax.ShapeDtypeStruct(s, t) for s, t in shapes],
        in_specs=[vmem_spec()] * 4 + [any_spec()] + [vmem_spec()] * 9,
        out_specs=[any_spec()] * len(shapes),
        scratch_shapes=scratch,
        name="forward",
        compiler_params=pltpu.CompilerParams(
            collective_id=1, has_side_effects=True, vmem_limit_bytes=VMEM_BYTES
        ),
    )(
        block_input, segment_ids.reshape(tokens, 1), segment_ids, cond_act, ada_weight,
        head_biases[3:].reshape(6, 1, columns), head_biases[:3].reshape(1, 3 * columns),
        inner_bias.reshape(1, hidden), shared_biases, place.astype(HALF), wq, wp, wi, wo,
    )


def on_device_general(
    block_input,
    conditions,
    segment_ids,
    segment_cond,
    cotangent,
    qkv_weight,
    proj_weight,
    inner_weight,
    outer_weight,
    ada_weight,
    head_biases,
    inner_bias,
    shared_biases,
    qkv_first,
    proj_first,
    inner_first,
    outer_first,
    ada_first,
    head_biases_first,
    inner_bias_first,
    shared_biases_first,
    qkv_second,
    proj_second,
    inner_second,
    outer_second,
    ada_second,
    head_biases_second,
    inner_bias_second,
    shared_biases_second,
):
    columns = qkv_weight.shape[2]
    heads_local = columns // HD
    rows_local = segment_ids.shape[0]
    row_length = segment_ids.shape[1]
    token_count = rows_local * row_length
    seg_count = segment_cond.shape[1]
    width = block_input.shape[1]
    share_count = token_count // lax.axis_size("tensor")
    share_start = lax.axis_index("tensor") * share_count

    def share(values):
        return lax.dynamic_slice_in_dim(values, share_start, share_count, 0)

    qkv_full, proj_full, inner_full, outer_full = (
        lax.all_gather(qkv_weight.astype(HALF), "dp", axis=0, tiled=True),
        lax.all_gather(proj_weight.astype(HALF), "dp", axis=0, tiled=True),
        lax.all_gather(inner_weight.astype(HALF), "dp", axis=0, tiled=True),
        lax.all_gather(outer_weight.astype(HALF), "dp", axis=0, tiled=True),
    )
    condition_select = (
        segment_cond[:, :, None] == jnp.arange(conditions.shape[0])[None, None, :]
    ).astype(FLOAT)
    condition_row_block = jnp.einsum(
        "btu,ua->bta", condition_select, conditions, precision=PRECISION_MAX
    )
    cond_act = silu(condition_row_block)
    local_mod = (
        jnp.einsum("rsd,kcd->rskc", cond_act, ada_weight, precision=PRECISION_MAX)
        + head_biases[3:][None, None]
    )
    full_mod = lax.all_gather(local_mod, "tensor", axis=3, tiled=True)
    seg_pick = (segment_ids[:, :, None] == jnp.arange(seg_count)[None, None, :]).astype(FLOAT)
    token_mod = jnp.einsum("rls,rskd->rlkd", seg_pick, full_mod, precision=PRECISION_MAX).reshape(
        token_count, 6, width
    )
    inputs = block_input.astype(FLOAT)
    normed_one, inv_one = normalize(inputs)
    hidden_one = (normed_one * (1.0 + token_mod[:, 1]) + token_mod[:, 0]).astype(HALF)
    qkv_values = (
        jnp.einsum("nd,dkc->nkc", hidden_one, qkv_full, preferred_element_type=FLOAT)
        + head_biases[:3][None]
    ).astype(HALF)
    row_qkv = qkv_values.reshape(rows_local, row_length, 3, heads_local, HD)
    row = 0
    attended_row, total_row = attend_forward(row_qkv[row], segment_ids[row])
    attended_rows = [attended_row]
    total_rows = [total_row]
    attended = jnp.stack(attended_rows).reshape(token_count, columns).astype(HALF)
    attn_partial = jnp.dot(attended, proj_full, preferred_element_type=FLOAT)
    share_mod = share(token_mod)
    branch_one = sum_to_shares(attn_partial) + shared_biases[0]
    middle = share(inputs) + share_mod[:, 2] * branch_one
    normed_two, inv_two = normalize(middle)
    hidden_two_share = (normed_two * (1.0 + share_mod[:, 4]) + share_mod[:, 3]).astype(HALF)
    hidden_two = lax.all_gather(hidden_two_share, "tensor", axis=0, tiled=True)
    pre_act = jnp.dot(hidden_two, inner_full, preferred_element_type=FLOAT) + inner_bias
    act_values, gelu_back = jax.vjp(gelu_tanh, pre_act)
    act_low = act_values.astype(HALF)
    ff_partial = jnp.dot(act_low, outer_full, preferred_element_type=FLOAT)
    branch_two = sum_to_shares(ff_partial) + shared_biases[1]
    output = middle + share_mod[:, 5] * branch_two
    grad_out = cotangent.astype(FLOAT)
    grad_two = (grad_out * token_mod[:, 5]).astype(HALF)
    outer_grad = jnp.einsum("nf,nd->fd", act_low, grad_two, preferred_element_type=FLOAT)
    grad_act = jnp.einsum("nd,fd->nf", grad_two, outer_full, preferred_element_type=FLOAT)
    grad_pre = gelu_back(grad_act)[0].astype(HALF)
    inner_grad = jnp.einsum("nd,nf->df", hidden_two, grad_pre, preferred_element_type=FLOAT)
    back_two_partial = jnp.einsum("nf,df->nd", grad_pre, inner_full, preferred_element_type=FLOAT)
    grad_hidden_two = sum_to_shares(back_two_partial)
    grad_out_share = share(grad_out)
    grad_middle = grad_out_share + norm_back(
        grad_hidden_two * (1.0 + share_mod[:, 4]), normed_two, inv_two
    )
    grad_one_share = (grad_middle * share_mod[:, 2]).astype(HALF)
    grad_one = lax.all_gather(grad_one_share, "tensor", axis=0, tiled=True)
    proj_grad = jnp.einsum("nc,nd->cd", attended, grad_one, preferred_element_type=FLOAT)
    grad_attended = jnp.einsum(
        "nd,cd->nc", grad_one, proj_full, preferred_element_type=FLOAT
    ).astype(HALF)
    grad_rows = grad_attended.reshape(rows_local, row_length, heads_local, HD)
    row = 0
    grad_qkv_rows = [
        attend_backward(row_qkv[row], segment_ids[row], grad_rows[row], total_rows[row])
    ]
    grad_qkv = jnp.stack(grad_qkv_rows).reshape(token_count, 3, columns).astype(HALF)
    qkv_grad = jnp.einsum("nd,nkc->dkc", hidden_one, grad_qkv, preferred_element_type=FLOAT)
    back_one_partial = jnp.einsum("nkc,dkc->nd", grad_qkv, qkv_full, preferred_element_type=FLOAT)
    grad_hidden_one = sum_to_shares(back_one_partial)
    normed_one_share, inv_one_share = share(normed_one), share(inv_one)
    input_out = grad_middle + norm_back(
        grad_hidden_one * (1.0 + share_mod[:, 1]), normed_one_share, inv_one_share
    )
    block_out = output.astype(HALF)
    contributions = jnp.concatenate(
        [
            grad_hidden_one,
            grad_hidden_one * normed_one_share,
            grad_middle * branch_one,
            grad_hidden_two,
            grad_hidden_two * normed_two,
            grad_out_share * branch_two,
        ],
        axis=1,
    )
    pick_share = share(seg_pick.reshape(token_count, seg_count))
    cond_pick = jnp.dot(pick_share, condition_select[0], precision=PRECISION_MAX)
    cond_sums = jnp.einsum("lq,lc->qc", cond_pick, contributions, precision=PRECISION_MAX)
    cond_sums = cond_sums.reshape(-1, 6, lax.axis_size("tensor"), columns)
    cond_sums = lax.psum_scatter(cond_sums, "tensor", scatter_dimension=2, tiled=True)[:, :, 0]
    cond_total = lax.psum(cond_sums, "dp")
    all_act, all_silu_back = jax.vjp(silu, conditions)
    grad_all_act = jnp.einsum("qkc,kcd->qd", cond_total, ada_weight, precision=PRECISION_MAX)
    cond_grad = all_silu_back(lax.psum(grad_all_act, "tensor"))[0]
    head_bias_grad = jnp.sum(grad_qkv.astype(FLOAT), axis=0)
    inner_bias_grad = jnp.sum(grad_pre.astype(FLOAT), axis=0)
    shared_bias_grad = jnp.stack(
        [jnp.sum(grad_one.astype(FLOAT), axis=0), jnp.sum(grad_two.astype(FLOAT), axis=0)]
    )
    ada_total = jnp.einsum("qd,qkc->kcd", all_act, cond_total, precision=PRECISION_MAX)
    head_total, inner_bias_total, shared_total = lax.psum(
        (head_bias_grad, inner_bias_grad, shared_bias_grad), "dp"
    )
    head_total = jnp.concatenate([head_total, jnp.sum(cond_total, axis=0)], axis=0)
    qkv_shard, proj_shard, inner_shard, outer_shard = (
        sum_to_owners(qkv_grad),
        sum_to_owners(proj_grad),
        sum_to_owners(inner_grad),
        sum_to_owners(outer_grad),
    )
    qkv_new = adam_update(qkv_weight, qkv_shard, qkv_first, qkv_second, RATES[0])
    proj_new = adam_update(proj_weight, proj_shard, proj_first, proj_second, RATES[1])
    inner_new = adam_update(inner_weight, inner_shard, inner_first, inner_second, RATES[2])
    outer_new = adam_update(outer_weight, outer_shard, outer_first, outer_second, RATES[3])
    ada_new = adam_update(ada_weight, ada_total, ada_first, ada_second, RATES[4])
    head_new = adam_update(head_biases, head_total, head_biases_first, head_biases_second, RATES[5])
    inner_bias_new = adam_update(
        inner_bias, inner_bias_total, inner_bias_first, inner_bias_second, RATES[6]
    )
    shared_new = adam_update(
        shared_biases, shared_total, shared_biases_first, shared_biases_second, RATES[7]
    )
    return (
        block_out,
        input_out,
        cond_grad,
        qkv_new[0],
        proj_new[0],
        inner_new[0],
        outer_new[0],
        ada_new[0],
        head_new[0],
        inner_bias_new[0],
        shared_new[0],
        qkv_new[1],
        proj_new[1],
        inner_new[1],
        outer_new[1],
        ada_new[1],
        head_new[1],
        inner_bias_new[1],
        shared_new[1],
        qkv_new[2],
        proj_new[2],
        inner_new[2],
        outer_new[2],
        ada_new[2],
        head_new[2],
        inner_bias_new[2],
        shared_new[2],
        qkv_new[0].astype(HALF),
        proj_new[0].astype(HALF),
        inner_new[0].astype(HALF),
        outer_new[0].astype(HALF),
    )


def on_device_kernels(
    block_input,
    conditions,
    segment_ids,
    segment_cond,
    cotangent,
    qkv_weight,
    proj_weight,
    inner_weight,
    outer_weight,
    ada_weight,
    head_biases,
    inner_bias,
    shared_biases,
    qkv_first,
    proj_first,
    inner_first,
    outer_first,
    ada_first,
    head_biases_first,
    inner_bias_first,
    shared_biases_first,
    qkv_second,
    proj_second,
    inner_second,
    outer_second,
    ada_second,
    head_biases_second,
    inner_bias_second,
    shared_biases_second,
):
    columns = qkv_weight.shape[2]
    heads_local = columns // HD
    rows_local = segment_ids.shape[0]
    row_length = segment_ids.shape[1]
    token_count = rows_local * row_length
    seg_count = segment_cond.shape[1]
    width = block_input.shape[1]
    share_count = token_count // lax.axis_size("tensor")
    share_start = lax.axis_index("tensor") * share_count

    def share(values):
        return lax.dynamic_slice_in_dim(values, share_start, share_count, 0)

    condition_select = (
        segment_cond[:, :, None] == jnp.arange(conditions.shape[0])[None, None, :]
    ).astype(FLOAT)
    condition_row_block = jnp.einsum(
        "btu,ua->bta", condition_select, conditions, precision=PRECISION_MAX
    )
    cond_act = silu(condition_row_block)
    sizes = sizes_of(block_input, segment_ids, qkv_weight, inner_weight)
    grow = -proj_weight.shape[0] % 16
    (qkv_full, proj_full, inner_full, outer_full, hidden_one, heads, log_sums, attended, hidden_two,
     act_low, slope, ff_partial, branch_one, middle, modk) = run_forward(
        sizes, block_input, segment_ids, cond_act[0], ada_weight, head_biases, inner_bias, shared_biases,
        qkv_weight.astype(HALF).reshape(-1, 3 * columns),
        jnp.pad(proj_weight.astype(HALF), ((0, grow), (0, 0))),
        inner_weight.astype(HALF), outer_weight.astype(HALF),
    )
    qkv_full = qkv_full.reshape(width, 3, columns)
    full_mod = (modk[:, :seg_count].astype(FLOAT) + modk[:, seg_count:].astype(FLOAT)).transpose(1, 0, 2)[None]
    seg_pick = (segment_ids[:, :, None] == jnp.arange(seg_count)[None, None, :]).astype(FLOAT)
    token_mod = jnp.einsum("rls,rskd->rlkd", seg_pick, full_mod, precision=PRECISION_MAX).reshape(
        token_count, 6, width
    )
    share_mod = share(token_mod)
    row_qkv = heads.reshape(1, 3, heads_local, token_count, HD).transpose(0, 3, 1, 2, 4)
    total_rows = [log_sums.reshape(heads_local, 2, token_count // 2).transpose(1, 0, 2)]
    inputs = block_input.astype(FLOAT)
    normed_one, inv_one = normalize(inputs)
    normed_two, inv_two = normalize(middle)
    branch_two = sum_to_shares(ff_partial) + shared_biases[1]
    output = middle + share_mod[:, 5] * branch_two
    grad_out = cotangent.astype(FLOAT)
    grad_two = (grad_out * token_mod[:, 5]).astype(HALF)
    outer_grad = jnp.einsum("nf,nd->fd", act_low, grad_two, preferred_element_type=FLOAT)
    grad_act = jnp.einsum("nd,fd->nf", grad_two, outer_full, preferred_element_type=FLOAT)
    grad_pre = (grad_act * slope.astype(FLOAT)).astype(HALF)
    inner_grad = jnp.einsum("nd,nf->df", hidden_two, grad_pre, preferred_element_type=FLOAT)
    back_two_partial = jnp.einsum("nf,df->nd", grad_pre, inner_full, preferred_element_type=FLOAT)
    grad_hidden_two = sum_to_shares(back_two_partial)
    grad_out_share = share(grad_out)
    grad_middle = grad_out_share + norm_back(
        grad_hidden_two * (1.0 + share_mod[:, 4]), normed_two, inv_two
    )
    grad_one_share = (grad_middle * share_mod[:, 2]).astype(HALF)
    grad_one = lax.all_gather(grad_one_share, "tensor", axis=0, tiled=True)
    proj_grad = jnp.einsum("nc,nd->cd", attended, grad_one, preferred_element_type=FLOAT)
    grad_attended = jnp.einsum(
        "nd,cd->nc", grad_one, proj_full, preferred_element_type=FLOAT
    ).astype(HALF)
    grad_rows = grad_attended.reshape(rows_local, row_length, heads_local, HD)
    row = 0
    grad_qkv_rows = [
        attend_backward(row_qkv[row], segment_ids[row], grad_rows[row], total_rows[row])
    ]
    grad_qkv = jnp.stack(grad_qkv_rows).reshape(token_count, 3, columns).astype(HALF)
    qkv_grad = jnp.einsum("nd,nkc->dkc", hidden_one, grad_qkv, preferred_element_type=FLOAT)
    back_one_partial = jnp.einsum("nkc,dkc->nd", grad_qkv, qkv_full, preferred_element_type=FLOAT)
    grad_hidden_one = sum_to_shares(back_one_partial)
    normed_one_share, inv_one_share = share(normed_one), share(inv_one)
    input_out = grad_middle + norm_back(
        grad_hidden_one * (1.0 + share_mod[:, 1]), normed_one_share, inv_one_share
    )
    block_out = output.astype(HALF)
    contributions = jnp.concatenate(
        [
            grad_hidden_one,
            grad_hidden_one * normed_one_share,
            grad_middle * branch_one,
            grad_hidden_two,
            grad_hidden_two * normed_two,
            grad_out_share * branch_two,
        ],
        axis=1,
    )
    pick_share = share(seg_pick.reshape(token_count, seg_count))
    cond_pick = jnp.dot(pick_share, condition_select[0], precision=PRECISION_MAX)
    cond_sums = jnp.einsum("lq,lc->qc", cond_pick, contributions, precision=PRECISION_MAX)
    cond_sums = cond_sums.reshape(-1, 6, lax.axis_size("tensor"), columns)
    cond_sums = lax.psum_scatter(cond_sums, "tensor", scatter_dimension=2, tiled=True)[:, :, 0]
    cond_total = lax.psum(cond_sums, "dp")
    all_act, all_silu_back = jax.vjp(silu, conditions)
    grad_all_act = jnp.einsum("qkc,kcd->qd", cond_total, ada_weight, precision=PRECISION_MAX)
    cond_grad = all_silu_back(lax.psum(grad_all_act, "tensor"))[0]
    head_bias_grad = jnp.sum(grad_qkv.astype(FLOAT), axis=0)
    inner_bias_grad = jnp.sum(grad_pre.astype(FLOAT), axis=0)
    shared_bias_grad = jnp.stack(
        [jnp.sum(grad_one.astype(FLOAT), axis=0), jnp.sum(grad_two.astype(FLOAT), axis=0)]
    )
    ada_total = jnp.einsum("qd,qkc->kcd", all_act, cond_total, precision=PRECISION_MAX)
    head_total, inner_bias_total, shared_total = lax.psum(
        (head_bias_grad, inner_bias_grad, shared_bias_grad), "dp"
    )
    head_total = jnp.concatenate([head_total, jnp.sum(cond_total, axis=0)], axis=0)
    qkv_shard, proj_shard, inner_shard, outer_shard = (
        sum_to_owners(qkv_grad),
        sum_to_owners(proj_grad),
        sum_to_owners(inner_grad),
        sum_to_owners(outer_grad),
    )
    qkv_new = adam_update(qkv_weight, qkv_shard, qkv_first, qkv_second, RATES[0])
    proj_new = adam_update(proj_weight, proj_shard, proj_first, proj_second, RATES[1])
    inner_new = adam_update(inner_weight, inner_shard, inner_first, inner_second, RATES[2])
    outer_new = adam_update(outer_weight, outer_shard, outer_first, outer_second, RATES[3])
    ada_new = adam_update(ada_weight, ada_total, ada_first, ada_second, RATES[4])
    head_new = adam_update(head_biases, head_total, head_biases_first, head_biases_second, RATES[5])
    inner_bias_new = adam_update(
        inner_bias, inner_bias_total, inner_bias_first, inner_bias_second, RATES[6]
    )
    shared_new = adam_update(
        shared_biases, shared_total, shared_biases_first, shared_biases_second, RATES[7]
    )
    return (
        block_out,
        input_out,
        cond_grad,
        qkv_new[0],
        proj_new[0],
        inner_new[0],
        outer_new[0],
        ada_new[0],
        head_new[0],
        inner_bias_new[0],
        shared_new[0],
        qkv_new[1],
        proj_new[1],
        inner_new[1],
        outer_new[1],
        ada_new[1],
        head_new[1],
        inner_bias_new[1],
        shared_new[1],
        qkv_new[2],
        proj_new[2],
        inner_new[2],
        outer_new[2],
        ada_new[2],
        head_new[2],
        inner_bias_new[2],
        shared_new[2],
        qkv_new[0].astype(HALF),
        proj_new[0].astype(HALF),
        inner_new[0].astype(HALF),
        outer_new[0].astype(HALF),
    )


def on_device(*args):
    sizes = sizes_of(args[0], args[2], args[5], args[7])
    return (on_device_kernels if kernels_fit(sizes) else on_device_general)(*args)


def solution(mesh):
    in_specs = (
        P("dp", None),
        P(),
        P("dp", None),
        P("dp", None),
        P("dp", None),
        P("dp", None, "tensor"),
        P(("tensor", "dp"), None),
        P("dp", "tensor"),
        P(("tensor", "dp"), None),
        P(None, "tensor", None),
        P(None, "tensor"),
        P("tensor"),
        P(),
        P("dp", None, "tensor"),
        P(("tensor", "dp"), None),
        P("dp", "tensor"),
        P(("tensor", "dp"), None),
        P(None, "tensor", None),
        P(None, "tensor"),
        P("tensor"),
        P(),
        P("dp", None, "tensor"),
        P(("tensor", "dp"), None),
        P("dp", "tensor"),
        P(("tensor", "dp"), None),
        P(None, "tensor", None),
        P(None, "tensor"),
        P("tensor"),
        P(),
    )
    out_specs = (
        P(("dp", "tensor"), None),
        P(("dp", "tensor"), None),
        P(),
        P("dp", None, "tensor"),
        P(("tensor", "dp"), None),
        P("dp", "tensor"),
        P(("tensor", "dp"), None),
        P(None, "tensor", None),
        P(None, "tensor"),
        P("tensor"),
        P(),
        P("dp", None, "tensor"),
        P(("tensor", "dp"), None),
        P("dp", "tensor"),
        P(("tensor", "dp"), None),
        P(None, "tensor", None),
        P(None, "tensor"),
        P("tensor"),
        P(),
        P("dp", None, "tensor"),
        P(("tensor", "dp"), None),
        P("dp", "tensor"),
        P(("tensor", "dp"), None),
        P(None, "tensor", None),
        P(None, "tensor"),
        P("tensor"),
        P(),
        P("dp", None, "tensor"),
        P(("tensor", "dp"), None),
        P("dp", "tensor"),
        P(("tensor", "dp"), None),
    )
    return jax.shard_map(
        on_device, mesh=mesh, in_specs=in_specs, out_specs=out_specs, check_vma=False
    )
```

```python
import functools
import math

import jax
import jax.numpy as jnp
import numpy as np
from jax import lax
from jax.experimental import pallas as pl
from jax.experimental.pallas import tpu as pltpu
from jax.sharding import PartitionSpec as P

HD = 72
STEP = 10


BETA_ONE = 0.5
BETA_TWO = 0.6
ADAM_EPS = 1e-08
DECAY = 0.01
NORM_EPSILON = 1e-06
RATES = (0.04, 0.3, 0.04, 0.04, 0.04, 0.4, 0.4, 0.4)
PRECISION_MAX = lax.Precision.HIGHEST
FLOAT = jnp.float32
HALF = jnp.bfloat16
DP, TP = "dp", "tensor"


def silu(values):
    return values / (1.0 + jnp.exp(-values))


def gelu_tanh(values):
    inner = math.sqrt(2.0 / math.pi) * (values + 0.044715 * values * values * values)
    return 0.5 * values * (1.0 + jnp.tanh(inner))


def normalize(values):
    centered = values - jnp.mean(values, axis=-1, keepdims=True)
    inv_std = lax.rsqrt(jnp.mean(centered * centered, axis=-1, keepdims=True) + NORM_EPSILON)
    return (centered * inv_std, inv_std)


def norm_back(grad_normed, normed, inv_std):
    first_mean = jnp.mean(grad_normed, axis=-1, keepdims=True)
    second_mean = jnp.mean(grad_normed * normed, axis=-1, keepdims=True)
    return inv_std * (grad_normed - first_mean - normed * second_mean)


def block_scores(query_block, keys, query_segs, key_segs):
    scores = jnp.einsum("qhe,khe->hqk", query_block, keys, preferred_element_type=FLOAT) * (
        1.0 / math.sqrt(HD)
    )
    same = query_segs[:, None] == key_segs[None, :]
    return jnp.where(same[None], scores, -1e30)


def attend_forward(row_qkv, row_segs):
    queries = row_qkv[:, 0]
    keys = row_qkv[:, 1]
    values = row_qkv[:, 2]
    length = queries.shape[0]
    heads_local = queries.shape[1]
    block = min(512, length)
    blocks = length // block

    def one_block(pieces):
        query_block, query_segs = pieces
        scores = block_scores(query_block, keys, query_segs, row_segs)
        top = jnp.max(scores, axis=-1, keepdims=True)
        expo = jnp.exp(scores - top)
        total = jnp.sum(expo, axis=-1, keepdims=True)
        probs = (expo / total).astype(HALF)
        attended = jnp.einsum("hqk,khe->qhe", probs, values, preferred_element_type=FLOAT)
        return (attended, (top + jnp.log(total))[:, :, 0])

    attended, log_totals = lax.map(
        one_block,
        (queries.reshape(blocks, block, heads_local, HD), row_segs.reshape(blocks, block)),
    )
    return (attended.reshape(length, heads_local, HD), log_totals)


def attend_backward(row_qkv, row_segs, grad_row, log_totals):
    queries = row_qkv[:, 0]
    keys = row_qkv[:, 1]
    values = row_qkv[:, 2]
    length = queries.shape[0]
    heads_local = queries.shape[1]
    block = min(512, length)
    blocks = length // block
    scale = 1.0 / math.sqrt(HD)

    def one_block(carry, pieces):
        key_sum, value_sum = carry
        query_block, query_segs, grad_block, block_total = pieces
        scores = block_scores(query_block, keys, query_segs, row_segs)
        probs = jnp.exp(scores - block_total[:, :, None])
        grad_probs = jnp.einsum("qhe,khe->hqk", grad_block, values, preferred_element_type=FLOAT)
        center = jnp.sum(probs * grad_probs, axis=-1, keepdims=True)
        grad_scores = (probs * (grad_probs - center)).astype(HALF)
        grad_query = (
            jnp.einsum("hqk,khe->qhe", grad_scores, keys, preferred_element_type=FLOAT) * scale
        )
        key_sum = (
            key_sum
            + jnp.einsum("hqk,qhe->khe", grad_scores, query_block, preferred_element_type=FLOAT)
            * scale
        )
        value_sum = value_sum + jnp.einsum(
            "hqk,qhe->khe", probs.astype(HALF), grad_block, preferred_element_type=FLOAT
        )
        return ((key_sum, value_sum), grad_query)

    zeros = jnp.zeros((length, heads_local, HD), FLOAT)
    sums, grad_queries = lax.scan(
        one_block,
        (zeros, zeros),
        (
            queries.reshape(blocks, block, heads_local, HD),
            row_segs.reshape(blocks, block),
            grad_row.reshape(blocks, block, heads_local, HD),
            log_totals,
        ),
    )
    return jnp.stack([grad_queries.reshape(length, heads_local, HD), sums[0], sums[1]], axis=1)


def adam_update(weight, grad, first, second, rate):
    first_new = BETA_ONE * first + (1.0 - BETA_ONE) * grad
    second_new = BETA_TWO * second + (1.0 - BETA_TWO) * grad * grad
    fix_one = 1.0 - BETA_ONE**STEP
    fix_two = 1.0 - BETA_TWO**STEP
    update = first_new / fix_one / (jnp.sqrt(second_new / fix_two) + ADAM_EPS)
    return (weight - rate * (update + DECAY * weight), first_new, second_new)


def sum_to_shares(partial):
    return lax.psum_scatter(
        partial.astype(HALF), TP, scatter_dimension=0, tiled=True
    ).astype(FLOAT)


def sum_to_owners(partial):
    return lax.psum_scatter(
        partial.astype(HALF), DP, scatter_dimension=0, tiled=True
    ).astype(FLOAT)


SEG_MOST = 256
CORES = 2
MESH = pl.DeviceIdType.MESH
NT_DIMS = (((1,), (1,)), ((), ()))
TN_DIMS = (((0,), (0,)), ((), ()))
VMEM_BYTES = 62 * 1024 * 1024


def line_length(count):
    length = 1
    while (2 * length) ** 2 <= count:
        length *= 2
    return length


def mm(left, right):
    return jnp.dot(left, right, preferred_element_type=FLOAT)


def mm_nt(left, right):
    return lax.dot_general(left, right, NT_DIMS, preferred_element_type=FLOAT)


def mm_tn(left, right):
    return lax.dot_general(left, right, TN_DIMS, preferred_element_type=FLOAT)


def split_two(values):
    high = values.astype(HALF)
    return high, (values - high.astype(FLOAT)).astype(HALF)


def cond_picks(seg_cond, conds):
    return (lax.broadcasted_iota(jnp.int32, (conds, 1), 0) == seg_cond[...]).astype(FLOAT).astype(HALF)


def pick_rows(picks, values):
    high, rest = split_two(values)
    middle, low = split_two(values - high.astype(FLOAT))
    return mm_tn(picks, high) + mm_tn(picks, middle) + mm_tn(picks, low)


class Place:
    def __init__(self, dp_count, tensor_count):
        self.dp_count, self.tensor_count = dp_count, tensor_count
        self.xs = line_length(dp_count)
        self.zs = dp_count // self.xs
        self.ys = tensor_count // CORES
        self.dp, self.tensor = lax.axis_index(DP), lax.axis_index(TP)
        self.z, self.x = lax.div(self.dp, self.xs), lax.rem(self.dp, self.xs)
        self.y, self.core = lax.div(self.tensor, CORES), lax.rem(self.tensor, CORES)

    def z_of(self, step):
        return lax.rem(self.z + step + self.zs, self.zs)

    def x_of(self, step):
        return lax.rem(self.x + step + self.xs, self.xs)

    def z_peer(self, step):
        return (self.z_of(step) * self.xs + self.x, self.tensor)

    def x_peer(self, step):
        return (self.z * self.xs + self.x_of(step), self.tensor)

    def tensor_peer(self, step):
        return (self.dp, lax.rem(self.tensor + step, self.tensor_count))

    def core_peer(self):
        return (self.dp, self.y * CORES + 1 - self.core)

    def y_peer(self):
        return (self.dp, (1 - self.y) * CORES + self.core)

    def share_of(self, other_y, other_core):
        y = 1 - self.y if other_y else self.y
        core = 1 - self.core if other_core else self.core
        return y * CORES + core


def greet(peers):
    barrier = pltpu.get_barrier_semaphore()
    for peer in peers:
        pl.semaphore_signal(barrier, inc=1, device_id=peer, device_id_type=MESH)
    pl.semaphore_wait(barrier, len(peers))


def remote(src, dst, sends, recvs, peer):
    return pltpu.make_async_remote_copy(
        src_ref=src, dst_ref=dst, send_sem=sends, recv_sem=recvs, device_id=peer, device_id_type=MESH
    )


def rows_at(start, count):
    return pl.ds(pl.multiple_of(start, 16), count)


def unit_rows(shard):
    return 48 if shard % 48 == 0 else shard


class Gather:
    def __init__(self, place, pieces, z_sems, x_sems):
        self.place, self.pieces = place, pieces
        self.z_send, self.z_recv = z_sems
        self.x_send, self.x_recv = x_sems
        self.pending = []

    def slot(self, piece, z, x):
        own, full, shard_rows, first, count = self.pieces[piece]
        return full.at[rows_at((z * self.place.xs + x) * shard_rows + first, count)]

    def z_copy(self, piece, step):
        own, full, shard_rows, first, count = self.pieces[piece]
        at = self.place
        return remote(
            own.at[pl.ds(first, count)], self.slot(piece, at.z, at.x),
            self.z_send.at[piece, step - 1], self.z_recv.at[piece, step - 1], at.z_peer(step),
        )

    def z_landing(self, piece, step):
        at = self.place
        landed = self.slot(piece, at.z_of(-step), at.x)
        return remote(
            landed, landed, self.z_send.at[piece, step - 1], self.z_recv.at[piece, step - 1], at.z_peer(step)
        )

    def x_copy(self, piece, back, step):
        at = self.place
        chunk = self.slot(piece, at.z_of(-back), at.x)
        source = chunk
        if back == 0:
            own, full, shard_rows, first, count = self.pieces[piece]
            source = own.at[pl.ds(first, count)]
        return remote(
            source, chunk, self.x_send.at[piece, back, step - 1], self.x_recv.at[piece, back, step - 1],
            at.x_peer(step),
        )

    def x_landing(self, piece, back, step):
        at = self.place
        landed = self.slot(piece, at.z_of(-back), at.x_of(-step))
        return remote(
            landed, landed, self.x_send.at[piece, back, step - 1], self.x_recv.at[piece, back, step - 1],
            at.x_peer(step),
        )

    def start(self, piece):
        at = self.place
        for step in sorted(range(1, at.zs), key=lambda s: -min(s, at.zs - s)):
            self.z_copy(piece, step).start()
        for step in range(1, at.xs):
            self.x_copy(piece, 0, step).start()

    def sent(self, piece):
        for step in range(1, self.place.zs):
            self.z_copy(piece, step).wait_send()

    def forward(self, piece):
        at = self.place
        for back in range(1, at.zs):
            self.z_landing(piece, back).wait_recv()
            for step in range(1, at.xs):
                self.x_copy(piece, back, step).start()

    def arrive(self, piece):
        at = self.place
        for back in range(at.zs):
            for step in range(1, at.xs):
                self.x_landing(piece, back, step).wait_recv()

    def finish(self, piece):
        at = self.place
        for back in range(at.zs):
            for step in range(1, at.xs):
                self.x_copy(piece, back, step).wait_send()


def layer_norm(values):
    mean = jnp.mean(values, axis=-1, keepdims=True)
    centered = values - mean
    inv_std = lax.rsqrt(jnp.mean(centered * centered, axis=-1, keepdims=True) + NORM_EPSILON)
    return centered * inv_std, inv_std


def forward_kernel(
    sizes,
    x_ref, seg_col, seg_row, seg_cond, cond_ref, ada_ref, head_bias, inner_bias, shared_bias,
    proj_place, wq_raw, wp_raw, wi_raw, wo_raw,
    wq_out, wp_out, wi_out, wo_out, hid_a_out, heads_out, lse_out, att_out, hid_b_out, act_out,
    slope_out, far_out, own_out, branch_out, middle_out, modk_out,
    wq_full, wp_full, wp_tight, wi_full, wo_full, hid_a, heads, lse, lse_heads, att_heads, att, part, core_in,
    y_out, y_in, hid_b, act, slope, ff_part, ff_in, ff_far, ff_own, branch, middle, modk, mods, ada_tile,
    wq, wp, wi, wo, wp_wide,
    z_send, z_recv, x_send, x_recv, mod_send, mod_recv, sum_send, sum_recv, gat_send, gat_recv, ff_send, ff_recv,
    ada_sem, save_sem,
):
    at = Place(sizes[DP], sizes[TP])
    tokens, width, columns, share = sizes["tokens"], sizes["width"], sizes["columns"], sizes["share"]
    nheads, segs = columns // HD, seg_cond.shape[1]
    window = min(tokens, share + 2 * SEG_MOST)
    greet(
        [at.z_peer(s) for s in range(1, at.zs)]
        + [at.x_peer(s) for s in range(1, at.xs)]
        + [at.tensor_peer(s) for s in range(1, at.tensor_count)]
    )
    pieces = []
    for own, full in ((wq, wq_full), (wp, wp_full), (wi, wi_full), (wo, wo_full)):
        shard = own.shape[0]
        unit = unit_rows(shard)
        pieces += [(own, full, shard, first, unit) for first in range(0, shard, unit)]
    gather = Gather(at, pieces, (z_send, z_recv), (x_send, x_recv))
    n_q, n_p, n_i = (own.shape[0] // unit_rows(own.shape[0]) for own in (wq, wp, wi))
    list_q, list_p = list(range(n_q)), [n_q]
    list_i = list(range(n_q + n_p, n_q + n_p + n_i))
    list_o = list(range(n_q + n_p + n_i, len(pieces)))
    last = len(pieces)
    started = [0]

    def push():
        piece = started[0]
        if piece < last:
            if piece >= 2:
                gather.sent(piece - 2)
            gather.start(piece)
            started[0] += 1

    wq[...] = jnp.concatenate([wq_raw[part_index] for part_index in range(3)], axis=1).astype(HALF)
    push()
    push()
    wp_wide[...] = jnp.zeros_like(wp_wide)
    wp_wide[0:wp_raw.shape[0], :] = wp_raw[...]
    wp[...] = wp_wide[...].astype(HALF)
    wi[...] = wi_raw[...].astype(HALF)
    wo[...] = wo_raw[...].astype(HALF)

    for own, full in ((wq, wq_full), (wp, wp_full), (wi, wi_full), (wo, wo_full)):
        full[rows_at(at.dp * own.shape[0], own.shape[0]), :] = own[...]

    def ada_copy(group):
        return pltpu.make_async_copy(ada_ref.at[group], ada_tile.at[group % 2], ada_sem.at[group % 2])

    ada_copy(0).start()
    cond_high, cond_low = split_two(silu(pick_rows(cond_picks(seg_cond, cond_ref.shape[0]), cond_ref[...])))
    cond_both = jnp.concatenate([cond_high, cond_low], axis=0)
    for group in range(6):
        if group < 5:
            ada_copy(group + 1).start()
        ada_copy(group).wait()
        weight_high, weight_low = split_two(ada_tile[group % 2])
        both = mm_nt(cond_both, weight_high)
        mods[at.tensor, group] = (
            both[:segs] + both[segs:] + mm_nt(cond_high, weight_low)
            + head_bias[3 + group:4 + group, :]
        )

    def mod_copy(step):
        own = mods.at[at.tensor]
        return remote(own, own, mod_send.at[step - 1], mod_recv.at[step - 1], at.tensor_peer(step))

    def mod_landing(step):
        landed = mods.at[lax.rem(at.tensor + at.tensor_count - step, at.tensor_count)]
        return remote(landed, landed, mod_send.at[step - 1], mod_recv.at[step - 1], at.tensor_peer(step))

    for step in range(1, at.tensor_count):
        mod_copy(step).start()
    for step in range(1, at.tensor_count):
        mod_landing(step).wait_recv()
    for group in range(6):
        whole = jnp.concatenate([mods[t, group] for t in range(at.tensor_count)], axis=1)
        high, low = split_two(whole)
        modk[group] = jnp.concatenate([high, low], axis=0)

    def pick(rows):
        ids = seg_col[rows, :]
        lanes = lax.broadcasted_iota(jnp.int32, (1, 2 * segs), 1)
        return (ids == lax.rem(lanes, segs)).astype(FLOAT).astype(HALF)

    gather.forward(0)
    push()

    def hidden_block(index, carry):
        rows = rows_at(index * share, share)
        normed, _ = layer_norm(x_ref[rows, :].astype(FLOAT))
        chosen = pick(rows)
        hid_a[rows, :] = (normed * (1.0 + mm(chosen, modk[1])) + mm(chosen, modk[0])).astype(HALF)
        return carry

    lax.fori_loop(0, tokens // share, hidden_block, 0)
    for piece in list_q[1:]:
        gather.forward(piece)
        push()
    for piece in list_q:
        gather.arrive(piece)
    gather.forward(list_p[0])
    push()

    qkv_bias = jnp.concatenate([head_bias[i:i + 1, :] for i in range(3)], axis=1)

    def qkv_block(index, carry):
        rows = rows_at(index * share, share)
        values = mm(hid_a[rows, :], wq_full[...]) + qkv_bias
        for head in range(3 * nheads):
            heads[head, rows, :] = values[:, head * HD:(head + 1) * HD].astype(HALF)
        return carry

    lax.fori_loop(0, tokens // share, qkv_block, 0)

    def attend(block):
        start = block * share
        rows = rows_at(start, share)
        first = pl.multiple_of(jnp.clip(start - SEG_MOST, 0, tokens - window), 128)
        keys = pl.ds(first, window)

        def one_head(head, carry):
            same = seg_col[rows, :] == seg_row[:, keys]
            scores = mm_nt(heads[head, rows, :], heads[nheads + head, keys, :]) * (1.0 / math.sqrt(HD))
            scores = jnp.where(same, scores, -1e30)
            top = jnp.max(scores, axis=-1, keepdims=True)
            expo = jnp.exp(scores - top)
            total = jnp.sum(expo, axis=-1, keepdims=True)
            probs = (expo * (1.0 / total)).astype(HALF)
            att_heads[head, :, :] = mm(probs, heads[2 * nheads + head, keys, :])
            lse_heads[head] = top + jnp.log(total)
            return carry

        lax.fori_loop(0, nheads, one_head, 0)
        joined = jnp.concatenate([att_heads[head] for head in range(nheads)], axis=1).astype(HALF)
        att[rows, :] = joined
        lse[rows, :] = jnp.concatenate([lse_heads[head] for head in range(nheads)], axis=1)
        return joined

    def core_copy(slot, src):
        return remote(src, core_in.at[slot], sum_send.at[slot], sum_recv.at[slot], at.core_peer())

    y_copy = remote(y_out, y_in, sum_send.at[2], sum_recv.at[2], at.y_peer())

    joined = attend(at.share_of(True, True))
    gather.arrive(list_p[0])
    wp_tight[...] = mm(proj_place[...], wp_full[...]).astype(HALF)
    part[0] = mm(joined, wp_tight[...]).astype(HALF)
    core_copy(0, part.at[0]).start()
    gather.forward(list_i[0])
    push()
    joined = attend(at.share_of(False, True))
    part[1] = mm(joined, wp_tight[...]).astype(HALF)
    core_copy(1, part.at[1]).start()
    joined = attend(at.share_of(True, False))
    summed = mm(joined, wp_tight[...])
    core_copy(0, part.at[0]).wait_recv()
    y_out[...] = (summed + core_in[0].astype(FLOAT)).astype(HALF)
    y_copy.start()
    joined = attend(at.share_of(False, False))
    summed = mm(joined, wp_tight[...])
    core_copy(1, part.at[1]).wait_recv()
    summed = summed + core_in[1].astype(FLOAT)
    if len(list_i) > 1:
        gather.forward(list_i[1])
        push()
    y_copy.wait_recv()
    branch[...] = summed + y_in[...].astype(FLOAT) + shared_bias[0:1, :]

    own_rows = rows_at(at.tensor * share, share)
    chosen = pick(own_rows)
    middle[...] = x_ref[own_rows, :].astype(FLOAT) + mm(chosen, modk[2]) * branch[...]
    normed, _ = layer_norm(middle[...])
    hid_b[own_rows, :] = (normed * (1.0 + mm(chosen, modk[4])) + mm(chosen, modk[3])).astype(HALF)

    def hid_rows(other_y, other_core):
        return hid_b.at[rows_at(at.share_of(other_y, other_core) * share, share)]

    own_hid = hid_rows(False, False)
    to_core = remote(own_hid, own_hid, gat_send.at[0], gat_recv.at[0], at.core_peer())
    to_y = remote(own_hid, own_hid, gat_send.at[1], gat_recv.at[1], at.y_peer())
    to_y.start()
    to_core.start()
    across = hid_rows(True, False)
    onward = remote(across, across, gat_send.at[2], gat_recv.at[2], at.core_peer())
    for piece in list_i[2:]:
        gather.forward(piece)
        push()
    remote(across, across, gat_send.at[1], gat_recv.at[1], at.y_peer()).wait_recv()
    onward.start()
    for piece in list_i:
        gather.arrive(piece)
    beside = hid_rows(False, True)
    remote(beside, beside, gat_send.at[0], gat_recv.at[0], at.core_peer()).wait_recv()
    far = hid_rows(True, True)
    remote(far, far, gat_send.at[2], gat_recv.at[2], at.core_peer()).wait_recv()
    gather.forward(list_o[0])
    push()

    def inner_block(index, carry):
        rows = rows_at(index * share, share)
        pre = mm(hid_b[rows, :], wi_full[...]) + inner_bias[...].reshape(1, -1)
        factor = math.sqrt(2.0 / math.pi)
        squared = pre * pre
        bend = jnp.tanh(factor * (pre + 0.044715 * squared * pre))
        act[rows, :] = (0.5 * pre * (1.0 + bend)).astype(HALF)
        slope[rows, :] = (
            0.5 * (1.0 + bend)
            + 0.5 * pre * (1.0 - bend * bend) * (factor * (1.0 + (3 * 0.044715) * squared))
        ).astype(HALF)
        return carry

    lax.fori_loop(0, tokens // share, inner_block, 0)

    saves = []

    def save(src, dst):
        copy = pltpu.make_async_copy(src, dst, save_sem.at[len(saves)])
        copy.start()
        saves.append(copy)

    for src, dst in (
        (wq_full, wq_out), (wp_tight, wp_out), (wi_full, wi_out), (hid_a, hid_a_out), (heads, heads_out),
        (lse, lse_out), (att, att_out), (hid_b, hid_b_out), (act, act_out), (slope, slope_out),
        (branch, branch_out), (middle, middle_out), (modk, modk_out),
    ):
        save(src, dst)
    for piece in list_o[1:]:
        gather.forward(piece)
        push()
    for piece in list_o:
        gather.arrive(piece)
    save(wo_full, wo_out)

    def outer_block(other_y, other_core):
        rows = rows_at(at.share_of(other_y, other_core) * share, share)
        return mm(act[rows, :], wo_full[...])

    def ff_copy(slot):
        return remote(ff_part.at[slot], ff_in.at[slot], ff_send.at[slot], ff_recv.at[slot], at.core_peer())

    ff_part[0] = outer_block(True, True).astype(HALF)
    ff_copy(0).start()
    ff_part[1] = outer_block(False, True).astype(HALF)
    ff_copy(1).start()
    summed = outer_block(True, False)
    ff_copy(0).wait_recv()
    ff_far[...] = (summed + ff_in[0].astype(FLOAT)).astype(HALF)
    save(ff_far, far_out)
    summed = outer_block(False, False)
    ff_copy(1).wait_recv()
    ff_own[...] = summed + ff_in[1].astype(FLOAT)
    save(ff_own, own_out)
    ff_copy(0).wait_send()
    ff_copy(1).wait_send()

    for step in range(1, at.tensor_count):
        mod_copy(step).wait_send()
    core_copy(0, part.at[0]).wait_send()
    core_copy(1, part.at[1]).wait_send()
    y_copy.wait_send()
    to_core.wait_send()
    to_y.wait_send()
    onward.wait_send()
    for piece in range(max(0, last - 2), last):
        gather.sent(piece)
    for piece in range(last):
        gather.finish(piece)
    for copy in saves:
        copy.wait()


def any_spec():
    return pl.BlockSpec(memory_space=pl.ANY)


def vmem_spec():
    return pl.BlockSpec(memory_space=pltpu.VMEM)


def sizes_of(block_input, conditions, segment_ids, segment_cond, qkv_weight, inner_weight):
    dp_count, tensor_count = lax.axis_size(DP), lax.axis_size(TP)
    tokens, width = block_input.shape
    return {
        DP: dp_count,
        TP: tensor_count,
        "tokens": tokens,
        "rows": segment_ids.shape[0],
        "width": width,
        "columns": qkv_weight.shape[2],
        "hidden": inner_weight.shape[1],
        "shard": qkv_weight.shape[0],
        "share": tokens // tensor_count,
        "segs": segment_cond.shape[1],
        "conds": conditions.shape[0],
    }


def kernels_fit(sizes):
    return (
        sizes[TP] == 2 * CORES
        and sizes["rows"] == 1
        and sizes["share"] % 128 == 0
        and sizes["width"] % 128 == 0
        and sizes["hidden"] % 128 == 0
        and sizes["shard"] % 16 == 0
        and sizes["columns"] % 32 == 0
        and sizes["conds"] % (8 * sizes[TP]) == 0
    )


def placing(columns, own_rows, pad_rows, dp_count):
    tight = np.arange(columns)
    place = (tight // own_rows * pad_rows + tight % own_rows)[:, None] == np.arange(dp_count * pad_rows)
    return place.astype(np.float32)


def run_forward(sizes, block_input, seg_col, segment_ids, segment_cond, conditions, ada_weight, head_biases,
                inner_bias, shared_biases, wq, wp, wi, wo):
    tokens, width, columns, share = (sizes[k] for k in ("tokens", "width", "columns", "share"))
    hidden, dp_count, tensor_count = sizes["hidden"], sizes[DP], sizes[TP]
    nheads, segs = columns // HD, sizes["segs"]
    own_rows = columns // dp_count
    pad_rows = own_rows + -own_rows % 16
    shards = (sizes["shard"], pad_rows, sizes["shard"], hidden // dp_count)
    xs = line_length(dp_count)
    zs = dp_count // xs
    units = sum(shard // unit_rows(shard) for shard in shards)
    place = jnp.asarray(placing(columns, own_rows, pad_rows, dp_count), HALF)
    shapes = [
        ((width, 3 * columns), HALF), ((columns, width), HALF), ((width, hidden), HALF),
        ((hidden, width), HALF), ((tokens, width), HALF), ((3 * nheads, tokens, HD), HALF),
        ((tokens, nheads), FLOAT), ((tokens, columns), HALF), ((tokens, width), HALF),
        ((tokens, hidden), HALF), ((tokens, hidden), HALF), ((share, width), HALF), ((share, width), FLOAT),
        ((share, width), FLOAT), ((share, width), FLOAT), ((6, 2 * segs, width), HALF),
    ]
    vmem = pltpu.VMEM
    dma = pltpu.SemaphoreType.DMA
    scratch = [
        vmem((width, 3 * columns), HALF), vmem((dp_count * pad_rows, width), HALF),
        vmem((columns, width), HALF), vmem((width, hidden), HALF), vmem((hidden, width), HALF),
        vmem((tokens, width), HALF), vmem((3 * nheads, tokens, HD), HALF),
        vmem((tokens, nheads), FLOAT), vmem((nheads, share, 1), FLOAT), vmem((nheads, share, HD), FLOAT),
        vmem((tokens, columns), HALF), vmem((2, share, width), HALF), vmem((2, share, width), HALF),
        vmem((share, width), HALF), vmem((share, width), HALF), vmem((tokens, width), HALF),
        vmem((tokens, hidden), HALF), vmem((tokens, hidden), HALF), vmem((2, share, width), HALF),
        vmem((2, share, width), HALF), vmem((share, width), HALF), vmem((share, width), FLOAT),
        vmem((share, width), FLOAT), vmem((share, width), FLOAT), vmem((6, 2 * segs, width), HALF),
        vmem((tensor_count, 6, segs, columns), FLOAT), vmem((2, columns, width), FLOAT),
        vmem((shards[0], 3 * columns), HALF), vmem((pad_rows, width), HALF), vmem((shards[2], hidden), HALF),
        vmem((shards[3], width), HALF), vmem((pad_rows, width), FLOAT),
        dma((units, zs - 1)), dma((units, zs - 1)), dma((units, zs, xs - 1)), dma((units, zs, xs - 1)),
        dma((tensor_count - 1,)), dma((tensor_count - 1,)), dma((3,)), dma((3,)), dma((3,)), dma((3,)), dma((2,)), dma((2,)),
        dma((2,)), dma((16,)),
    ]
    return pl.pallas_call(
        functools.partial(forward_kernel, sizes),
        out_shape=[jax.ShapeDtypeStruct(s, t) for s, t in shapes],
        in_specs=[vmem_spec()] * 5 + [any_spec()] + [vmem_spec()] * 8,
        out_specs=[any_spec()] * len(shapes),
        scratch_shapes=scratch,
        name="forward",
        compiler_params=pltpu.CompilerParams(
            collective_id=1, has_side_effects=True, vmem_limit_bytes=VMEM_BYTES
        ),
    )(
        block_input, seg_col, segment_ids, segment_cond, conditions, ada_weight, head_biases, inner_bias,
        shared_biases, place, wq, wp, wi, wo,
    )


class Scatter:
    def __init__(self, place, pieces, x_sems, z_sems):
        self.place, self.pieces = place, pieces
        self.x_send, self.x_recv = x_sems
        self.z_send, self.z_recv = z_sems

    def slot(self, piece, z, x):
        whole, x_in, z_in, shard, first, count = self.pieces[piece]
        return whole.at[rows_at((z * self.place.xs + x) * shard + first, count)]

    def x_copy(self, piece, step, z):
        at = self.place
        whole, x_in, z_in, shard, first, count = self.pieces[piece]
        return remote(
            self.slot(piece, z, at.x_of(step)), x_in.at[step - 1, z, pl.ds(first, count)],
            self.x_send.at[piece, step - 1, z], self.x_recv.at[piece, step - 1, z], at.x_peer(step),
        )

    def z_copy(self, piece, step):
        at = self.place
        whole, x_in, z_in, shard, first, count = self.pieces[piece]
        return remote(
            self.slot(piece, at.z_of(step), at.x), z_in.at[step - 1, pl.ds(first, count)],
            self.z_send.at[piece, step - 1], self.z_recv.at[piece, step - 1], at.z_peer(step),
        )

    def start(self, piece):
        at = self.place
        for step in range(1, at.xs):
            for z in range(at.zs):
                self.x_copy(piece, step, z).start()

    def pass_on(self, piece):
        at = self.place
        whole, x_in, z_in, shard, first, count = self.pieces[piece]
        for z in range(at.zs):
            rows = rows_at((z * at.xs + at.x) * shard + first, count)
            total = whole[rows, :].astype(FLOAT)
            for step in range(1, at.xs):
                self.x_copy(piece, step, z).wait_recv()
                total = total + x_in[step - 1, z, first:first + count, :].astype(FLOAT)
            whole[rows, :] = total.astype(HALF)
        for step in sorted(range(1, at.zs), key=lambda s: -min(s, at.zs - s)):
            self.z_copy(piece, step).start()

    def total(self, piece):
        at = self.place
        whole, x_in, z_in, shard, first, count = self.pieces[piece]
        total = whole[rows_at((at.z * at.xs + at.x) * shard + first, count), :].astype(FLOAT)
        for step in range(1, at.zs):
            self.z_copy(piece, step).wait_recv()
            total = total + z_in[step - 1, first:first + count, :].astype(FLOAT)
        return total

    def finish(self, piece):
        at = self.place
        for step in range(1, at.xs):
            for z in range(at.zs):
                self.x_copy(piece, step, z).wait_send()
        for step in range(1, at.zs):
            self.z_copy(piece, step).wait_send()


def image_sums(chosen, values):
    high, low = split_two(values)
    return mm_tn(chosen, high) + mm_tn(chosen, low)


def backward_kernel(
    sizes,
    seg_col, seg_row, seg_cond, shared_bias, place_back,
    x_in, cot_in, wq_in, wp_in, wi_in, wo_in, hid_a_in, heads_in, lse_in, att_in, hid_b_in, act_in, slope_in,
    far_in, own_in, branch_in, middle_in, modk_in,
    block_out, input_out, qkv_out, proj_out, inner_out, outer_out, mods_out, packs_out,
    wq, wp, wi, wo, heads, lse, att, hid_b, act, slope, cot, modk, branch, middle, ff_own,
    cot_own, x_own, gatt, key_sum, value_sum, grad_a, part, core_in, y_out, y_in, ff_in, grad_mid,
    whole_o, whole_i, whole_p, whole_q, xin_o, xin_i, xin_p, xin_q, zin_o, zin_i, zin_p, zin_q,
    mod_send_buf, mod_in, mods, packs,
    load_sem, save_sem, x_send, x_recv, z_send, z_recv, sum_send, sum_recv, gat_send, gat_recv,
    ff_send, ff_recv, mod_send, mod_recv, all_send, all_recv,
):
    at = Place(sizes[DP], sizes[TP])
    tokens, width, columns, share = sizes["tokens"], sizes["width"], sizes["columns"], sizes["share"]
    hidden = sizes["hidden"]
    nheads, segs = columns // HD, sizes["segs"]
    blocks = tokens // share
    scale = 1.0 / math.sqrt(HD)

    def dp_peer(step):
        return (lax.rem(at.dp + step, at.dp_count), at.tensor)

    own_rows = rows_at(at.tensor * share, share)
    loads = {}

    def load(name, src, dst):
        copy = pltpu.make_async_copy(src, dst, load_sem.at[len(loads)])
        copy.start()
        loads[name] = copy

    load("cot", cot_in, cot)
    load("modk", modk_in, modk)
    load("act", act_in, act)
    load("wo", wo_in, wo)
    load("slope", slope_in, slope)
    load("wi", wi_in, wi)
    load("hid_b", hid_b_in, hid_b)
    load("middle", middle_in, middle)
    load("branch", branch_in, branch)
    load("ff_own", own_in, ff_own)
    load("att", att_in, att)
    load("wp", wp_in, wp)
    load("heads", heads_in, heads)
    load("lse", lse_in, lse)
    load("wq", wq_in, wq)
    load("x", x_in.at[own_rows], x_own)
    greet(
        [dp_peer(s) for s in range(1, at.dp_count)]
        + [at.tensor_peer(s) for s in range(1, at.tensor_count)]
    )
    ff_copy = remote(far_in, ff_in, ff_send, ff_recv, at.y_peer())
    ff_copy.start()

    pieces = []
    for whole, x_in, z_in in (
        (whole_o, xin_o, zin_o), (whole_i, xin_i, zin_i), (whole_p, xin_p, zin_p), (whole_q, xin_q, zin_q)
    ):
        shard = x_in.shape[2]
        unit = unit_rows(shard)
        pieces.append([(whole, x_in, z_in, shard, first, unit) for first in range(0, shard, unit)])
    flat = [piece for group in pieces for piece in group]
    scatter = Scatter(at, flat, (x_send, x_recv), (z_send, z_recv))
    bounds = [sum(len(g) for g in pieces[:i]) for i in range(len(pieces) + 1)]
    list_o, list_i, list_p, list_q = (list(range(bounds[i], bounds[i + 1])) for i in range(4))

    def one_hot(rows, count):
        lanes = lax.broadcasted_iota(jnp.int32, (1, count), 1)
        return (seg_col[rows, :] == lax.rem(lanes, segs)).astype(FLOAT).astype(HALF)

    loads["cot"].wait()
    loads["modk"].wait()
    cot_own[...] = cot[own_rows, :]
    packs[at.dp] = jnp.zeros_like(packs[at.dp])

    def grad_b_block(index, total):
        rows = rows_at(index * share, share)
        gate = mm(one_hot(rows, 2 * segs), modk[5])
        value = (cot[rows, :].astype(FLOAT) * gate).astype(HALF)
        cot[rows, :] = value
        return total + jnp.sum(value.astype(FLOAT), axis=0, keepdims=True)

    packs[at.dp, 3:4, 0:width] = lax.fori_loop(0, blocks, grad_b_block, jnp.zeros((1, width), FLOAT))
    loads["act"].wait()

    def lanes_at(index):
        return pl.ds(pl.multiple_of(index * 128, 128), 128)

    def outer_grad_block(index, carry):
        whole_o[rows_at(index * 128, 128), :] = mm_tn(act[:, lanes_at(index)], cot[...]).astype(HALF)
        return carry

    lax.fori_loop(0, hidden // 128, outer_grad_block, 0)
    for piece in list_o:
        scatter.start(piece)
    load("hid_a", hid_a_in, act)
    loads["wo"].wait()
    loads["slope"].wait()
    loads["wi"].wait()

    def back_two(block):
        rows = rows_at(block * share, share)
        grad_act = mm_nt(cot[rows, :], wo[...])
        grad_pre = (grad_act * slope[rows, :].astype(FLOAT)).astype(HALF)
        slope[rows, :] = grad_pre
        return mm_nt(grad_pre, wi[...]), jnp.sum(grad_pre.astype(FLOAT), axis=0, keepdims=True)

    def core_copy(slot):
        return remote(part.at[slot], core_in.at[slot], sum_send.at[slot], sum_recv.at[slot], at.core_peer())

    y_copy = remote(y_out, y_in, sum_send.at[2], sum_recv.at[2], at.y_peer())

    def sum_shares(make, between, held):
        part[0] = make(at.share_of(True, True)).astype(HALF)
        core_copy(0).start()
        part[1] = make(at.share_of(False, True)).astype(HALF)
        core_copy(1).start()
        summed = make(at.share_of(True, False))
        core_copy(0).wait_recv()
        y_out[...] = (summed + core_in[0].astype(FLOAT)).astype(HALF)
        y_copy.start()
        summed = make(at.share_of(False, False))
        core_copy(1).wait_recv()
        held[...] = summed + core_in[1].astype(FLOAT)
        between()
        y_copy.wait_recv()
        core_copy(0).wait_send()
        core_copy(1).wait_send()
        y_copy.wait_send()
        return held[...] + y_in[...].astype(FLOAT)

    bias_total = [jnp.zeros((1, hidden), FLOAT)]

    def make_two(block):
        value, bias = back_two(block)
        bias_total[0] = bias_total[0] + bias
        return value

    def inner_grads():
        packs[at.dp, 1:2, 0:hidden] = bias_total[0]
        loads["hid_b"].wait()

        def inner_grad_block(index, carry):
            whole_i[rows_at(index * 128, 128), :] = mm_tn(hid_b[:, lanes_at(index)], slope[...]).astype(HALF)
            return carry

        lax.fori_loop(0, width // 128, inner_grad_block, 0)
        for piece in list_i:
            scatter.start(piece)

    grad_hid_b = sum_shares(make_two, inner_grads, grad_mid)

    loads["middle"].wait()
    loads["branch"].wait()
    loads["ff_own"].wait()
    chosen = one_hot(own_rows, 2 * segs)
    normed, inv_std = layer_norm(middle[...])
    grad_normed = grad_hid_b * (1.0 + mm(chosen, modk[4]))
    first_mean = jnp.mean(grad_normed, axis=-1, keepdims=True)
    second_mean = jnp.mean(grad_normed * normed, axis=-1, keepdims=True)
    grad_mid[...] = cot_own[...].astype(FLOAT) + inv_std * (grad_normed - first_mean - normed * second_mean)
    grad_a[own_rows, :] = (grad_mid[...] * mm(chosen, modk[2])).astype(HALF)

    def hid_rows(other_y, other_core):
        return grad_a.at[rows_at(at.share_of(other_y, other_core) * share, share)]

    own_hid = hid_rows(False, False)
    to_core = remote(own_hid, own_hid, gat_send.at[0], gat_recv.at[0], at.core_peer())
    to_y = remote(own_hid, own_hid, gat_send.at[1], gat_recv.at[1], at.y_peer())
    to_y.start()
    to_core.start()
    across, beside, far = hid_rows(True, False), hid_rows(False, True), hid_rows(True, True)
    onward = remote(across, across, gat_send.at[2], gat_recv.at[2], at.core_peer())

    images = one_hot(own_rows, segs)

    def keep_mod(group, values):
        sums = image_sums(images, values)
        for t in range(at.tensor_count):
            mod_send_buf[t, group] = sums[:, t * columns:(t + 1) * columns]

    keep_mod(2, grad_mid[...] * branch[...])
    keep_mod(3, grad_hid_b)
    keep_mod(4, grad_hid_b * normed)
    ff_copy.wait_recv()
    branch_b = ff_own[...] + ff_in[...].astype(FLOAT) + shared_bias[1:2, :]
    keep_mod(5, cot_own[...].astype(FLOAT) * branch_b)
    ff_in[...] = (middle[...] + mm(chosen, modk[5]) * branch_b).astype(HALF)

    def mod_copy(part_index, first, count, step):
        to = lax.rem(at.tensor + step, at.tensor_count)
        return remote(
            mod_send_buf.at[to, pl.ds(first, count)], mod_in.at[step - 1, pl.ds(first, count)],
            mod_send.at[part_index, step - 1], mod_recv.at[part_index, step - 1], at.tensor_peer(step),
        )

    def all_copy(part_index, ref, step):
        return remote(
            ref, ref, all_send.at[part_index, step - 1], all_recv.at[part_index, step - 1], dp_peer(step)
        )

    mod_parts = ((2, 4), (0, 2))

    def mod_start(part_index):
        first, count = mod_parts[part_index]
        for step in range(1, at.tensor_count):
            mod_copy(part_index, first, count, step).start()

    def mod_spread(part_index):
        first, count = mod_parts[part_index]
        total = mod_send_buf[at.tensor, first:first + count]
        for step in range(1, at.tensor_count):
            mod_copy(part_index, first, count, step).wait_recv()
            total = total + mod_in[step - 1, first:first + count]
        mods[at.dp, first:first + count] = total
        for step in range(1, at.dp_count):
            all_copy(part_index, mods.at[at.dp, pl.ds(first, count)], step).start()

    mod_start(0)
    for piece in list_o:
        scatter.pass_on(piece)
    remote(across, across, gat_send.at[1], gat_recv.at[1], at.y_peer()).wait_recv()
    onward.start()
    mod_spread(0)
    remote(beside, beside, gat_send.at[0], gat_recv.at[0], at.core_peer()).wait_recv()
    loads["wp"].wait()
    loads["att"].wait()
    remote(far, far, gat_send.at[2], gat_recv.at[2], at.core_peer()).wait_recv()

    def grad_att_block(index, total):
        rows = rows_at(index * share, share)
        values = mm_nt(grad_a[rows, :], wp[...])
        for head in range(nheads):
            gatt[head, rows, :] = values[:, head * HD:(head + 1) * HD].astype(HALF)
        return total + jnp.sum(grad_a[rows, :].astype(FLOAT), axis=0, keepdims=True)

    packs[at.dp, 2:3, 0:width] = lax.fori_loop(0, blocks, grad_att_block, jnp.zeros((1, width), FLOAT))
    proj_grad = mm_tn(att[...], grad_a[...]).astype(HALF)
    whole_p[...] = mm(place_back[...], proj_grad).astype(HALF)
    for piece in list_p:
        scatter.start(piece)
    loads["heads"].wait()
    loads["lse"].wait()

    def attend_back(head, carry):
        key_sum[...] = jnp.zeros_like(key_sum)
        value_sum[...] = jnp.zeros_like(value_sum)
        for block in range(blocks):
            low, high = block * share, (block + 1) * share
            first, end = max(0, low - SEG_MOST), min(tokens, high + SEG_MOST)
            query = heads[head, low:high, :]
            keys = heads[nheads + head, first:end, :]
            values = heads[2 * nheads + head, first:end, :]
            grad = gatt[head, low:high, :]
            same = seg_col[low:high, :] == seg_row[:, first:end]
            scores = jnp.where(same, mm_nt(query, keys) * scale, -1e30)
            lanes = lax.broadcasted_iota(jnp.int32, (1, nheads), 1)
            peak = jnp.sum(jnp.where(lanes == head, lse[low:high, :], 0.0), axis=-1, keepdims=True)
            probs = jnp.exp(scores - peak)
            grad_probs = mm_nt(grad, values)
            center = jnp.sum(probs * grad_probs, axis=-1, keepdims=True)
            grad_scores = (probs * (grad_probs - center)).astype(HALF)
            heads[head, low:high, :] = (mm(grad_scores, keys) * scale).astype(HALF)
            key_sum[first:end, :] += mm_tn(grad_scores, query)
            value_sum[first:end, :] += mm_tn(probs.astype(HALF), grad)
        heads[nheads + head] = (key_sum[...] * scale).astype(HALF)
        heads[2 * nheads + head] = value_sum[...].astype(HALF)
        return carry

    lax.fori_loop(0, nheads // 2, attend_back, 0)
    for piece in list_i + list_p:
        scatter.pass_on(piece)
    lax.fori_loop(nheads // 2, nheads, attend_back, 0)

    to_core.wait_send()
    to_y.wait_send()
    onward.wait_send()

    def join_block(index, total):
        rows = rows_at(index * share, share)
        values = jnp.concatenate([heads[head, rows, :].astype(FLOAT) for head in range(3 * nheads)], axis=1)
        grad_a[rows, 0:3 * columns] = values.astype(HALF)
        return total + jnp.sum(values, axis=0, keepdims=True)

    packs[at.dp, 0:1, 0:3 * columns] = lax.fori_loop(0, blocks, join_block, jnp.zeros((1, 3 * columns), FLOAT))
    unit = lax.broadcasted_iota(jnp.int32, (segs, 1), 0) == lax.broadcasted_iota(jnp.int32, (1, segs), 1)
    conds = sizes["conds"]
    packs[at.dp, 8:8 + segs, 0:conds] = mm_nt(unit.astype(FLOAT).astype(HALF), cond_picks(seg_cond, conds))
    for step in range(1, at.dp_count):
        all_copy(2, packs.at[at.dp], step).start()
    loads["hid_a"].wait()

    def qkv_grad_block(index, carry):
        whole_q[rows_at(index * 128, 128), :] = mm_tn(act[:, lanes_at(index)], grad_a[:, 0:3 * columns]).astype(HALF)
        return carry

    lax.fori_loop(0, width // 128, qkv_grad_block, 0)
    for piece in list_q:
        scatter.start(piece)
    loads["wq"].wait()

    saves = []

    def save(src, dst):
        copy = pltpu.make_async_copy(src, dst, save_sem.at[len(saves)])
        copy.start()
        saves.append(copy)

    save(ff_in, block_out)

    def store_totals(pieces_of, out):
        for piece in pieces_of:
            first, count = flat[piece][4], flat[piece][5]
            total = scatter.total(piece)
            if len(out.shape) == 2:
                out[first:first + count, :] = total
            else:
                for plane in range(out.shape[0]):
                    out[plane, first:first + count, :] = total[:, plane * columns:(plane + 1) * columns]

    grad_hid_a = sum_shares(
        lambda block: mm_nt(grad_a[rows_at(block * share, share), 0:3 * columns], wq[...]),
        lambda: store_totals(list_o, outer_out),
        branch,
    )
    loads["x"].wait()
    normed, inv_std = layer_norm(x_own[...].astype(FLOAT))
    grad_normed = grad_hid_a * (1.0 + mm(chosen, modk[1]))
    first_mean = jnp.mean(grad_normed, axis=-1, keepdims=True)
    second_mean = jnp.mean(grad_normed * normed, axis=-1, keepdims=True)
    grad_mid[...] = grad_mid[...] + inv_std * (grad_normed - first_mean - normed * second_mean)
    save(grad_mid, input_out)
    keep_mod(0, grad_hid_a)
    keep_mod(1, grad_hid_a * normed)
    mod_start(1)
    for piece in list_q:
        scatter.pass_on(piece)
    mod_spread(1)
    store_totals(list_i, inner_out)
    store_totals(list_p, proj_out)
    store_totals(list_q, qkv_out)

    for step in range(1, at.dp_count):
        source = lax.rem(at.dp + at.dp_count - step, at.dp_count)
        for part_index in range(2):
            first, count = mod_parts[part_index]
            all_copy(part_index, mods.at[source, pl.ds(first, count)], step).wait_recv()
        all_copy(2, packs.at[source], step).wait_recv()
    save(mods, mods_out)
    save(packs, packs_out)
    ff_copy.wait_send()
    for piece in range(len(flat)):
        scatter.finish(piece)
    for part_index in range(2):
        first, count = mod_parts[part_index]
        for step in range(1, at.tensor_count):
            mod_copy(part_index, first, count, step).wait_send()
        for step in range(1, at.dp_count):
            all_copy(part_index, mods.at[at.dp, pl.ds(first, count)], step).wait_send()
    for step in range(1, at.dp_count):
        all_copy(2, packs.at[at.dp], step).wait_send()
    for copy in saves:
        copy.wait()

def run_backward(sizes, block_input, seg_col, segment_ids, segment_cond, shared_biases, cotangent, kept):
    (wq, wp, wi, wo, hid_a, heads, lse, att, hid_b, act, slope, far, own, branch, middle, modk) = kept
    tokens, width, columns, share = (sizes[k] for k in ("tokens", "width", "columns", "share"))
    hidden, dp_count, tensor_count, segs = sizes["hidden"], sizes[DP], sizes[TP], sizes["segs"]
    nheads = columns // HD
    own_rows = columns // dp_count
    pad_rows = own_rows + -own_rows % 16
    xs = line_length(dp_count)
    zs = dp_count // xs
    shards = (hidden // dp_count, width // dp_count, pad_rows, width // dp_count)
    wholes = ((hidden, width), (width, hidden), (dp_count * pad_rows, width), (width, 3 * columns))
    units = sum(shard // unit_rows(shard) for shard in shards)
    place = jnp.asarray(placing(columns, own_rows, pad_rows, dp_count).T, HALF)
    pack_width = max(width, hidden, 3 * columns)
    shapes = [((share, width), HALF), ((share, width), FLOAT)]
    shapes += [((3, shards[3], columns), FLOAT)]
    shapes += [((shards[i], wholes[i][1]), FLOAT) for i in (2, 1, 0)]
    shapes += [((dp_count, 6, segs, columns), FLOAT), ((dp_count, 16, pack_width), FLOAT)]
    vmem, dma = pltpu.VMEM, pltpu.SemaphoreType.DMA
    scratch = [
        vmem((width, 3 * columns), HALF), vmem((columns, width), HALF), vmem((width, hidden), HALF),
        vmem((hidden, width), HALF), vmem((3 * nheads, tokens, HD), HALF), vmem((tokens, nheads), FLOAT),
        vmem((tokens, columns), HALF), vmem((tokens, width), HALF), vmem((tokens, hidden), HALF),
        vmem((tokens, hidden), HALF), vmem((tokens, width), HALF), vmem((6, 2 * segs, width), HALF),
        vmem((share, width), FLOAT), vmem((share, width), FLOAT), vmem((share, width), FLOAT),
        vmem((share, width), HALF), vmem((share, width), HALF), vmem((nheads, tokens, HD), HALF),
        vmem((tokens, HD), FLOAT), vmem((tokens, HD), FLOAT), vmem((tokens, width), HALF),
        vmem((2, share, width), HALF), vmem((2, share, width), HALF), vmem((share, width), HALF),
        vmem((share, width), HALF), vmem((share, width), HALF), vmem((share, width), FLOAT),
    ]
    scratch += [vmem(shape, HALF) for shape in wholes]
    scratch += [vmem((xs - 1, zs, shards[i], wholes[i][1]), HALF) for i in range(4)]
    scratch += [vmem((zs - 1, shards[i], wholes[i][1]), HALF) for i in range(4)]
    scratch += [
        vmem((tensor_count, 6, segs, columns), FLOAT), vmem((tensor_count - 1, 6, segs, columns), FLOAT),
        vmem((dp_count, 6, segs, columns), FLOAT), vmem((dp_count, 16, pack_width), FLOAT),
        dma((17,)), dma((4,)), dma((units, xs - 1, zs)), dma((units, xs - 1, zs)),
        dma((units, zs - 1)), dma((units, zs - 1)), dma((3,)), dma((3,)), dma((3,)), dma((3,)),
        dma(()), dma(()), dma((2, tensor_count - 1)), dma((2, tensor_count - 1)),
        dma((3, dp_count - 1)), dma((3, dp_count - 1)),
    ]
    return pl.pallas_call(
        functools.partial(backward_kernel, sizes),
        out_shape=[jax.ShapeDtypeStruct(s, t) for s, t in shapes],
        in_specs=[vmem_spec()] * 5 + [any_spec()] * 18,
        out_specs=[any_spec()] * 2 + [vmem_spec()] * 4 + [any_spec()] * 2,
        scratch_shapes=scratch,
        name="backward",
        compiler_params=pltpu.CompilerParams(
            collective_id=2, has_side_effects=True, vmem_limit_bytes=VMEM_BYTES
        ),
    )(
        seg_col, segment_ids, segment_cond, shared_biases, place, block_input, cotangent, wq, wp, wi, wo, hid_a, heads, lse, att, hid_b, act, slope, far, own,
        branch, middle, modk,
    )


def on_device_general(
    block_input,
    conditions,
    segment_ids,
    segment_cond,
    cotangent,
    qkv_weight,
    proj_weight,
    inner_weight,
    outer_weight,
    ada_weight,
    head_biases,
    inner_bias,
    shared_biases,
    qkv_first,
    proj_first,
    inner_first,
    outer_first,
    ada_first,
    head_biases_first,
    inner_bias_first,
    shared_biases_first,
    qkv_second,
    proj_second,
    inner_second,
    outer_second,
    ada_second,
    head_biases_second,
    inner_bias_second,
    shared_biases_second,
):
    columns = qkv_weight.shape[2]
    heads_local = columns // HD
    rows_local = segment_ids.shape[0]
    row_length = segment_ids.shape[1]
    token_count = rows_local * row_length
    seg_count = segment_cond.shape[1]
    width = block_input.shape[1]
    share_count = token_count // lax.axis_size(TP)
    share_start = lax.axis_index(TP) * share_count

    def share(values):
        return lax.dynamic_slice_in_dim(values, share_start, share_count, 0)

    qkv_full, proj_full, inner_full, outer_full = (
        lax.all_gather(qkv_weight.astype(HALF), DP, axis=0, tiled=True),
        lax.all_gather(proj_weight.astype(HALF), DP, axis=0, tiled=True),
        lax.all_gather(inner_weight.astype(HALF), DP, axis=0, tiled=True),
        lax.all_gather(outer_weight.astype(HALF), DP, axis=0, tiled=True),
    )
    condition_select = (
        segment_cond[:, :, None] == jnp.arange(conditions.shape[0])[None, None, :]
    ).astype(FLOAT)
    condition_row_block = jnp.einsum(
        "btu,ua->bta", condition_select, conditions, precision=PRECISION_MAX
    )
    cond_act = silu(condition_row_block)
    local_mod = (
        jnp.einsum("rsd,kcd->rskc", cond_act, ada_weight, precision=PRECISION_MAX)
        + head_biases[3:][None, None]
    )
    full_mod = lax.all_gather(local_mod, TP, axis=3, tiled=True)
    seg_pick = (segment_ids[:, :, None] == jnp.arange(seg_count)[None, None, :]).astype(FLOAT)
    token_mod = jnp.einsum("rls,rskd->rlkd", seg_pick, full_mod, precision=PRECISION_MAX).reshape(
        token_count, 6, width
    )
    inputs = block_input.astype(FLOAT)
    normed_one, inv_one = normalize(inputs)
    hidden_one = (normed_one * (1.0 + token_mod[:, 1]) + token_mod[:, 0]).astype(HALF)
    qkv_values = (
        jnp.einsum("nd,dkc->nkc", hidden_one, qkv_full, preferred_element_type=FLOAT)
        + head_biases[:3][None]
    ).astype(HALF)
    row_qkv = qkv_values.reshape(rows_local, row_length, 3, heads_local, HD)
    row = 0
    attended_row, total_row = attend_forward(row_qkv[row], segment_ids[row])
    attended_rows = [attended_row]
    total_rows = [total_row]
    attended = jnp.stack(attended_rows).reshape(token_count, columns).astype(HALF)
    attn_partial = jnp.dot(attended, proj_full, preferred_element_type=FLOAT)
    share_mod = share(token_mod)
    branch_one = sum_to_shares(attn_partial) + shared_biases[0]
    middle = share(inputs) + share_mod[:, 2] * branch_one
    normed_two, inv_two = normalize(middle)
    hidden_two_share = (normed_two * (1.0 + share_mod[:, 4]) + share_mod[:, 3]).astype(HALF)
    hidden_two = lax.all_gather(hidden_two_share, TP, axis=0, tiled=True)
    pre_act = jnp.dot(hidden_two, inner_full, preferred_element_type=FLOAT) + inner_bias
    act_values, gelu_back = jax.vjp(gelu_tanh, pre_act)
    act_low = act_values.astype(HALF)
    ff_partial = jnp.dot(act_low, outer_full, preferred_element_type=FLOAT)
    branch_two = sum_to_shares(ff_partial) + shared_biases[1]
    output = middle + share_mod[:, 5] * branch_two
    grad_out = cotangent.astype(FLOAT)
    grad_two = (grad_out * token_mod[:, 5]).astype(HALF)
    outer_grad = jnp.einsum("nf,nd->fd", act_low, grad_two, preferred_element_type=FLOAT)
    grad_act = jnp.einsum("nd,fd->nf", grad_two, outer_full, preferred_element_type=FLOAT)
    grad_pre = gelu_back(grad_act)[0].astype(HALF)
    inner_grad = jnp.einsum("nd,nf->df", hidden_two, grad_pre, preferred_element_type=FLOAT)
    back_two_partial = jnp.einsum("nf,df->nd", grad_pre, inner_full, preferred_element_type=FLOAT)
    grad_hidden_two = sum_to_shares(back_two_partial)
    grad_out_share = share(grad_out)
    grad_middle = grad_out_share + norm_back(
        grad_hidden_two * (1.0 + share_mod[:, 4]), normed_two, inv_two
    )
    grad_one_share = (grad_middle * share_mod[:, 2]).astype(HALF)
    grad_one = lax.all_gather(grad_one_share, TP, axis=0, tiled=True)
    proj_grad = jnp.einsum("nc,nd->cd", attended, grad_one, preferred_element_type=FLOAT)
    grad_attended = jnp.einsum(
        "nd,cd->nc", grad_one, proj_full, preferred_element_type=FLOAT
    ).astype(HALF)
    grad_rows = grad_attended.reshape(rows_local, row_length, heads_local, HD)
    row = 0
    grad_qkv_rows = [
        attend_backward(row_qkv[row], segment_ids[row], grad_rows[row], total_rows[row])
    ]
    grad_qkv = jnp.stack(grad_qkv_rows).reshape(token_count, 3, columns).astype(HALF)
    qkv_grad = jnp.einsum("nd,nkc->dkc", hidden_one, grad_qkv, preferred_element_type=FLOAT)
    back_one_partial = jnp.einsum("nkc,dkc->nd", grad_qkv, qkv_full, preferred_element_type=FLOAT)
    grad_hidden_one = sum_to_shares(back_one_partial)
    normed_one_share, inv_one_share = share(normed_one), share(inv_one)
    input_out = grad_middle + norm_back(
        grad_hidden_one * (1.0 + share_mod[:, 1]), normed_one_share, inv_one_share
    )
    block_out = output.astype(HALF)
    contributions = jnp.concatenate(
        [
            grad_hidden_one,
            grad_hidden_one * normed_one_share,
            grad_middle * branch_one,
            grad_hidden_two,
            grad_hidden_two * normed_two,
            grad_out_share * branch_two,
        ],
        axis=1,
    )
    pick_share = share(seg_pick.reshape(token_count, seg_count))
    cond_pick = jnp.dot(pick_share, condition_select[0], precision=PRECISION_MAX)
    cond_sums = jnp.einsum("lq,lc->qc", cond_pick, contributions, precision=PRECISION_MAX)
    cond_sums = cond_sums.reshape(-1, 6, lax.axis_size(TP), columns)
    cond_sums = lax.psum_scatter(cond_sums, TP, scatter_dimension=2, tiled=True)[:, :, 0]
    cond_total = lax.psum(cond_sums, DP)
    all_act, all_silu_back = jax.vjp(silu, conditions)
    grad_all_act = jnp.einsum("qkc,kcd->qd", cond_total, ada_weight, precision=PRECISION_MAX)
    cond_grad = all_silu_back(lax.psum(grad_all_act, TP))[0]
    head_bias_grad = jnp.sum(grad_qkv.astype(FLOAT), axis=0)
    inner_bias_grad = jnp.sum(grad_pre.astype(FLOAT), axis=0)
    shared_bias_grad = jnp.stack(
        [jnp.sum(grad_one.astype(FLOAT), axis=0), jnp.sum(grad_two.astype(FLOAT), axis=0)]
    )
    ada_total = jnp.einsum("qd,qkc->kcd", all_act, cond_total, precision=PRECISION_MAX)
    head_total, inner_bias_total, shared_total = lax.psum(
        (head_bias_grad, inner_bias_grad, shared_bias_grad), DP
    )
    head_total = jnp.concatenate([head_total, jnp.sum(cond_total, axis=0)], axis=0)
    qkv_shard, proj_shard, inner_shard, outer_shard = (
        sum_to_owners(qkv_grad),
        sum_to_owners(proj_grad),
        sum_to_owners(inner_grad),
        sum_to_owners(outer_grad),
    )
    qkv_new = adam_update(qkv_weight, qkv_shard, qkv_first, qkv_second, RATES[0])
    proj_new = adam_update(proj_weight, proj_shard, proj_first, proj_second, RATES[1])
    inner_new = adam_update(inner_weight, inner_shard, inner_first, inner_second, RATES[2])
    outer_new = adam_update(outer_weight, outer_shard, outer_first, outer_second, RATES[3])
    ada_new = adam_update(ada_weight, ada_total, ada_first, ada_second, RATES[4])
    head_new = adam_update(head_biases, head_total, head_biases_first, head_biases_second, RATES[5])
    inner_bias_new = adam_update(
        inner_bias, inner_bias_total, inner_bias_first, inner_bias_second, RATES[6]
    )
    shared_new = adam_update(
        shared_biases, shared_total, shared_biases_first, shared_biases_second, RATES[7]
    )
    return (
        block_out,
        input_out,
        cond_grad,
        qkv_new[0],
        proj_new[0],
        inner_new[0],
        outer_new[0],
        ada_new[0],
        head_new[0],
        inner_bias_new[0],
        shared_new[0],
        qkv_new[1],
        proj_new[1],
        inner_new[1],
        outer_new[1],
        ada_new[1],
        head_new[1],
        inner_bias_new[1],
        shared_new[1],
        qkv_new[2],
        proj_new[2],
        inner_new[2],
        outer_new[2],
        ada_new[2],
        head_new[2],
        inner_bias_new[2],
        shared_new[2],
        qkv_new[0].astype(HALF),
        proj_new[0].astype(HALF),
        inner_new[0].astype(HALF),
        outer_new[0].astype(HALF),
    )


def update_kernel(
    sizes,
    cond_ref, mods, packs, head_w, head_m, head_v, hidden_w, hidden_m, hidden_v, shared_w, shared_m, shared_v,
    *refs,
):
    width, columns, segs, hidden = sizes["width"], sizes["columns"], sizes["segs"], sizes["hidden"]
    big_in = [refs[i * 4:i * 4 + 4] for i in range(4)]
    ada_in = refs[16:19]
    part, *small_out = refs[19:29]
    ada_out = refs[29:32]
    big_out = [refs[32 + i * 4:36 + i * 4] for i in range(4)]
    refs = refs[48:]
    ada = refs[:3]
    big = [refs[3 + i * 5:8 + i * 5] for i in range(4)]
    gt, act_rows, head_grad = refs[23:26]
    ada_load, ada_save, big_load, big_save = refs[26:]
    conds, dp_count = cond_ref.shape[0], sizes[DP]

    def ada_copy(kind, group):
        return pltpu.make_async_copy(ada_in[kind].at[group], ada[kind].at[group], ada_load.at[kind, group])

    for group in range(6):
        ada_copy(0, group).start()
    for group in range(6):
        ada_copy(1, group).start()
        ada_copy(2, group).start()
    big_loads = []
    for index in range(4):
        copies = [
            pltpu.make_async_copy(big_in[index][kind], big[index][kind], big_load.at[index, kind])
            for kind in range(4)
        ]
        for copy in copies:
            copy.start()
        big_loads.append(copies)

    act = silu(cond_ref[...])
    act_high, act_low = split_two(act)
    act_rows[...] = jnp.concatenate([act_high, act_high, act_low], axis=0)
    picked = jnp.concatenate(
        [packs[row, 8:8 + segs, 0:conds] for row in range(dp_count)], axis=0
    ).astype(HALF)
    for group in range(6):
        images = jnp.concatenate([mods[row, group] for row in range(dp_count)], axis=0)
        head_grad[3 + group:4 + group, :] = jnp.sum(images, axis=0, keepdims=True)
        high, low = split_two(images)
        sums_high, sums_low = split_two(mm_tn(high, picked) + mm_tn(low, picked))
        gt[group] = jnp.concatenate([sums_high, sums_low, sums_high], axis=1)

    part[...] = jnp.zeros_like(part)
    for group in range(6):
        ada_copy(0, group).wait()
        weight_high, weight_low = split_two(ada[0][group])
        both = mm_tn(gt[group, :, 0:2 * conds], weight_high)
        part[...] += both[:conds] + both[conds:] + mm_tn(gt[group, :, 0:conds], weight_low)

    def update(values, rate, grad):
        weight, first, second = values
        return adam_update(weight, grad, first, second, rate)

    tile = 96 if columns % 96 == 0 else columns
    saves = []

    def ada_group(group):
        for kind in (1, 2):
            ada_copy(kind, group).wait()

        def ada_tile(index, carry):
            rows = pl.ds(pl.multiple_of(index * tile, 8), tile)
            grad = mm(gt[group, rows, :], act_rows[...])
            new = update([ref[group, rows, :] for ref in ada], RATES[4], grad)
            for ref, value in zip(ada, new, strict=True):
                ref[group, rows, :] = value
            return carry

        lax.fori_loop(0, columns // tile, ada_tile, 0)
        for kind in range(3):
            copy = pltpu.make_async_copy(ada[kind].at[group], ada_out[kind].at[group], ada_save.at[kind, group])
            copy.start()
            saves.append(copy)

    for group in range(6):
        ada_group(group)

    pack = packs[0, 0:8, :]
    for row in range(1, dp_count):
        pack = pack + packs[row, 0:8, :]
    for part_index in range(3):
        head_grad[part_index:part_index + 1, :] = pack[0:1, part_index * columns:(part_index + 1) * columns]
    smalls = (
        ((head_w, head_m, head_v), RATES[5], head_grad[...]),
        ((hidden_w, hidden_m, hidden_v), RATES[6], pack[1:2, 0:hidden].reshape(hidden_w.shape)),
        ((shared_w, shared_m, shared_v), RATES[7], pack[2:4, 0:width]),
    )
    for index, (kinds, rate, grad) in enumerate(smalls):
        for kind, value in enumerate(update([ref[...] for ref in kinds], rate, grad)):
            small_out[index * 3 + kind][...] = value

    for index in range(4):
        for copy in big_loads[index]:
            copy.wait()
        weight, first, second, grad, low = big[index]
        planes = weight.shape[0] if len(weight.shape) == 3 else 0
        for plane in range(max(planes, 1)):
            where = (plane,) if planes else (slice(0, weight.shape[0]),)
            gradient = grad[plane] if planes else grad[0:weight.shape[0], :]
            new = update([ref[where] for ref in (weight, first, second)], RATES[index], gradient)
            for ref, value in zip((weight, first, second), new, strict=True):
                ref[where] = value
            low[where] = new[0].astype(HALF)
        for kind, ref in enumerate((weight, first, second, low)):
            copy = pltpu.make_async_copy(ref, big_out[index][kind], big_save.at[index, kind])
            copy.start()
            saves.append(copy)

    for copy in saves:
        copy.wait()


def run_update(sizes, conditions, mods, packs, smalls, bigs, ada):
    width, columns, segs = sizes["width"], sizes["columns"], sizes["segs"]
    conds = conditions.shape[0]
    vmem, dma = pltpu.VMEM, pltpu.SemaphoreType.DMA
    flat_small = [array for kinds in smalls for array in kinds]
    flat_big = [array for kinds in bigs for array in kinds]

    def like(array, dtype=FLOAT):
        return jax.ShapeDtypeStruct(array.shape, dtype)

    outs = [like(conditions)] + [like(a) for a in flat_small] + [like(a) for a in ada]
    for weight, first, second, grad in bigs:
        outs += [like(weight), like(first), like(second), like(weight, HALF)]
    scratch = [vmem(array.shape, FLOAT) for array in ada]
    for kinds in bigs:
        scratch += [vmem(array.shape, FLOAT) for array in kinds] + [vmem(kinds[0].shape, HALF)]
    scratch += [
        vmem((6, columns, 3 * conds), HALF), vmem((3 * conds, width), HALF), vmem((9, columns), FLOAT),
        dma((3, 6)), dma((3, 6)), dma((4, 4)), dma((4, 4)),
    ]
    return pl.pallas_call(
        functools.partial(update_kernel, sizes),
        out_shape=outs,
        in_specs=[vmem_spec()] * 12 + [any_spec()] * 19,
        out_specs=[vmem_spec()] * 10 + [any_spec()] * 19,
        scratch_shapes=scratch,
        name="update",
        compiler_params=pltpu.CompilerParams(vmem_limit_bytes=VMEM_BYTES),
    )(conditions, mods, packs, *flat_small, *flat_big, *ada)


def cond_kernel(sizes, cond_ref, part_in, cond_out, part, landing, result, out_send, out_recv, back_send, back_recv):
    at = Place(sizes[DP], sizes[TP])
    slice_rows = cond_ref.shape[0] // at.tensor_count
    part[...] = part_in[...]
    greet([at.tensor_peer(s) for s in range(1, at.tensor_count)])

    def slice_at(index):
        return pl.ds(pl.multiple_of(index * slice_rows, 8), slice_rows)

    def out_copy(step):
        to = lax.rem(at.tensor + step, at.tensor_count)
        return remote(
            part.at[slice_at(to)], landing.at[step - 1], out_send.at[step - 1], out_recv.at[step - 1],
            at.tensor_peer(step),
        )

    def back_copy(step, owner):
        rows = result.at[slice_at(owner)]
        return remote(rows, rows, back_send.at[step - 1], back_recv.at[step - 1], at.tensor_peer(step))

    for step in range(1, at.tensor_count):
        out_copy(step).start()

    total = part[slice_at(at.tensor), :]
    for step in range(1, at.tensor_count):
        out_copy(step).wait_recv()
        total = total + landing[step - 1]
    own = cond_ref[slice_at(at.tensor), :]
    gate = 1.0 / (1.0 + jnp.exp(-own))
    result[slice_at(at.tensor), :] = total * (gate * (1.0 + own * (1.0 - gate)))
    for step in range(1, at.tensor_count):
        back_copy(step, at.tensor).start()
    for step in range(1, at.tensor_count):
        back_copy(step, lax.rem(at.tensor + at.tensor_count - step, at.tensor_count)).wait_recv()
    cond_out[...] = result[...]
    for step in range(1, at.tensor_count):
        out_copy(step).wait_send()
        back_copy(step, at.tensor).wait_send()


def run_cond(sizes, conditions, part):
    tensor_count, vmem, dma = sizes[TP], pltpu.VMEM, pltpu.SemaphoreType.DMA
    shape = conditions.shape
    return pl.pallas_call(
        functools.partial(cond_kernel, sizes),
        out_shape=jax.ShapeDtypeStruct(shape, FLOAT),
        in_specs=[vmem_spec()] * 2,
        out_specs=vmem_spec(),
        scratch_shapes=[
            vmem(shape, FLOAT), vmem((tensor_count - 1, shape[0] // tensor_count, shape[1]), FLOAT),
            vmem(shape, FLOAT), *[dma((tensor_count - 1,))] * 4,
        ],
        name="cond",
        compiler_params=pltpu.CompilerParams(collective_id=3, has_side_effects=True),
    )(conditions, part)


def on_device_kernels(
    block_input, conditions, segment_ids, segment_cond, cotangent, qkv_weight, proj_weight, inner_weight,
    outer_weight, ada_weight, head_biases, inner_bias, shared_biases, *moments,
):
    firsts, seconds = moments[:8], moments[8:]
    sizes = sizes_of(block_input, conditions, segment_ids, segment_cond, qkv_weight, inner_weight)
    seg_col = segment_ids.reshape(-1, 1)

    def planes(array):
        return array.transpose(1, 0, 2)

    kept = run_forward(
        sizes, block_input, seg_col, segment_ids, segment_cond, conditions, ada_weight, head_biases, inner_bias,
        shared_biases, planes(qkv_weight), proj_weight, inner_weight, outer_weight,
    )
    block_out, input_out, *grads, mods, packs = run_backward(
        sizes, block_input, seg_col, segment_ids, segment_cond, shared_biases, cotangent, kept
    )
    weights = (qkv_weight, proj_weight, inner_weight, outer_weight)
    bigs = [[w, m, v, g] for w, m, v, g in zip(weights, firsts[:4], seconds[:4], grads, strict=True)]
    bigs[0][:3] = [planes(array) for array in bigs[0][:3]]
    smalls = list(zip((head_biases, inner_bias, shared_biases), firsts[5:], seconds[5:], strict=True))
    cond_part, *news = run_update(
        sizes, conditions, mods, packs, smalls, bigs, (ada_weight, firsts[4], seconds[4])
    )
    small_new, ada_new, big_new = news[:9], news[9:12], news[12:]
    big_new[:4] = [planes(array) for array in big_new[:4]]
    outs = [block_out, input_out, run_cond(sizes, conditions, cond_part)]
    for kind in range(3):
        outs += [big_new[4 * i + kind] for i in range(4)]
        outs += [ada_new[kind]] + [small_new[3 * i + kind] for i in range(3)]
    return (*outs, *big_new[3::4])


def on_device(*args):
    sizes = sizes_of(args[0], args[1], args[2], args[3], args[5], args[7])
    return (on_device_kernels if kernels_fit(sizes) else on_device_general)(*args)


def solution(mesh):
    in_specs = (
        P(DP, None),
        P(),
        P(DP, None),
        P(DP, None),
        P(DP, None),
        P(DP, None, TP),
        P((TP, DP), None),
        P(DP, TP),
        P((TP, DP), None),
        P(None, TP, None),
        P(None, TP),
        P(TP),
        P(),
        P(DP, None, TP),
        P((TP, DP), None),
        P(DP, TP),
        P((TP, DP), None),
        P(None, TP, None),
        P(None, TP),
        P(TP),
        P(),
        P(DP, None, TP),
        P((TP, DP), None),
        P(DP, TP),
        P((TP, DP), None),
        P(None, TP, None),
        P(None, TP),
        P(TP),
        P(),
    )
    out_specs = (
        P((DP, TP), None),
        P((DP, TP), None),
        P(),
        P(DP, None, TP),
        P((TP, DP), None),
        P(DP, TP),
        P((TP, DP), None),
        P(None, TP, None),
        P(None, TP),
        P(TP),
        P(),
        P(DP, None, TP),
        P((TP, DP), None),
        P(DP, TP),
        P((TP, DP), None),
        P(None, TP, None),
        P(None, TP),
        P(TP),
        P(),
        P(DP, None, TP),
        P((TP, DP), None),
        P(DP, TP),
        P((TP, DP), None),
        P(None, TP, None),
        P(None, TP),
        P(TP),
        P(),
        P(DP, None, TP),
        P((TP, DP), None),
        P(DP, TP),
        P((TP, DP), None),
    )
    return jax.shard_map(
        on_device, mesh=mesh, in_specs=in_specs, out_specs=out_specs, check_vma=False
    )
```

```python
import functools
import math

import jax
import jax.numpy as jnp
import numpy as np
from jax import lax
from jax.experimental import pallas as pl
from jax.experimental.pallas import tpu as pltpu
from jax.sharding import PartitionSpec as P

HD = 72
STEP = 10


BETA_ONE = 0.5
BETA_TWO = 0.6
ADAM_EPS = 1e-08
DECAY = 0.01
NORM_EPSILON = 1e-06
RATES = (0.04, 0.3, 0.04, 0.04, 0.04, 0.4, 0.4, 0.4)
PRECISION_MAX = lax.Precision.HIGHEST
FLOAT = jnp.float32
HALF = jnp.bfloat16
DP, TP = "dp", "tensor"


def silu(values):
    return values / (1.0 + jnp.exp(-values))


def gelu_tanh(values):
    inner = math.sqrt(2.0 / math.pi) * (values + 0.044715 * values * values * values)
    return 0.5 * values * (1.0 + jnp.tanh(inner))


def normalize(values):
    centered = values - jnp.mean(values, axis=-1, keepdims=True)
    inv_std = lax.rsqrt(jnp.mean(centered * centered, axis=-1, keepdims=True) + NORM_EPSILON)
    return (centered * inv_std, inv_std)


def norm_back(grad_normed, normed, inv_std):
    first_mean = jnp.mean(grad_normed, axis=-1, keepdims=True)
    second_mean = jnp.mean(grad_normed * normed, axis=-1, keepdims=True)
    return inv_std * (grad_normed - first_mean - normed * second_mean)


def block_scores(query_block, keys, query_segs, key_segs):
    scores = jnp.einsum("qhe,khe->hqk", query_block, keys, preferred_element_type=FLOAT) * (
        1.0 / math.sqrt(HD)
    )
    same = query_segs[:, None] == key_segs[None, :]
    return jnp.where(same[None], scores, -1e30)


def attend_forward(row_qkv, row_segs):
    queries = row_qkv[:, 0]
    keys = row_qkv[:, 1]
    values = row_qkv[:, 2]
    length = queries.shape[0]
    heads_local = queries.shape[1]
    block = min(512, length)
    blocks = length // block

    def one_block(pieces):
        query_block, query_segs = pieces
        scores = block_scores(query_block, keys, query_segs, row_segs)
        top = jnp.max(scores, axis=-1, keepdims=True)
        expo = jnp.exp(scores - top)
        total = jnp.sum(expo, axis=-1, keepdims=True)
        probs = (expo / total).astype(HALF)
        attended = jnp.einsum("hqk,khe->qhe", probs, values, preferred_element_type=FLOAT)
        return (attended, (top + jnp.log(total))[:, :, 0])

    attended, log_totals = lax.map(
        one_block,
        (queries.reshape(blocks, block, heads_local, HD), row_segs.reshape(blocks, block)),
    )
    return (attended.reshape(length, heads_local, HD), log_totals)


def attend_backward(row_qkv, row_segs, grad_row, log_totals):
    queries = row_qkv[:, 0]
    keys = row_qkv[:, 1]
    values = row_qkv[:, 2]
    length = queries.shape[0]
    heads_local = queries.shape[1]
    block = min(512, length)
    blocks = length // block
    scale = 1.0 / math.sqrt(HD)

    def one_block(carry, pieces):
        key_sum, value_sum = carry
        query_block, query_segs, grad_block, block_total = pieces
        scores = block_scores(query_block, keys, query_segs, row_segs)
        probs = jnp.exp(scores - block_total[:, :, None])
        grad_probs = jnp.einsum("qhe,khe->hqk", grad_block, values, preferred_element_type=FLOAT)
        center = jnp.sum(probs * grad_probs, axis=-1, keepdims=True)
        grad_scores = (probs * (grad_probs - center)).astype(HALF)
        grad_query = (
            jnp.einsum("hqk,khe->qhe", grad_scores, keys, preferred_element_type=FLOAT) * scale
        )
        key_sum = (
            key_sum
            + jnp.einsum("hqk,qhe->khe", grad_scores, query_block, preferred_element_type=FLOAT)
            * scale
        )
        value_sum = value_sum + jnp.einsum(
            "hqk,qhe->khe", probs.astype(HALF), grad_block, preferred_element_type=FLOAT
        )
        return ((key_sum, value_sum), grad_query)

    zeros = jnp.zeros((length, heads_local, HD), FLOAT)
    sums, grad_queries = lax.scan(
        one_block,
        (zeros, zeros),
        (
            queries.reshape(blocks, block, heads_local, HD),
            row_segs.reshape(blocks, block),
            grad_row.reshape(blocks, block, heads_local, HD),
            log_totals,
        ),
    )
    return jnp.stack([grad_queries.reshape(length, heads_local, HD), sums[0], sums[1]], axis=1)


def adam_update(weight, grad, first, second, rate):
    first_new = BETA_ONE * first + (1.0 - BETA_ONE) * grad
    second_new = BETA_TWO * second + (1.0 - BETA_TWO) * grad * grad
    fix_one = 1.0 - BETA_ONE**STEP
    fix_two = 1.0 - BETA_TWO**STEP
    update = first_new / fix_one / (jnp.sqrt(second_new / fix_two) + ADAM_EPS)
    return (weight - rate * (update + DECAY * weight), first_new, second_new)


def sum_to_shares(partial):
    return lax.psum_scatter(
        partial.astype(HALF), TP, scatter_dimension=0, tiled=True
    ).astype(FLOAT)


def sum_to_owners(partial):
    return lax.psum_scatter(
        partial.astype(HALF), DP, scatter_dimension=0, tiled=True
    ).astype(FLOAT)


SEG_MOST = 256
CORES = 2
MESH = pl.DeviceIdType.MESH
NT_DIMS = (((1,), (1,)), ((), ()))
TN_DIMS = (((0,), (0,)), ((), ()))
VMEM_BYTES = 62 * 1024 * 1024


def line_length(count):
    length = 1
    while (2 * length) ** 2 <= count:
        length *= 2
    return length


def mm(left, right):
    return jnp.dot(left, right, preferred_element_type=FLOAT)


def mm_nt(left, right):
    return lax.dot_general(left, right, NT_DIMS, preferred_element_type=FLOAT)


def mm_tn(left, right):
    return lax.dot_general(left, right, TN_DIMS, preferred_element_type=FLOAT)


def split_two(values):
    high = values.astype(HALF)
    return high, (values - high.astype(FLOAT)).astype(HALF)


def cond_picks(seg_cond, conds):
    return (lax.broadcasted_iota(jnp.int32, (conds, 1), 0) == seg_cond[...]).astype(FLOAT).astype(HALF)


def pick_rows(picks, values):
    high, rest = split_two(values)
    middle, low = split_two(values - high.astype(FLOAT))
    return mm_tn(picks, high) + mm_tn(picks, middle) + mm_tn(picks, low)


class Place:
    def __init__(self, dp_count, tensor_count):
        self.dp_count, self.tensor_count = dp_count, tensor_count
        self.xs = line_length(dp_count)
        self.zs = dp_count // self.xs
        self.ys = tensor_count // CORES
        self.dp, self.tensor = lax.axis_index(DP), lax.axis_index(TP)
        self.z, self.x = lax.div(self.dp, self.xs), lax.rem(self.dp, self.xs)
        self.y, self.core = lax.div(self.tensor, CORES), lax.rem(self.tensor, CORES)

    def z_of(self, step):
        return lax.rem(self.z + step + self.zs, self.zs)

    def x_of(self, step):
        return lax.rem(self.x + step + self.xs, self.xs)

    def z_peer(self, step):
        return (self.z_of(step) * self.xs + self.x, self.tensor)

    def x_peer(self, step):
        return (self.z * self.xs + self.x_of(step), self.tensor)

    def tensor_peer(self, step):
        return (self.dp, lax.rem(self.tensor + step, self.tensor_count))

    def core_peer(self):
        return (self.dp, self.y * CORES + 1 - self.core)

    def y_peer(self):
        return (self.dp, (1 - self.y) * CORES + self.core)

    def share_of(self, other_y, other_core):
        y = 1 - self.y if other_y else self.y
        core = 1 - self.core if other_core else self.core
        return y * CORES + core


def greet(peers):
    barrier = pltpu.get_barrier_semaphore()
    for peer in peers:
        pl.semaphore_signal(barrier, inc=1, device_id=peer, device_id_type=MESH)
    pl.semaphore_wait(barrier, len(peers))


def remote(src, dst, sends, recvs, peer):
    return pltpu.make_async_remote_copy(
        src_ref=src, dst_ref=dst, send_sem=sends, recv_sem=recvs, device_id=peer, device_id_type=MESH
    )


def rows_at(start, count):
    return pl.ds(pl.multiple_of(start, 16), count)


def unit_rows(shard):
    return 48 if shard % 48 == 0 else shard


class Gather:
    def __init__(self, place, pieces, z_sems, x_sems):
        self.place, self.pieces = place, pieces
        self.z_send, self.z_recv = z_sems
        self.x_send, self.x_recv = x_sems
        self.hops = place.zs - 1
        self.ticks = 0

    def slot(self, piece, z, x):
        full, shard, first, count = self.pieces[piece]
        return full.at[rows_at((z * self.place.xs + x) * shard + first, count)]

    def hop(self, piece, source, step, sem):
        at = self.place
        chunk = self.slot(piece, source, at.x)
        return remote(chunk, chunk, self.z_send.at[piece, sem], self.z_recv.at[piece, sem], at.z_peer(step))

    def x_copy(self, piece, source, step):
        at = self.place
        chunk = self.slot(piece, source, at.x)
        sems = self.x_send.at[piece, source, step - 1], self.x_recv.at[piece, source, step - 1]
        return remote(chunk, chunk, *sems, at.x_peer(step))

    def x_landing(self, piece, source, step):
        at = self.place
        chunk = self.slot(piece, source, at.x_of(-step))
        sems = self.x_send.at[piece, source, step - 1], self.x_recv.at[piece, source, step - 1]
        return remote(chunk, chunk, *sems, at.x_peer(step))

    def along_x(self, piece, source):
        for step in range(1, self.place.xs):
            self.x_copy(piece, source, step).start()

    def start(self, piece):
        at = self.place

        @pl.when(at.z < at.zs - 1)
        def _():
            self.hop(piece, at.z, 1, 0).start()

        @pl.when(at.z > 0)
        def _():
            self.hop(piece, at.z, -1, self.hops).start()

        self.along_x(piece, at.z)

    def pass_on(self, piece, away):
        at, hops = self.place, self.hops

        @pl.when(at.z >= away)
        def _():
            self.hop(piece, at.z - away, 1, away - 1).wait_recv()
            if away < hops:
                @pl.when(at.z < at.zs - 1)
                def _():
                    self.hop(piece, at.z - away, 1, away).start()
            self.along_x(piece, at.z - away)

        @pl.when(at.z + away < at.zs)
        def _():
            self.hop(piece, at.z + away, -1, hops + away - 1).wait_recv()
            if away < hops:
                @pl.when(at.z > 0)
                def _():
                    self.hop(piece, at.z + away, -1, hops + away).start()
            self.along_x(piece, at.z + away)

    def tick(self):
        now = self.ticks
        for away in range(1, self.hops + 1):
            if 0 <= now - away + 1 < len(self.pieces):
                self.pass_on(now - away + 1, away)
        if now + 3 < len(self.pieces):
            self.start(now + 3)
        self.ticks += 1

    def tick_until(self, piece):
        while self.ticks < min(piece, len(self.pieces) - 1) + self.hops:
            self.tick()

    def arrive(self, piece):
        at = self.place
        for source in range(at.zs):
            for step in range(1, at.xs):
                self.x_landing(piece, source, step).wait_recv()

    def finish(self, piece):
        at, hops = self.place, self.hops
        for away in range(hops):
            @pl.when((at.z >= away) & (at.z < at.zs - 1))
            def _(away=away):
                self.hop(piece, at.z - away, 1, away).wait_send()

            @pl.when((at.z + away < at.zs) & (at.z > 0))
            def _(away=away):
                self.hop(piece, at.z + away, -1, hops + away).wait_send()
        for source in range(at.zs):
            for step in range(1, at.xs):
                self.x_copy(piece, source, step).wait_send()


def layer_norm(values):
    mean = jnp.mean(values, axis=-1, keepdims=True)
    centered = values - mean
    inv_std = lax.rsqrt(jnp.mean(centered * centered, axis=-1, keepdims=True) + NORM_EPSILON)
    return centered * inv_std, inv_std


def forward_kernel(
    sizes,
    x_ref, seg_col, seg_row, seg_cond, cond_ref, ada_ref, head_bias, inner_bias, shared_bias,
    proj_place, wq_raw, wp_raw, wi_raw, wo_raw,
    wq_out, wp_out, wi_out, wo_out, hid_a_out, heads_out, lse_out, att_out, hid_b_out, act_out,
    slope_out, far_out, own_out, branch_out, middle_out, modk_out,
    wq_full, wp_full, wp_tight, wi_full, wo_full, hid_a, heads, lse, lse_heads, att_heads, att, part, core_in,
    y_out, y_in, hid_b, act, slope, ff_part, ff_in, ff_far, ff_own, branch, middle, modk, mods, ada_tile,
    wp_wide,
    z_send, z_recv, x_send, x_recv, mod_send, mod_recv, sum_send, sum_recv, gat_send, gat_recv, ff_send, ff_recv,
    ada_sem, save_sem,
):
    at = Place(sizes[DP], sizes[TP])
    tokens, width, columns, share = sizes["tokens"], sizes["width"], sizes["columns"], sizes["share"]
    nheads, segs = columns // HD, seg_cond.shape[1]
    window = min(tokens, share + 2 * SEG_MOST)
    greet(
        [at.z_peer(s) for s in range(1, at.zs)]
        + [at.x_peer(s) for s in range(1, at.xs)]
        + [at.tensor_peer(s) for s in range(1, at.tensor_count)]
    )
    pieces, lists = [], []
    for full, shard in (
        (wq_full, wq_raw.shape[1]), (wp_full, wp_wide.shape[0]), (wi_full, wi_raw.shape[0]), (wo_full, wo_raw.shape[0])
    ):
        unit = unit_rows(shard)
        lists.append(list(range(len(pieces), len(pieces) + shard // unit)))
        pieces += [(full, shard, first, unit) for first in range(0, shard, unit)]
    list_q, list_p, list_i, list_o = lists
    gather = Gather(at, pieces, (z_send, z_recv), (x_send, x_recv))
    last = len(pieces)

    def own_rows_of(full, shard):
        return rows_at(at.dp * shard, shard)

    wq_full[own_rows_of(wq_full, wq_raw.shape[1]), :] = jnp.concatenate(
        [wq_raw[part_index] for part_index in range(3)], axis=1
    ).astype(HALF)
    for piece in list_q[:3]:
        gather.start(piece)
    wp_wide[...] = jnp.zeros_like(wp_wide)
    wp_wide[0:wp_raw.shape[0], :] = wp_raw[...]
    for raw, full in ((wp_wide, wp_full), (wi_raw, wi_full), (wo_raw, wo_full)):
        full[own_rows_of(full, raw.shape[0]), :] = raw[...].astype(HALF)
    for piece in range(len(list_q[:3]), 3):
        gather.start(piece)

    def ada_copy(group):
        return pltpu.make_async_copy(ada_ref.at[group], ada_tile.at[group % 2], ada_sem.at[group % 2])

    ada_copy(0).start()
    cond_high, cond_low = split_two(silu(pick_rows(cond_picks(seg_cond, cond_ref.shape[0]), cond_ref[...])))
    cond_both = jnp.concatenate([cond_high, cond_low], axis=0)
    for group in range(6):
        if group == 3:
            gather.tick()
        if group < 5:
            ada_copy(group + 1).start()
        ada_copy(group).wait()
        weight_high, weight_low = split_two(ada_tile[group % 2])
        both = mm_nt(cond_both, weight_high)
        mods[at.tensor, group] = (
            both[:segs] + both[segs:] + mm_nt(cond_high, weight_low)
            + head_bias[3 + group:4 + group, :]
        )

    def mod_copy(step):
        own = mods.at[at.tensor]
        return remote(own, own, mod_send.at[step - 1], mod_recv.at[step - 1], at.tensor_peer(step))

    def mod_landing(step):
        landed = mods.at[lax.rem(at.tensor + at.tensor_count - step, at.tensor_count)]
        return remote(landed, landed, mod_send.at[step - 1], mod_recv.at[step - 1], at.tensor_peer(step))

    for step in range(1, at.tensor_count):
        mod_copy(step).start()
    gather.tick()
    for step in range(1, at.tensor_count):
        mod_landing(step).wait_recv()
    for group in range(6):
        whole = jnp.concatenate([mods[t, group] for t in range(at.tensor_count)], axis=1)
        high, low = split_two(whole)
        modk[group] = jnp.concatenate([high, low], axis=0)

    def pick(rows):
        ids = seg_col[rows, :]
        lanes = lax.broadcasted_iota(jnp.int32, (1, 2 * segs), 1)
        return (ids == lax.rem(lanes, segs)).astype(FLOAT).astype(HALF)

    gather.tick()

    def hidden_block(index, carry):
        rows = rows_at(index * share, share)
        normed, _ = layer_norm(x_ref[rows, :].astype(FLOAT))
        chosen = pick(rows)
        hid_a[rows, :] = (normed * (1.0 + mm(chosen, modk[1])) + mm(chosen, modk[0])).astype(HALF)
        return carry

    lax.fori_loop(0, tokens // share, hidden_block, 0)
    gather.tick_until(list_q[-1])
    for piece in list_q:
        gather.arrive(piece)

    qkv_bias = jnp.concatenate([head_bias[i:i + 1, :] for i in range(3)], axis=1)

    def qkv_block(index, carry):
        rows = rows_at(index * share, share)
        values = mm(hid_a[rows, :], wq_full[...]) + qkv_bias
        for head in range(3 * nheads):
            heads[head, rows, :] = values[:, head * HD:(head + 1) * HD].astype(HALF)
        return carry

    lax.fori_loop(0, tokens // share, qkv_block, 0)

    def attend(block):
        start = block * share
        rows = rows_at(start, share)
        first = pl.multiple_of(jnp.clip(start - SEG_MOST, 0, tokens - window), 128)
        keys = pl.ds(first, window)

        def one_head(head, carry):
            same = seg_col[rows, :] == seg_row[:, keys]
            scores = mm_nt(heads[head, rows, :], heads[nheads + head, keys, :]) * (1.0 / math.sqrt(HD))
            scores = jnp.where(same, scores, -1e30)
            top = jnp.max(scores, axis=-1, keepdims=True)
            expo = jnp.exp(scores - top)
            total = jnp.sum(expo, axis=-1, keepdims=True)
            probs = (expo * (1.0 / total)).astype(HALF)
            att_heads[head, :, :] = mm(probs, heads[2 * nheads + head, keys, :])
            lse_heads[head] = top + jnp.log(total)
            return carry

        lax.fori_loop(0, nheads, one_head, 0)
        joined = jnp.concatenate([att_heads[head] for head in range(nheads)], axis=1).astype(HALF)
        att[rows, :] = joined
        lse[rows, :] = jnp.concatenate([lse_heads[head] for head in range(nheads)], axis=1)
        return joined

    def core_copy(slot, src):
        return remote(src, core_in.at[slot], sum_send.at[slot], sum_recv.at[slot], at.core_peer())

    y_copy = remote(y_out, y_in, sum_send.at[2], sum_recv.at[2], at.y_peer())

    gather.tick_until(list_p[0])
    joined = attend(at.share_of(True, True))
    gather.arrive(list_p[0])
    wp_tight[...] = mm(proj_place[...], wp_full[...]).astype(HALF)
    part[0] = mm(joined, wp_tight[...]).astype(HALF)
    core_copy(0, part.at[0]).start()
    gather.tick_until(list_i[0])
    joined = attend(at.share_of(False, True))
    part[1] = mm(joined, wp_tight[...]).astype(HALF)
    core_copy(1, part.at[1]).start()
    joined = attend(at.share_of(True, False))
    summed = mm(joined, wp_tight[...])
    core_copy(0, part.at[0]).wait_recv()
    y_out[...] = (summed + core_in[0].astype(FLOAT)).astype(HALF)
    y_copy.start()
    joined = attend(at.share_of(False, False))
    summed = mm(joined, wp_tight[...])
    core_copy(1, part.at[1]).wait_recv()
    summed = summed + core_in[1].astype(FLOAT)
    gather.tick_until(list_i[0] + 1)
    y_copy.wait_recv()
    branch[...] = summed + y_in[...].astype(FLOAT) + shared_bias[0:1, :]

    own_rows = rows_at(at.tensor * share, share)
    chosen = pick(own_rows)
    middle[...] = x_ref[own_rows, :].astype(FLOAT) + mm(chosen, modk[2]) * branch[...]
    normed, _ = layer_norm(middle[...])
    hid_b[own_rows, :] = (normed * (1.0 + mm(chosen, modk[4])) + mm(chosen, modk[3])).astype(HALF)

    def hid_rows(other_y, other_core):
        return hid_b.at[rows_at(at.share_of(other_y, other_core) * share, share)]

    own_hid = hid_rows(False, False)
    to_core = remote(own_hid, own_hid, gat_send.at[0], gat_recv.at[0], at.core_peer())
    to_y = remote(own_hid, own_hid, gat_send.at[1], gat_recv.at[1], at.y_peer())
    to_y.start()
    to_core.start()
    across = hid_rows(True, False)
    onward = remote(across, across, gat_send.at[2], gat_recv.at[2], at.core_peer())
    gather.tick_until(list_i[-1])
    remote(across, across, gat_send.at[1], gat_recv.at[1], at.y_peer()).wait_recv()
    onward.start()
    for piece in list_i:
        gather.arrive(piece)
    beside = hid_rows(False, True)
    remote(beside, beside, gat_send.at[0], gat_recv.at[0], at.core_peer()).wait_recv()
    far = hid_rows(True, True)
    remote(far, far, gat_send.at[2], gat_recv.at[2], at.core_peer()).wait_recv()
    gather.tick_until(list_o[0])

    def inner_block(index, carry):
        rows = rows_at(index * share, share)
        pre = mm(hid_b[rows, :], wi_full[...]) + inner_bias[...].reshape(1, -1)
        factor = math.sqrt(2.0 / math.pi)
        squared = pre * pre
        bend = jnp.tanh(factor * (pre + 0.044715 * squared * pre))
        act[rows, :] = (0.5 * pre * (1.0 + bend)).astype(HALF)
        slope[rows, :] = (
            0.5 * (1.0 + bend)
            + 0.5 * pre * (1.0 - bend * bend) * (factor * (1.0 + (3 * 0.044715) * squared))
        ).astype(HALF)
        return carry

    lax.fori_loop(0, tokens // share // 2, inner_block, 0)
    gather.tick_until(list_o[0] + 1)
    lax.fori_loop(tokens // share // 2, tokens // share, inner_block, 0)

    saves = []

    def save(src, dst):
        copy = pltpu.make_async_copy(src, dst, save_sem.at[len(saves)])
        copy.start()
        saves.append(copy)

    for src, dst in (
        (wq_full, wq_out), (wp_tight, wp_out), (wi_full, wi_out), (hid_a, hid_a_out), (heads, heads_out),
        (lse, lse_out), (att, att_out), (hid_b, hid_b_out), (act, act_out), (slope, slope_out),
        (branch, branch_out), (middle, middle_out), (modk, modk_out),
    ):
        save(src, dst)
    gather.tick_until(list_o[-1])
    for piece in list_o:
        gather.arrive(piece)
    save(wo_full, wo_out)

    def outer_block(other_y, other_core):
        rows = rows_at(at.share_of(other_y, other_core) * share, share)
        return mm(act[rows, :], wo_full[...])

    def ff_copy(slot):
        return remote(ff_part.at[slot], ff_in.at[slot], ff_send.at[slot], ff_recv.at[slot], at.core_peer())

    ff_part[0] = outer_block(True, True).astype(HALF)
    ff_copy(0).start()
    ff_part[1] = outer_block(False, True).astype(HALF)
    ff_copy(1).start()
    summed = outer_block(True, False)
    ff_copy(0).wait_recv()
    ff_far[...] = (summed + ff_in[0].astype(FLOAT)).astype(HALF)
    save(ff_far, far_out)
    summed = outer_block(False, False)
    ff_copy(1).wait_recv()
    ff_own[...] = summed + ff_in[1].astype(FLOAT)
    save(ff_own, own_out)
    ff_copy(0).wait_send()
    ff_copy(1).wait_send()

    for step in range(1, at.tensor_count):
        mod_copy(step).wait_send()
    core_copy(0, part.at[0]).wait_send()
    core_copy(1, part.at[1]).wait_send()
    y_copy.wait_send()
    to_core.wait_send()
    to_y.wait_send()
    onward.wait_send()
    for piece in range(last):
        gather.finish(piece)
    for copy in saves:
        copy.wait()


def any_spec():
    return pl.BlockSpec(memory_space=pl.ANY)


def vmem_spec():
    return pl.BlockSpec(memory_space=pltpu.VMEM)


def sizes_of(block_input, conditions, segment_ids, segment_cond, qkv_weight, inner_weight):
    dp_count, tensor_count = lax.axis_size(DP), lax.axis_size(TP)
    tokens, width = block_input.shape
    return {
        DP: dp_count,
        TP: tensor_count,
        "tokens": tokens,
        "rows": segment_ids.shape[0],
        "width": width,
        "columns": qkv_weight.shape[2],
        "hidden": inner_weight.shape[1],
        "shard": qkv_weight.shape[0],
        "share": tokens // tensor_count,
        "segs": segment_cond.shape[1],
        "conds": conditions.shape[0],
    }


def kernels_fit(sizes):
    return (
        sizes[TP] == 2 * CORES
        and sizes["rows"] == 1
        and sizes["share"] % 128 == 0
        and sizes["width"] % 128 == 0
        and sizes["hidden"] % 128 == 0
        and sizes["shard"] % 16 == 0
        and sizes["columns"] % 32 == 0
        and sizes["conds"] % (8 * sizes[TP]) == 0
    )


def placing(columns, own_rows, pad_rows, dp_count):
    tight = np.arange(columns)
    place = (tight // own_rows * pad_rows + tight % own_rows)[:, None] == np.arange(dp_count * pad_rows)
    return place.astype(np.float32)


def run_forward(sizes, block_input, seg_col, segment_ids, segment_cond, conditions, ada_weight, head_biases,
                inner_bias, shared_biases, wq, wp, wi, wo):
    tokens, width, columns, share = (sizes[k] for k in ("tokens", "width", "columns", "share"))
    hidden, dp_count, tensor_count = sizes["hidden"], sizes[DP], sizes[TP]
    nheads, segs = columns // HD, sizes["segs"]
    own_rows = columns // dp_count
    pad_rows = own_rows + -own_rows % 16
    shards = (sizes["shard"], pad_rows, sizes["shard"], hidden // dp_count)
    xs = line_length(dp_count)
    zs = dp_count // xs
    units = sum(shard // unit_rows(shard) for shard in shards)
    place = jnp.asarray(placing(columns, own_rows, pad_rows, dp_count), HALF)
    shapes = [
        ((width, 3 * columns), HALF), ((columns, width), HALF), ((width, hidden), HALF),
        ((hidden, width), HALF), ((tokens, width), HALF), ((3 * nheads, tokens, HD), HALF),
        ((tokens, nheads), FLOAT), ((tokens, columns), HALF), ((tokens, width), HALF),
        ((tokens, hidden), HALF), ((tokens, hidden), HALF), ((share, width), HALF), ((share, width), FLOAT),
        ((share, width), FLOAT), ((share, width), FLOAT), ((6, 2 * segs, width), HALF),
    ]
    vmem = pltpu.VMEM
    dma = pltpu.SemaphoreType.DMA
    scratch = [
        vmem((width, 3 * columns), HALF), vmem((dp_count * pad_rows, width), HALF),
        vmem((columns, width), HALF), vmem((width, hidden), HALF), vmem((hidden, width), HALF),
        vmem((tokens, width), HALF), vmem((3 * nheads, tokens, HD), HALF),
        vmem((tokens, nheads), FLOAT), vmem((nheads, share, 1), FLOAT), vmem((nheads, share, HD), FLOAT),
        vmem((tokens, columns), HALF), vmem((2, share, width), HALF), vmem((2, share, width), HALF),
        vmem((share, width), HALF), vmem((share, width), HALF), vmem((tokens, width), HALF),
        vmem((tokens, hidden), HALF), vmem((tokens, hidden), HALF), vmem((2, share, width), HALF),
        vmem((2, share, width), HALF), vmem((share, width), HALF), vmem((share, width), FLOAT),
        vmem((share, width), FLOAT), vmem((share, width), FLOAT), vmem((6, 2 * segs, width), HALF),
        vmem((tensor_count, 6, segs, columns), FLOAT), vmem((2, columns, width), FLOAT),
        vmem((pad_rows, width), FLOAT),
        dma((units, 2 * (zs - 1))), dma((units, 2 * (zs - 1))), dma((units, zs, xs - 1)),
        dma((units, zs, xs - 1)),
        dma((tensor_count - 1,)), dma((tensor_count - 1,)), dma((3,)), dma((3,)), dma((3,)), dma((3,)), dma((2,)), dma((2,)),
        dma((2,)), dma((16,)),
    ]
    return pl.pallas_call(
        functools.partial(forward_kernel, sizes),
        out_shape=[jax.ShapeDtypeStruct(s, t) for s, t in shapes],
        in_specs=[vmem_spec()] * 5 + [any_spec()] + [vmem_spec()] * 8,
        out_specs=[any_spec()] * len(shapes),
        scratch_shapes=scratch,
        name="forward",
        compiler_params=pltpu.CompilerParams(
            collective_id=1, has_side_effects=True, vmem_limit_bytes=VMEM_BYTES
        ),
    )(
        block_input, seg_col, segment_ids, segment_cond, conditions, ada_weight, head_biases, inner_bias,
        shared_biases, place, wq, wp, wi, wo,
    )


class Scatter:
    def __init__(self, place, pieces, x_sems, z_sems):
        self.place, self.pieces = place, pieces
        self.x_send, self.x_recv = x_sems
        self.z_send, self.z_recv = z_sems

    def slot(self, piece, z, x):
        whole, x_in, z_in, shard, first, count = self.pieces[piece]
        return whole.at[rows_at((z * self.place.xs + x) * shard + first, count)]

    def x_copy(self, piece, step, z):
        at = self.place
        whole, x_in, z_in, shard, first, count = self.pieces[piece]
        return remote(
            self.slot(piece, z, at.x_of(step)), x_in.at[step - 1, z, pl.ds(first, count)],
            self.x_send.at[piece, step - 1, z], self.x_recv.at[piece, step - 1, z], at.x_peer(step),
        )

    def z_copy(self, piece, step):
        at = self.place
        whole, x_in, z_in, shard, first, count = self.pieces[piece]
        return remote(
            self.slot(piece, at.z_of(step), at.x), z_in.at[step - 1, pl.ds(first, count)],
            self.z_send.at[piece, step - 1], self.z_recv.at[piece, step - 1], at.z_peer(step),
        )

    def start(self, piece):
        at = self.place
        for step in range(1, at.xs):
            for z in range(at.zs):
                self.x_copy(piece, step, z).start()

    def pass_on(self, piece):
        at = self.place
        whole, x_in, z_in, shard, first, count = self.pieces[piece]
        for z in range(at.zs):
            rows = rows_at((z * at.xs + at.x) * shard + first, count)
            total = whole[rows, :].astype(FLOAT)
            for step in range(1, at.xs):
                self.x_copy(piece, step, z).wait_recv()
                total = total + x_in[step - 1, z, first:first + count, :].astype(FLOAT)
            whole[rows, :] = total.astype(HALF)
        for step in sorted(range(1, at.zs), key=lambda s: -min(s, at.zs - s)):
            self.z_copy(piece, step).start()

    def arrive(self, piece):
        for step in range(1, self.place.zs):
            self.z_copy(piece, step).wait_recv()

    def finish(self, piece):
        at = self.place
        for step in range(1, at.xs):
            for z in range(at.zs):
                self.x_copy(piece, step, z).wait_send()
        for step in range(1, at.zs):
            self.z_copy(piece, step).wait_send()


class Spread:
    def __init__(self, place, chunks, z_sems, x_sems):
        self.place, self.chunks = place, chunks
        self.z_send, self.z_recv = z_sems
        self.x_send, self.x_recv = x_sems

    def z_copy(self, part, step, source):
        at = self.place
        chunk = self.chunks[part](self.place.z_of(source) * at.xs + at.x)
        return remote(chunk, chunk, self.z_send.at[part, step - 1], self.z_recv.at[part, step - 1], at.z_peer(step))

    def x_copy(self, part, back, step, source):
        at = self.place
        chunk = self.chunks[part](at.z_of(-back) * at.xs + at.x_of(source))
        sems = self.x_send.at[part, back, step - 1], self.x_recv.at[part, back, step - 1]
        return remote(chunk, chunk, *sems, at.x_peer(step))

    def start(self, part):
        for step in range(1, self.place.zs):
            self.z_copy(part, step, 0).start()

    def pass_on(self, part):
        for back in range(self.place.zs):
            if back > 0:
                self.z_copy(part, back, -back).wait_recv()
            for step in range(1, self.place.xs):
                self.x_copy(part, back, step, 0).start()

    def finish(self, part):
        at = self.place
        for step in range(1, at.zs):
            self.z_copy(part, step, 0).wait_send()
        for back in range(at.zs):
            for step in range(1, at.xs):
                self.x_copy(part, back, step, -step).wait_recv()
                self.x_copy(part, back, step, 0).wait_send()


def image_sums(chosen, values):
    high, low = split_two(values)
    return mm_tn(chosen, high) + mm_tn(chosen, low)


def backward_kernel(
    sizes,
    seg_col, seg_row, seg_cond, shared_bias, place_back,
    x_in, cot_in, wq_in, wp_in, wi_in, wo_in, hid_a_in, heads_in, lse_in, att_in, hid_b_in, act_in, slope_in,
    far_in, own_in, branch_in, middle_in, modk_in,
    block_out, input_out, qkv_out, proj_out, inner_out, outer_out, mods_out, packs_out, picks_out,
    wq, wp, wi, wo, heads, lse, att, hid_b, act, slope, cot, modk, branch, middle, ff_own,
    cot_own, x_own, gatt, key_sum, value_sum, grad_a, part, core_in, y_out, y_in, ff_in, grad_mid,
    whole_o, whole_i, whole_p, whole_q, xin_o, xin_i, xin_p, xin_q, zin_o, zin_i, zin_p, zin_q,
    mod_send_buf, mod_in, mods, packs, picks,
    load_sem, save_sem, x_send, x_recv, z_send, z_recv, sum_send, sum_recv, gat_send, gat_recv,
    ff_send, ff_recv, mod_send, mod_recv, all_z_send, all_z_recv, all_x_send, all_x_recv,
):
    at = Place(sizes[DP], sizes[TP])
    tokens, width, columns, share = sizes["tokens"], sizes["width"], sizes["columns"], sizes["share"]
    hidden = sizes["hidden"]
    nheads, segs = columns // HD, sizes["segs"]
    blocks = tokens // share
    scale = 1.0 / math.sqrt(HD)

    own_rows = rows_at(at.tensor * share, share)
    loads = {}

    def load(name, src, dst):
        copy = pltpu.make_async_copy(src, dst, load_sem.at[len(loads)])
        copy.start()
        loads[name] = copy

    load("cot", cot_in, cot)
    load("modk", modk_in, modk)
    load("act", act_in, act)
    load("wo", wo_in, wo)
    load("slope", slope_in, slope)
    load("wi", wi_in, wi)
    load("hid_b", hid_b_in, hid_b)
    load("middle", middle_in, middle)
    load("branch", branch_in, branch)
    load("ff_own", own_in, ff_own)
    load("att", att_in, att)
    load("wp", wp_in, wp)
    load("heads", heads_in, heads)
    load("lse", lse_in, lse)
    load("wq", wq_in, wq)
    load("x", x_in.at[own_rows], x_own)
    greet(
        [at.z_peer(s) for s in range(1, at.zs)]
        + [at.x_peer(s) for s in range(1, at.xs)]
        + [at.tensor_peer(s) for s in range(1, at.tensor_count)]
    )
    ff_copy = remote(far_in, ff_in, ff_send, ff_recv, at.y_peer())
    ff_copy.start()

    pieces = []
    for whole, x_in, z_in in (
        (whole_o, xin_o, zin_o), (whole_i, xin_i, zin_i), (whole_p, xin_p, zin_p), (whole_q, xin_q, zin_q)
    ):
        shard = x_in.shape[2]
        unit = unit_rows(shard)
        pieces.append([(whole, x_in, z_in, shard, first, unit) for first in range(0, shard, unit)])
    flat = [piece for group in pieces for piece in group]
    scatter = Scatter(at, flat, (x_send, x_recv), (z_send, z_recv))
    bounds = [sum(len(g) for g in pieces[:i]) for i in range(len(pieces) + 1)]
    list_o, list_i, list_p, list_q = (list(range(bounds[i], bounds[i + 1])) for i in range(4))

    def one_hot(rows, count):
        lanes = lax.broadcasted_iota(jnp.int32, (1, count), 1)
        return (seg_col[rows, :] == lax.rem(lanes, segs)).astype(FLOAT).astype(HALF)

    loads["cot"].wait()
    loads["modk"].wait()
    cot_own[...] = cot[own_rows, :]
    packs[at.dp] = jnp.zeros_like(packs[at.dp])
    picks[at.dp] = jnp.zeros_like(picks[at.dp])

    def grad_b_block(index, total):
        rows = rows_at(index * share, share)
        gate = mm(one_hot(rows, 2 * segs), modk[5])
        value = (cot[rows, :].astype(FLOAT) * gate).astype(HALF)
        cot[rows, :] = value
        return total + jnp.sum(value.astype(FLOAT), axis=0, keepdims=True)

    packs[at.dp, 3:4, 0:width] = lax.fori_loop(0, blocks, grad_b_block, jnp.zeros((1, width), FLOAT))
    loads["act"].wait()

    def lanes_at(index):
        return pl.ds(pl.multiple_of(index * 128, 128), 128)

    def outer_grad_block(index, carry):
        whole_o[rows_at(index * 128, 128), :] = mm_tn(act[:, lanes_at(index)], cot[...]).astype(HALF)
        return carry

    lax.fori_loop(0, hidden // 128, outer_grad_block, 0)
    for piece in list_o:
        scatter.start(piece)
    load("hid_a", hid_a_in, act)
    loads["wo"].wait()
    loads["slope"].wait()
    loads["wi"].wait()

    def back_two(block):
        rows = rows_at(block * share, share)
        grad_act = mm_nt(cot[rows, :], wo[...])
        grad_pre = (grad_act * slope[rows, :].astype(FLOAT)).astype(HALF)
        slope[rows, :] = grad_pre
        return mm_nt(grad_pre, wi[...]), jnp.sum(grad_pre.astype(FLOAT), axis=0, keepdims=True)

    def core_copy(slot):
        return remote(part.at[slot], core_in.at[slot], sum_send.at[slot], sum_recv.at[slot], at.core_peer())

    y_copy = remote(y_out, y_in, sum_send.at[2], sum_recv.at[2], at.y_peer())

    def sum_shares(make, between, held):
        part[0] = make(at.share_of(True, True)).astype(HALF)
        core_copy(0).start()
        part[1] = make(at.share_of(False, True)).astype(HALF)
        core_copy(1).start()
        summed = make(at.share_of(True, False))
        core_copy(0).wait_recv()
        y_out[...] = (summed + core_in[0].astype(FLOAT)).astype(HALF)
        y_copy.start()
        summed = make(at.share_of(False, False))
        core_copy(1).wait_recv()
        held[...] = summed + core_in[1].astype(FLOAT)
        between()
        y_copy.wait_recv()
        core_copy(0).wait_send()
        core_copy(1).wait_send()
        y_copy.wait_send()
        return held[...] + y_in[...].astype(FLOAT)

    bias_total = [jnp.zeros((1, hidden), FLOAT)]

    def make_two(block):
        value, bias = back_two(block)
        bias_total[0] = bias_total[0] + bias
        return value

    def inner_grads():
        packs[at.dp, 1:2, 0:hidden] = bias_total[0]
        loads["hid_b"].wait()

        def inner_grad_block(index, carry):
            whole_i[rows_at(index * 128, 128), :] = mm_tn(hid_b[:, lanes_at(index)], slope[...]).astype(HALF)
            return carry

        lax.fori_loop(0, width // 128, inner_grad_block, 0)
        for piece in list_i:
            scatter.start(piece)
        for piece in list_o[:2]:
            scatter.pass_on(piece)

    grad_hid_b = sum_shares(make_two, inner_grads, grad_mid)

    loads["middle"].wait()
    loads["branch"].wait()
    loads["ff_own"].wait()
    chosen = one_hot(own_rows, 2 * segs)
    normed, inv_std = layer_norm(middle[...])
    grad_normed = grad_hid_b * (1.0 + mm(chosen, modk[4]))
    first_mean = jnp.mean(grad_normed, axis=-1, keepdims=True)
    second_mean = jnp.mean(grad_normed * normed, axis=-1, keepdims=True)
    grad_mid[...] = cot_own[...].astype(FLOAT) + inv_std * (grad_normed - first_mean - normed * second_mean)
    grad_a[own_rows, :] = (grad_mid[...] * mm(chosen, modk[2])).astype(HALF)

    def hid_rows(other_y, other_core):
        return grad_a.at[rows_at(at.share_of(other_y, other_core) * share, share)]

    own_hid = hid_rows(False, False)
    to_core = remote(own_hid, own_hid, gat_send.at[0], gat_recv.at[0], at.core_peer())
    to_y = remote(own_hid, own_hid, gat_send.at[1], gat_recv.at[1], at.y_peer())
    to_y.start()
    to_core.start()
    across, beside, far = hid_rows(True, False), hid_rows(False, True), hid_rows(True, True)
    onward = remote(across, across, gat_send.at[2], gat_recv.at[2], at.core_peer())

    images = one_hot(own_rows, segs)

    def keep_mod(group, values):
        sums = image_sums(images, values)
        for t in range(at.tensor_count):
            mod_send_buf[t, group] = sums[:, t * columns:(t + 1) * columns]

    keep_mod(2, grad_mid[...] * branch[...])
    keep_mod(3, grad_hid_b)
    keep_mod(4, grad_hid_b * normed)
    mod_parts = ((2, 4), (0, 2))
    spread = Spread(
        at,
        [
            lambda source: mods.at[source, pl.ds(2, 4)],
            lambda source: mods.at[source, pl.ds(0, 2)],
            lambda source: packs.at[source],
            lambda source: picks.at[source],
        ],
        (all_z_send, all_z_recv), (all_x_send, all_x_recv),
    )

    def mod_copy(part_index, step):
        first, count = mod_parts[part_index]
        to = lax.rem(at.tensor + step, at.tensor_count)
        return remote(
            mod_send_buf.at[to, pl.ds(first, count)], mod_in.at[step - 1, pl.ds(first, count)],
            mod_send.at[part_index, step - 1], mod_recv.at[part_index, step - 1], at.tensor_peer(step),
        )

    def mod_start(part_index):
        for step in range(1, at.tensor_count):
            mod_copy(part_index, step).start()

    def mod_spread(part_index):
        first, count = mod_parts[part_index]
        total = mod_send_buf[at.tensor, first:first + count]
        for step in range(1, at.tensor_count):
            mod_copy(part_index, step).wait_recv()
            total = total + mod_in[step - 1, first:first + count]
        mods[at.dp, first:first + count] = total
        spread.start(part_index)

    window = min(tokens, share + 2 * SEG_MOST)
    key_sum[...] = jnp.zeros_like(key_sum)
    value_sum[...] = jnp.zeros_like(value_sum)

    def grad_att(block):
        rows = rows_at(block * share, share)
        values = mm_nt(grad_a[rows, :], wp[...])
        for head in range(nheads):
            gatt[head] = values[:, head * HD:(head + 1) * HD].astype(HALF)
        return jnp.sum(grad_a[rows, :].astype(FLOAT), axis=0, keepdims=True)

    def attend_back(block):
        start = block * share
        rows = rows_at(start, share)
        keys_at = pl.ds(pl.multiple_of(jnp.clip(start - SEG_MOST, 0, tokens - window), 128), window)

        def one_head(head, carry):
            query = heads[head, rows, :]
            keys = heads[nheads + head, keys_at, :]
            values = heads[2 * nheads + head, keys_at, :]
            grad = gatt[head]
            same = seg_col[rows, :] == seg_row[:, keys_at]
            scores = jnp.where(same, mm_nt(query, keys) * scale, -1e30)
            lanes = lax.broadcasted_iota(jnp.int32, (1, nheads), 1)
            peak = jnp.sum(jnp.where(lanes == head, lse[rows, :], 0.0), axis=-1, keepdims=True)
            probs = jnp.exp(scores - peak)
            grad_probs = mm_nt(grad, values)
            center = jnp.sum(probs * grad_probs, axis=-1, keepdims=True)
            grad_scores = (probs * (grad_probs - center)).astype(HALF)
            heads[head, rows, :] = (mm(grad_scores, keys) * scale).astype(HALF)
            key_sum[head, keys_at, :] += mm_tn(grad_scores, query)
            value_sum[head, keys_at, :] += mm_tn(probs.astype(HALF), grad)
            return carry

        lax.fori_loop(0, nheads, one_head, 0)

    loads["wp"].wait()
    loads["heads"].wait()
    loads["lse"].wait()
    grad_a_sum = grad_att(at.share_of(False, False))
    attend_back(at.share_of(False, False))
    for piece in list_o[2:]:
        scatter.pass_on(piece)
    remote(beside, beside, gat_send.at[0], gat_recv.at[0], at.core_peer()).wait_recv()
    grad_a_sum = grad_a_sum + grad_att(at.share_of(False, True))
    remote(across, across, gat_send.at[1], gat_recv.at[1], at.y_peer()).wait_recv()
    onward.start()
    attend_back(at.share_of(False, True))
    grad_a_sum = grad_a_sum + grad_att(at.share_of(True, False))
    attend_back(at.share_of(True, False))
    scatter.pass_on(list_i[0])
    remote(far, far, gat_send.at[2], gat_recv.at[2], at.core_peer()).wait_recv()
    grad_a_sum = grad_a_sum + grad_att(at.share_of(True, True))
    attend_back(at.share_of(True, True))
    packs[at.dp, 2:3, 0:width] = grad_a_sum
    loads["att"].wait()
    proj_grad = mm_tn(att[...], grad_a[...]).astype(HALF)
    whole_p[...] = mm(place_back[...], proj_grad).astype(HALF)
    for piece in list_p:
        scatter.start(piece)
    to_core.wait_send()
    to_y.wait_send()
    onward.wait_send()

    def join_block(index, total):
        rows = rows_at(index * share, share)
        parts = [heads[head, rows, :].astype(FLOAT) for head in range(nheads)]
        parts += [(key_sum[head, rows, :] * scale).astype(HALF).astype(FLOAT) for head in range(nheads)]
        parts += [value_sum[head, rows, :].astype(HALF).astype(FLOAT) for head in range(nheads)]
        values = jnp.concatenate(parts, axis=1)
        grad_a[rows, 0:3 * columns] = values.astype(HALF)
        return total + jnp.sum(values, axis=0, keepdims=True)

    packs[at.dp, 0:1, 0:3 * columns] = lax.fori_loop(0, blocks, join_block, jnp.zeros((1, 3 * columns), FLOAT))
    for piece in list_i[1:2]:
        scatter.pass_on(piece)
    loads["hid_a"].wait()

    def qkv_grad_block(index, carry):
        whole_q[rows_at(index * 128, 128), :] = mm_tn(act[:, lanes_at(index)], grad_a[:, 0:3 * columns]).astype(HALF)
        return carry

    lax.fori_loop(0, width // 128, qkv_grad_block, 0)
    for piece in list_q:
        scatter.start(piece)
    loads["wq"].wait()

    saves = []

    def save(src, dst):
        copy = pltpu.make_async_copy(src, dst, save_sem.at[len(saves)])
        copy.start()
        saves.append(copy)

    def mod_sums():
        for piece in list_i[2:] + list_p:
            scatter.pass_on(piece)
        ff_copy.wait_recv()
        branch_b = ff_own[...] + ff_in[...].astype(FLOAT) + shared_bias[1:2, :]
        keep_mod(5, cot_own[...].astype(FLOAT) * branch_b)
        ff_in[...] = (middle[...] + mm(chosen, modk[5]) * branch_b).astype(HALF)
        save(ff_in, block_out)
        mod_start(0)
        for part_index in (2, 3):
            spread.start(part_index)
        for piece in list_q[:1]:
            scatter.pass_on(piece)

    unit = lax.broadcasted_iota(jnp.int32, (segs, 1), 0) == lax.broadcasted_iota(jnp.int32, (1, segs), 1)
    conds = sizes["conds"]
    picks[at.dp, 0:segs, 0:conds] = mm_nt(unit.astype(FLOAT).astype(HALF), cond_picks(seg_cond, conds))
    grad_hid_a = sum_shares(
        lambda block: mm_nt(grad_a[rows_at(block * share, share), 0:3 * columns], wq[...]), mod_sums, branch
    )
    loads["x"].wait()
    normed, inv_std = layer_norm(x_own[...].astype(FLOAT))
    grad_normed = grad_hid_a * (1.0 + mm(chosen, modk[1]))
    first_mean = jnp.mean(grad_normed, axis=-1, keepdims=True)
    second_mean = jnp.mean(grad_normed * normed, axis=-1, keepdims=True)
    grad_mid[...] = grad_mid[...] + inv_std * (grad_normed - first_mean - normed * second_mean)
    save(grad_mid, input_out)
    mod_spread(0)
    keep_mod(0, grad_hid_a)
    keep_mod(1, grad_hid_a * normed)
    mod_start(1)
    for piece in list_q[1:]:
        scatter.pass_on(piece)
    for part_index in (2, 3, 0):
        spread.pass_on(part_index)
    mod_spread(1)
    spread.pass_on(1)
    outs = ((list_o, outer_out), (list_i, inner_out), (list_p, proj_out), (list_q, qkv_out))
    for pieces_of, out in outs:
        whole, x_in, z_in, shard = flat[pieces_of[0]][:4]
        for piece in pieces_of:
            scatter.arrive(piece)
        save(whole.at[rows_at((at.z * at.xs + at.x) * shard, shard)], out.at[0])
        for step in range(1, at.zs):
            save(z_in.at[step - 1], out.at[step])
    for part_index in range(4):
        spread.finish(part_index)
    save(mods, mods_out)
    save(packs, packs_out)
    save(picks, picks_out)
    ff_copy.wait_send()
    for piece in range(len(flat)):
        scatter.finish(piece)
    for part_index in range(2):
        for step in range(1, at.tensor_count):
            mod_copy(part_index, step).wait_send()
    for copy in saves:
        copy.wait()


def run_backward(sizes, block_input, seg_col, segment_ids, segment_cond, shared_biases, cotangent, kept):
    (wq, wp, wi, wo, hid_a, heads, lse, att, hid_b, act, slope, far, own, branch, middle, modk) = kept
    tokens, width, columns, share = (sizes[k] for k in ("tokens", "width", "columns", "share"))
    hidden, dp_count, tensor_count, segs = sizes["hidden"], sizes[DP], sizes[TP], sizes["segs"]
    nheads = columns // HD
    own_rows = columns // dp_count
    pad_rows = own_rows + -own_rows % 16
    xs = line_length(dp_count)
    zs = dp_count // xs
    shards = (hidden // dp_count, width // dp_count, pad_rows, width // dp_count)
    wholes = ((hidden, width), (width, hidden), (dp_count * pad_rows, width), (width, 3 * columns))
    units = sum(shard // unit_rows(shard) for shard in shards)
    place = jnp.asarray(placing(columns, own_rows, pad_rows, dp_count).T, HALF)
    pack_width = max(width, hidden, 3 * columns)
    shapes = [((share, width), HALF), ((share, width), FLOAT)]
    shapes += [((zs, shards[i], wholes[i][1]), HALF) for i in (3, 2, 1, 0)]
    shapes += [((dp_count, 6, segs, columns), FLOAT), ((dp_count, 4, pack_width), FLOAT)]
    shapes += [((dp_count, 8, 128), FLOAT)]
    vmem, dma = pltpu.VMEM, pltpu.SemaphoreType.DMA
    scratch = [
        vmem((width, 3 * columns), HALF), vmem((columns, width), HALF), vmem((width, hidden), HALF),
        vmem((hidden, width), HALF), vmem((3 * nheads, tokens, HD), HALF), vmem((tokens, nheads), FLOAT),
        vmem((tokens, columns), HALF), vmem((tokens, width), HALF), vmem((tokens, hidden), HALF),
        vmem((tokens, hidden), HALF), vmem((tokens, width), HALF), vmem((6, 2 * segs, width), HALF),
        vmem((share, width), FLOAT), vmem((share, width), FLOAT), vmem((share, width), FLOAT),
        vmem((share, width), HALF), vmem((share, width), HALF), vmem((nheads, share, HD), HALF),
        vmem((nheads, tokens, HD), FLOAT), vmem((nheads, tokens, HD), FLOAT), vmem((tokens, width), HALF),
        vmem((2, share, width), HALF), vmem((2, share, width), HALF), vmem((share, width), HALF),
        vmem((share, width), HALF), vmem((share, width), HALF), vmem((share, width), FLOAT),
    ]
    scratch += [vmem(shape, HALF) for shape in wholes]
    scratch += [vmem((xs - 1, zs, shards[i], wholes[i][1]), HALF) for i in range(4)]
    scratch += [vmem((zs - 1, shards[i], wholes[i][1]), HALF) for i in range(4)]
    scratch += [
        vmem((tensor_count, 6, segs, columns), FLOAT), vmem((tensor_count - 1, 6, segs, columns), FLOAT),
        vmem((dp_count, 6, segs, columns), FLOAT), vmem((dp_count, 4, pack_width), FLOAT),
        vmem((dp_count, 8, 128), FLOAT),
        dma((17,)), dma((5 + 4 * zs,)), dma((units, xs - 1, zs)), dma((units, xs - 1, zs)),
        dma((units, zs - 1)), dma((units, zs - 1)), dma((3,)), dma((3,)), dma((3,)), dma((3,)),
        dma(()), dma(()), dma((2, tensor_count - 1)), dma((2, tensor_count - 1)),
        dma((4, zs - 1)), dma((4, zs - 1)), dma((4, zs, xs - 1)), dma((4, zs, xs - 1)),
    ]
    return pl.pallas_call(
        functools.partial(backward_kernel, sizes),
        out_shape=[jax.ShapeDtypeStruct(s, t) for s, t in shapes],
        in_specs=[vmem_spec()] * 5 + [any_spec()] * 18,
        out_specs=[any_spec()] * len(shapes),
        scratch_shapes=scratch,
        name="backward",
        compiler_params=pltpu.CompilerParams(
            collective_id=2, has_side_effects=True, vmem_limit_bytes=VMEM_BYTES
        ),
    )(
        seg_col, segment_ids, segment_cond, shared_biases, place, block_input, cotangent, wq, wp, wi, wo, hid_a, heads, lse, att, hid_b, act, slope, far, own,
        branch, middle, modk,
    )


def on_device_general(
    block_input,
    conditions,
    segment_ids,
    segment_cond,
    cotangent,
    qkv_weight,
    proj_weight,
    inner_weight,
    outer_weight,
    ada_weight,
    head_biases,
    inner_bias,
    shared_biases,
    qkv_first,
    proj_first,
    inner_first,
    outer_first,
    ada_first,
    head_biases_first,
    inner_bias_first,
    shared_biases_first,
    qkv_second,
    proj_second,
    inner_second,
    outer_second,
    ada_second,
    head_biases_second,
    inner_bias_second,
    shared_biases_second,
):
    columns = qkv_weight.shape[2]
    heads_local = columns // HD
    rows_local = segment_ids.shape[0]
    row_length = segment_ids.shape[1]
    token_count = rows_local * row_length
    seg_count = segment_cond.shape[1]
    width = block_input.shape[1]
    share_count = token_count // lax.axis_size(TP)
    share_start = lax.axis_index(TP) * share_count

    def share(values):
        return lax.dynamic_slice_in_dim(values, share_start, share_count, 0)

    qkv_full, proj_full, inner_full, outer_full = (
        lax.all_gather(qkv_weight.astype(HALF), DP, axis=0, tiled=True),
        lax.all_gather(proj_weight.astype(HALF), DP, axis=0, tiled=True),
        lax.all_gather(inner_weight.astype(HALF), DP, axis=0, tiled=True),
        lax.all_gather(outer_weight.astype(HALF), DP, axis=0, tiled=True),
    )
    condition_select = (
        segment_cond[:, :, None] == jnp.arange(conditions.shape[0])[None, None, :]
    ).astype(FLOAT)
    condition_row_block = jnp.einsum(
        "btu,ua->bta", condition_select, conditions, precision=PRECISION_MAX
    )
    cond_act = silu(condition_row_block)
    local_mod = (
        jnp.einsum("rsd,kcd->rskc", cond_act, ada_weight, precision=PRECISION_MAX)
        + head_biases[3:][None, None]
    )
    full_mod = lax.all_gather(local_mod, TP, axis=3, tiled=True)
    seg_pick = (segment_ids[:, :, None] == jnp.arange(seg_count)[None, None, :]).astype(FLOAT)
    token_mod = jnp.einsum("rls,rskd->rlkd", seg_pick, full_mod, precision=PRECISION_MAX).reshape(
        token_count, 6, width
    )
    inputs = block_input.astype(FLOAT)
    normed_one, inv_one = normalize(inputs)
    hidden_one = (normed_one * (1.0 + token_mod[:, 1]) + token_mod[:, 0]).astype(HALF)
    qkv_values = (
        jnp.einsum("nd,dkc->nkc", hidden_one, qkv_full, preferred_element_type=FLOAT)
        + head_biases[:3][None]
    ).astype(HALF)
    row_qkv = qkv_values.reshape(rows_local, row_length, 3, heads_local, HD)
    row = 0
    attended_row, total_row = attend_forward(row_qkv[row], segment_ids[row])
    attended_rows = [attended_row]
    total_rows = [total_row]
    attended = jnp.stack(attended_rows).reshape(token_count, columns).astype(HALF)
    attn_partial = jnp.dot(attended, proj_full, preferred_element_type=FLOAT)
    share_mod = share(token_mod)
    branch_one = sum_to_shares(attn_partial) + shared_biases[0]
    middle = share(inputs) + share_mod[:, 2] * branch_one
    normed_two, inv_two = normalize(middle)
    hidden_two_share = (normed_two * (1.0 + share_mod[:, 4]) + share_mod[:, 3]).astype(HALF)
    hidden_two = lax.all_gather(hidden_two_share, TP, axis=0, tiled=True)
    pre_act = jnp.dot(hidden_two, inner_full, preferred_element_type=FLOAT) + inner_bias
    act_values, gelu_back = jax.vjp(gelu_tanh, pre_act)
    act_low = act_values.astype(HALF)
    ff_partial = jnp.dot(act_low, outer_full, preferred_element_type=FLOAT)
    branch_two = sum_to_shares(ff_partial) + shared_biases[1]
    output = middle + share_mod[:, 5] * branch_two
    grad_out = cotangent.astype(FLOAT)
    grad_two = (grad_out * token_mod[:, 5]).astype(HALF)
    outer_grad = jnp.einsum("nf,nd->fd", act_low, grad_two, preferred_element_type=FLOAT)
    grad_act = jnp.einsum("nd,fd->nf", grad_two, outer_full, preferred_element_type=FLOAT)
    grad_pre = gelu_back(grad_act)[0].astype(HALF)
    inner_grad = jnp.einsum("nd,nf->df", hidden_two, grad_pre, preferred_element_type=FLOAT)
    back_two_partial = jnp.einsum("nf,df->nd", grad_pre, inner_full, preferred_element_type=FLOAT)
    grad_hidden_two = sum_to_shares(back_two_partial)
    grad_out_share = share(grad_out)
    grad_middle = grad_out_share + norm_back(
        grad_hidden_two * (1.0 + share_mod[:, 4]), normed_two, inv_two
    )
    grad_one_share = (grad_middle * share_mod[:, 2]).astype(HALF)
    grad_one = lax.all_gather(grad_one_share, TP, axis=0, tiled=True)
    proj_grad = jnp.einsum("nc,nd->cd", attended, grad_one, preferred_element_type=FLOAT)
    grad_attended = jnp.einsum(
        "nd,cd->nc", grad_one, proj_full, preferred_element_type=FLOAT
    ).astype(HALF)
    grad_rows = grad_attended.reshape(rows_local, row_length, heads_local, HD)
    row = 0
    grad_qkv_rows = [
        attend_backward(row_qkv[row], segment_ids[row], grad_rows[row], total_rows[row])
    ]
    grad_qkv = jnp.stack(grad_qkv_rows).reshape(token_count, 3, columns).astype(HALF)
    qkv_grad = jnp.einsum("nd,nkc->dkc", hidden_one, grad_qkv, preferred_element_type=FLOAT)
    back_one_partial = jnp.einsum("nkc,dkc->nd", grad_qkv, qkv_full, preferred_element_type=FLOAT)
    grad_hidden_one = sum_to_shares(back_one_partial)
    normed_one_share, inv_one_share = share(normed_one), share(inv_one)
    input_out = grad_middle + norm_back(
        grad_hidden_one * (1.0 + share_mod[:, 1]), normed_one_share, inv_one_share
    )
    block_out = output.astype(HALF)
    contributions = jnp.concatenate(
        [
            grad_hidden_one,
            grad_hidden_one * normed_one_share,
            grad_middle * branch_one,
            grad_hidden_two,
            grad_hidden_two * normed_two,
            grad_out_share * branch_two,
        ],
        axis=1,
    )
    pick_share = share(seg_pick.reshape(token_count, seg_count))
    cond_pick = jnp.dot(pick_share, condition_select[0], precision=PRECISION_MAX)
    cond_sums = jnp.einsum("lq,lc->qc", cond_pick, contributions, precision=PRECISION_MAX)
    cond_sums = cond_sums.reshape(-1, 6, lax.axis_size(TP), columns)
    cond_sums = lax.psum_scatter(cond_sums, TP, scatter_dimension=2, tiled=True)[:, :, 0]
    cond_total = lax.psum(cond_sums, DP)
    all_act, all_silu_back = jax.vjp(silu, conditions)
    grad_all_act = jnp.einsum("qkc,kcd->qd", cond_total, ada_weight, precision=PRECISION_MAX)
    cond_grad = all_silu_back(lax.psum(grad_all_act, TP))[0]
    head_bias_grad = jnp.sum(grad_qkv.astype(FLOAT), axis=0)
    inner_bias_grad = jnp.sum(grad_pre.astype(FLOAT), axis=0)
    shared_bias_grad = jnp.stack(
        [jnp.sum(grad_one.astype(FLOAT), axis=0), jnp.sum(grad_two.astype(FLOAT), axis=0)]
    )
    ada_total = jnp.einsum("qd,qkc->kcd", all_act, cond_total, precision=PRECISION_MAX)
    head_total, inner_bias_total, shared_total = lax.psum(
        (head_bias_grad, inner_bias_grad, shared_bias_grad), DP
    )
    head_total = jnp.concatenate([head_total, jnp.sum(cond_total, axis=0)], axis=0)
    qkv_shard, proj_shard, inner_shard, outer_shard = (
        sum_to_owners(qkv_grad),
        sum_to_owners(proj_grad),
        sum_to_owners(inner_grad),
        sum_to_owners(outer_grad),
    )
    qkv_new = adam_update(qkv_weight, qkv_shard, qkv_first, qkv_second, RATES[0])
    proj_new = adam_update(proj_weight, proj_shard, proj_first, proj_second, RATES[1])
    inner_new = adam_update(inner_weight, inner_shard, inner_first, inner_second, RATES[2])
    outer_new = adam_update(outer_weight, outer_shard, outer_first, outer_second, RATES[3])
    ada_new = adam_update(ada_weight, ada_total, ada_first, ada_second, RATES[4])
    head_new = adam_update(head_biases, head_total, head_biases_first, head_biases_second, RATES[5])
    inner_bias_new = adam_update(
        inner_bias, inner_bias_total, inner_bias_first, inner_bias_second, RATES[6]
    )
    shared_new = adam_update(
        shared_biases, shared_total, shared_biases_first, shared_biases_second, RATES[7]
    )
    return (
        block_out,
        input_out,
        cond_grad,
        qkv_new[0],
        proj_new[0],
        inner_new[0],
        outer_new[0],
        ada_new[0],
        head_new[0],
        inner_bias_new[0],
        shared_new[0],
        qkv_new[1],
        proj_new[1],
        inner_new[1],
        outer_new[1],
        ada_new[1],
        head_new[1],
        inner_bias_new[1],
        shared_new[1],
        qkv_new[2],
        proj_new[2],
        inner_new[2],
        outer_new[2],
        ada_new[2],
        head_new[2],
        inner_bias_new[2],
        shared_new[2],
        qkv_new[0].astype(HALF),
        proj_new[0].astype(HALF),
        inner_new[0].astype(HALF),
        outer_new[0].astype(HALF),
    )


def update_kernel(
    sizes,
    cond_ref, mods, packs, picks, head_w, head_m, head_v, hidden_w, hidden_m, hidden_v, shared_w, shared_m, shared_v,
    *refs,
):
    width, columns, segs, hidden = sizes["width"], sizes["columns"], sizes["segs"], sizes["hidden"]
    big_in = [refs[i * 4:i * 4 + 4] for i in range(4)]
    ada_in = refs[16:19]
    part, *small_out = refs[19:29]
    ada_out = refs[29:32]
    big_out = [refs[32 + i * 4:36 + i * 4] for i in range(4)]
    refs = refs[48:]
    ada = refs[:3]
    big = [refs[3 + i * 5:8 + i * 5] for i in range(4)]
    gt, act_rows, head_grad = refs[23:26]
    ada_load, ada_save, big_load, big_save = refs[26:]
    conds, dp_count = cond_ref.shape[0], sizes[DP]

    def ada_copy(kind, group):
        return pltpu.make_async_copy(ada_in[kind].at[group], ada[kind].at[group], ada_load.at[kind, group])

    for group in range(6):
        ada_copy(0, group).start()
    for group in range(6):
        ada_copy(1, group).start()
        ada_copy(2, group).start()
    big_loads = []
    for index in range(4):
        copies = [
            pltpu.make_async_copy(big_in[index][kind], big[index][kind], big_load.at[index, kind])
            for kind in range(4)
        ]
        for copy in copies:
            copy.start()
        big_loads.append(copies)

    act = silu(cond_ref[...])
    act_high, act_low = split_two(act)
    act_rows[...] = jnp.concatenate([act_high, act_high, act_low], axis=0)
    picked = jnp.concatenate(
        [picks[row, 0:segs, 0:conds] for row in range(dp_count)], axis=0
    ).astype(HALF)
    for group in range(6):
        images = jnp.concatenate([mods[row, group] for row in range(dp_count)], axis=0)
        head_grad[3 + group:4 + group, :] = jnp.sum(images, axis=0, keepdims=True)
        high, low = split_two(images)
        sums_high, sums_low = split_two(mm_tn(high, picked) + mm_tn(low, picked))
        gt[group] = jnp.concatenate([sums_high, sums_low, sums_high], axis=1)

    part[...] = jnp.zeros_like(part)
    for group in range(6):
        ada_copy(0, group).wait()
        weight_high, weight_low = split_two(ada[0][group])
        both = mm_tn(gt[group, :, 0:2 * conds], weight_high)
        part[...] += both[:conds] + both[conds:] + mm_tn(gt[group, :, 0:conds], weight_low)

    def update(values, rate, grad):
        weight, first, second = values
        return adam_update(weight, grad, first, second, rate)

    tile = 96 if columns % 96 == 0 else columns
    saves = []

    def ada_group(group):
        for kind in (1, 2):
            ada_copy(kind, group).wait()

        def ada_tile(index, carry):
            rows = pl.ds(pl.multiple_of(index * tile, 8), tile)
            grad = mm(gt[group, rows, :], act_rows[...])
            new = update([ref[group, rows, :] for ref in ada], RATES[4], grad)
            for ref, value in zip(ada, new, strict=True):
                ref[group, rows, :] = value
            return carry

        lax.fori_loop(0, columns // tile, ada_tile, 0)
        for kind in range(3):
            copy = pltpu.make_async_copy(ada[kind].at[group], ada_out[kind].at[group], ada_save.at[kind, group])
            copy.start()
            saves.append(copy)

    for group in range(6):
        ada_group(group)

    pack = packs[0]
    for row in range(1, dp_count):
        pack = pack + packs[row]
    for part_index in range(3):
        head_grad[part_index:part_index + 1, :] = pack[0:1, part_index * columns:(part_index + 1) * columns]
    smalls = (
        ((head_w, head_m, head_v), RATES[5], head_grad[...]),
        ((hidden_w, hidden_m, hidden_v), RATES[6], pack[1:2, 0:hidden].reshape(hidden_w.shape)),
        ((shared_w, shared_m, shared_v), RATES[7], pack[2:4, 0:width]),
    )
    for index, (kinds, rate, grad) in enumerate(smalls):
        for kind, value in enumerate(update([ref[...] for ref in kinds], rate, grad)):
            small_out[index * 3 + kind][...] = value

    for index in range(4):
        for copy in big_loads[index]:
            copy.wait()
        weight, first, second, grad, low = big[index]
        planes = weight.shape[0] if len(weight.shape) == 3 else 0
        for plane in range(max(planes, 1)):
            where = (plane,) if planes else (slice(0, weight.shape[0]),)
            lanes = weight.shape[-1]
            gradient = grad[0, :, plane * lanes:(plane + 1) * lanes].astype(FLOAT)
            for source in range(1, grad.shape[0]):
                gradient = gradient + grad[source, :, plane * lanes:(plane + 1) * lanes].astype(FLOAT)
            gradient = gradient[0:weight.shape[-2], :]
            new = update([ref[where] for ref in (weight, first, second)], RATES[index], gradient)
            for ref, value in zip((weight, first, second), new, strict=True):
                ref[where] = value
            low[where] = new[0].astype(HALF)
        for kind, ref in enumerate((weight, first, second, low)):
            copy = pltpu.make_async_copy(ref, big_out[index][kind], big_save.at[index, kind])
            copy.start()
            saves.append(copy)

    for copy in saves:
        copy.wait()


def run_update(sizes, conditions, mods, packs, picks, smalls, bigs, ada):
    width, columns, segs = sizes["width"], sizes["columns"], sizes["segs"]
    conds = conditions.shape[0]
    vmem, dma = pltpu.VMEM, pltpu.SemaphoreType.DMA
    flat_small = [array for kinds in smalls for array in kinds]
    flat_big = [array for kinds in bigs for array in kinds]

    def like(array, dtype=FLOAT):
        return jax.ShapeDtypeStruct(array.shape, dtype)

    outs = [like(conditions)] + [like(a) for a in flat_small] + [like(a) for a in ada]
    for weight, first, second, grad in bigs:
        outs += [like(weight), like(first), like(second), like(weight, HALF)]
    scratch = [vmem(array.shape, FLOAT) for array in ada]
    for kinds in bigs:
        scratch += [vmem(array.shape, array.dtype) for array in kinds] + [vmem(kinds[0].shape, HALF)]
    scratch += [
        vmem((6, columns, 3 * conds), HALF), vmem((3 * conds, width), HALF), vmem((9, columns), FLOAT),
        dma((3, 6)), dma((3, 6)), dma((4, 4)), dma((4, 4)),
    ]
    return pl.pallas_call(
        functools.partial(update_kernel, sizes),
        out_shape=outs,
        in_specs=[vmem_spec()] * 13 + [any_spec()] * 19,
        out_specs=[vmem_spec()] * 10 + [any_spec()] * 19,
        scratch_shapes=scratch,
        name="update",
        compiler_params=pltpu.CompilerParams(vmem_limit_bytes=VMEM_BYTES),
    )(conditions, mods, packs, picks, *flat_small, *flat_big, *ada)


def cond_kernel(sizes, cond_ref, part_in, cond_out, part, landing, result, out_send, out_recv, back_send, back_recv):
    at = Place(sizes[DP], sizes[TP])
    slice_rows = cond_ref.shape[0] // at.tensor_count
    part[...] = part_in[...]
    greet([at.tensor_peer(s) for s in range(1, at.tensor_count)])

    def slice_at(index):
        return pl.ds(pl.multiple_of(index * slice_rows, 8), slice_rows)

    def out_copy(step):
        to = lax.rem(at.tensor + step, at.tensor_count)
        return remote(
            part.at[slice_at(to)], landing.at[step - 1], out_send.at[step - 1], out_recv.at[step - 1],
            at.tensor_peer(step),
        )

    def back_copy(step, owner):
        rows = result.at[slice_at(owner)]
        return remote(rows, rows, back_send.at[step - 1], back_recv.at[step - 1], at.tensor_peer(step))

    for step in range(1, at.tensor_count):
        out_copy(step).start()

    total = part[slice_at(at.tensor), :]
    for step in range(1, at.tensor_count):
        out_copy(step).wait_recv()
        total = total + landing[step - 1]
    own = cond_ref[slice_at(at.tensor), :]
    gate = 1.0 / (1.0 + jnp.exp(-own))
    result[slice_at(at.tensor), :] = total * (gate * (1.0 + own * (1.0 - gate)))
    for step in range(1, at.tensor_count):
        back_copy(step, at.tensor).start()
    for step in range(1, at.tensor_count):
        back_copy(step, lax.rem(at.tensor + at.tensor_count - step, at.tensor_count)).wait_recv()
    cond_out[...] = result[...]
    for step in range(1, at.tensor_count):
        out_copy(step).wait_send()
        back_copy(step, at.tensor).wait_send()


def run_cond(sizes, conditions, part):
    tensor_count, vmem, dma = sizes[TP], pltpu.VMEM, pltpu.SemaphoreType.DMA
    shape = conditions.shape
    return pl.pallas_call(
        functools.partial(cond_kernel, sizes),
        out_shape=jax.ShapeDtypeStruct(shape, FLOAT),
        in_specs=[vmem_spec()] * 2,
        out_specs=vmem_spec(),
        scratch_shapes=[
            vmem(shape, FLOAT), vmem((tensor_count - 1, shape[0] // tensor_count, shape[1]), FLOAT),
            vmem(shape, FLOAT), *[dma((tensor_count - 1,))] * 4,
        ],
        name="cond",
        compiler_params=pltpu.CompilerParams(collective_id=3, has_side_effects=True),
    )(conditions, part)


def on_device_kernels(
    block_input, conditions, segment_ids, segment_cond, cotangent, qkv_weight, proj_weight, inner_weight,
    outer_weight, ada_weight, head_biases, inner_bias, shared_biases, *moments,
):
    firsts, seconds = moments[:8], moments[8:]
    sizes = sizes_of(block_input, conditions, segment_ids, segment_cond, qkv_weight, inner_weight)
    seg_col = segment_ids.reshape(-1, 1)

    def planes(array):
        return array.transpose(1, 0, 2)

    kept = run_forward(
        sizes, block_input, seg_col, segment_ids, segment_cond, conditions, ada_weight, head_biases, inner_bias,
        shared_biases, planes(qkv_weight), proj_weight, inner_weight, outer_weight,
    )
    block_out, input_out, *grads, mods, packs, picks = run_backward(
        sizes, block_input, seg_col, segment_ids, segment_cond, shared_biases, cotangent, kept
    )
    weights = (qkv_weight, proj_weight, inner_weight, outer_weight)
    bigs = [[w, m, v, g] for w, m, v, g in zip(weights, firsts[:4], seconds[:4], grads, strict=True)]
    bigs[0][:3] = [planes(array) for array in bigs[0][:3]]
    smalls = list(zip((head_biases, inner_bias, shared_biases), firsts[5:], seconds[5:], strict=True))
    cond_part, *news = run_update(
        sizes, conditions, mods, packs, picks, smalls, bigs, (ada_weight, firsts[4], seconds[4])
    )
    small_new, ada_new, big_new = news[:9], news[9:12], news[12:]
    big_new[:4] = [planes(array) for array in big_new[:4]]
    outs = [block_out, input_out, run_cond(sizes, conditions, cond_part)]
    for kind in range(3):
        outs += [big_new[4 * i + kind] for i in range(4)]
        outs += [ada_new[kind]] + [small_new[3 * i + kind] for i in range(3)]
    return (*outs, *big_new[3::4])


def on_device(*args):
    sizes = sizes_of(args[0], args[1], args[2], args[3], args[5], args[7])
    return (on_device_kernels if kernels_fit(sizes) else on_device_general)(*args)


def solution(mesh):
    in_specs = (
        P(DP, None),
        P(),
        P(DP, None),
        P(DP, None),
        P(DP, None),
        P(DP, None, TP),
        P((TP, DP), None),
        P(DP, TP),
        P((TP, DP), None),
        P(None, TP, None),
        P(None, TP),
        P(TP),
        P(),
        P(DP, None, TP),
        P((TP, DP), None),
        P(DP, TP),
        P((TP, DP), None),
        P(None, TP, None),
        P(None, TP),
        P(TP),
        P(),
        P(DP, None, TP),
        P((TP, DP), None),
        P(DP, TP),
        P((TP, DP), None),
        P(None, TP, None),
        P(None, TP),
        P(TP),
        P(),
    )
    out_specs = (
        P((DP, TP), None),
        P((DP, TP), None),
        P(),
        P(DP, None, TP),
        P((TP, DP), None),
        P(DP, TP),
        P((TP, DP), None),
        P(None, TP, None),
        P(None, TP),
        P(TP),
        P(),
        P(DP, None, TP),
        P((TP, DP), None),
        P(DP, TP),
        P((TP, DP), None),
        P(None, TP, None),
        P(None, TP),
        P(TP),
        P(),
        P(DP, None, TP),
        P((TP, DP), None),
        P(DP, TP),
        P((TP, DP), None),
        P(None, TP, None),
        P(None, TP),
        P(TP),
        P(),
        P(DP, None, TP),
        P((TP, DP), None),
        P(DP, TP),
        P((TP, DP), None),
    )
    return jax.shard_map(
        on_device, mesh=mesh, in_specs=in_specs, out_specs=out_specs, check_vma=False
    )
```

```python
import functools
import math

import jax
import jax.numpy as jnp
import numpy as np
from jax import lax
from jax.experimental import pallas as pl
from jax.experimental.pallas import tpu as pltpu
from jax.sharding import PartitionSpec as P

HD = 72
STEP = 10


BETA_ONE = 0.5
BETA_TWO = 0.6
ADAM_EPS = 1e-08
DECAY = 0.01
NORM_EPSILON = 1e-06
RATES = (0.04, 0.3, 0.04, 0.04, 0.04, 0.4, 0.4, 0.4)
PRECISION_MAX = lax.Precision.HIGHEST
FLOAT = jnp.float32
HALF = jnp.bfloat16
DP, TP = "dp", "tensor"


def silu(values):
    return values / (1.0 + jnp.exp(-values))


def gelu_tanh(values):
    inner = math.sqrt(2.0 / math.pi) * (values + 0.044715 * values * values * values)
    return 0.5 * values * (1.0 + jnp.tanh(inner))


def normalize(values):
    centered = values - jnp.mean(values, axis=-1, keepdims=True)
    inv_std = lax.rsqrt(jnp.mean(centered * centered, axis=-1, keepdims=True) + NORM_EPSILON)
    return (centered * inv_std, inv_std)


def norm_back(grad_normed, normed, inv_std):
    first_mean = jnp.mean(grad_normed, axis=-1, keepdims=True)
    second_mean = jnp.mean(grad_normed * normed, axis=-1, keepdims=True)
    return inv_std * (grad_normed - first_mean - normed * second_mean)


def block_scores(query_block, keys, query_segs, key_segs):
    scores = jnp.einsum("qhe,khe->hqk", query_block, keys, preferred_element_type=FLOAT) * (
        1.0 / math.sqrt(HD)
    )
    same = query_segs[:, None] == key_segs[None, :]
    return jnp.where(same[None], scores, -1e30)


def attend_forward(row_qkv, row_segs):
    queries = row_qkv[:, 0]
    keys = row_qkv[:, 1]
    values = row_qkv[:, 2]
    length = queries.shape[0]
    heads_local = queries.shape[1]
    block = min(512, length)
    blocks = length // block

    def one_block(pieces):
        query_block, query_segs = pieces
        scores = block_scores(query_block, keys, query_segs, row_segs)
        top = jnp.max(scores, axis=-1, keepdims=True)
        expo = jnp.exp(scores - top)
        total = jnp.sum(expo, axis=-1, keepdims=True)
        probs = (expo / total).astype(HALF)
        attended = jnp.einsum("hqk,khe->qhe", probs, values, preferred_element_type=FLOAT)
        return (attended, (top + jnp.log(total))[:, :, 0])

    attended, log_totals = lax.map(
        one_block,
        (queries.reshape(blocks, block, heads_local, HD), row_segs.reshape(blocks, block)),
    )
    return (attended.reshape(length, heads_local, HD), log_totals)


def attend_backward(row_qkv, row_segs, grad_row, log_totals):
    queries = row_qkv[:, 0]
    keys = row_qkv[:, 1]
    values = row_qkv[:, 2]
    length = queries.shape[0]
    heads_local = queries.shape[1]
    block = min(512, length)
    blocks = length // block
    scale = 1.0 / math.sqrt(HD)

    def one_block(carry, pieces):
        key_sum, value_sum = carry
        query_block, query_segs, grad_block, block_total = pieces
        scores = block_scores(query_block, keys, query_segs, row_segs)
        probs = jnp.exp(scores - block_total[:, :, None])
        grad_probs = jnp.einsum("qhe,khe->hqk", grad_block, values, preferred_element_type=FLOAT)
        center = jnp.sum(probs * grad_probs, axis=-1, keepdims=True)
        grad_scores = (probs * (grad_probs - center)).astype(HALF)
        grad_query = (
            jnp.einsum("hqk,khe->qhe", grad_scores, keys, preferred_element_type=FLOAT) * scale
        )
        key_sum = (
            key_sum
            + jnp.einsum("hqk,qhe->khe", grad_scores, query_block, preferred_element_type=FLOAT)
            * scale
        )
        value_sum = value_sum + jnp.einsum(
            "hqk,qhe->khe", probs.astype(HALF), grad_block, preferred_element_type=FLOAT
        )
        return ((key_sum, value_sum), grad_query)

    zeros = jnp.zeros((length, heads_local, HD), FLOAT)
    sums, grad_queries = lax.scan(
        one_block,
        (zeros, zeros),
        (
            queries.reshape(blocks, block, heads_local, HD),
            row_segs.reshape(blocks, block),
            grad_row.reshape(blocks, block, heads_local, HD),
            log_totals,
        ),
    )
    return jnp.stack([grad_queries.reshape(length, heads_local, HD), sums[0], sums[1]], axis=1)


def adam_update(weight, grad, first, second, rate):
    first_new = BETA_ONE * first + (1.0 - BETA_ONE) * grad
    second_new = BETA_TWO * second + (1.0 - BETA_TWO) * grad * grad
    fix_one = 1.0 - BETA_ONE**STEP
    fix_two = 1.0 - BETA_TWO**STEP
    update = first_new / fix_one / (jnp.sqrt(second_new / fix_two) + ADAM_EPS)
    return (weight - rate * (update + DECAY * weight), first_new, second_new)


def sum_to_shares(partial):
    return lax.psum_scatter(
        partial.astype(HALF), TP, scatter_dimension=0, tiled=True
    ).astype(FLOAT)


def sum_to_owners(partial):
    return lax.psum_scatter(
        partial.astype(HALF), DP, scatter_dimension=0, tiled=True
    ).astype(FLOAT)


SEG_MOST = 256
CORES = 2
MESH = pl.DeviceIdType.MESH
NT_DIMS = (((1,), (1,)), ((), ()))
TN_DIMS = (((0,), (0,)), ((), ()))
VMEM_BYTES = 62 * 1024 * 1024


def line_length(count):
    length = 1
    while (2 * length) ** 2 <= count:
        length *= 2
    return length


def mm(left, right):
    return jnp.dot(left, right, preferred_element_type=FLOAT)


def mm_nt(left, right):
    return lax.dot_general(left, right, NT_DIMS, preferred_element_type=FLOAT)


def mm_tn(left, right):
    return lax.dot_general(left, right, TN_DIMS, preferred_element_type=FLOAT)


def split_two(values):
    high = values.astype(HALF)
    return high, (values - high.astype(FLOAT)).astype(HALF)


def cond_picks(seg_cond, conds):
    return (lax.broadcasted_iota(jnp.int32, (conds, 1), 0) == seg_cond[...]).astype(FLOAT).astype(HALF)


def pick_rows(picks, values):
    high, rest = split_two(values)
    middle, low = split_two(values - high.astype(FLOAT))
    return mm_tn(picks, high) + mm_tn(picks, middle) + mm_tn(picks, low)


class Place:
    def __init__(self, dp_count, tensor_count):
        self.dp_count, self.tensor_count = dp_count, tensor_count
        self.xs = line_length(dp_count)
        self.zs = dp_count // self.xs
        self.ys = tensor_count // CORES
        self.dp, self.tensor = lax.axis_index(DP), lax.axis_index(TP)
        self.z, self.x = lax.div(self.dp, self.xs), lax.rem(self.dp, self.xs)
        self.y, self.core = lax.div(self.tensor, CORES), lax.rem(self.tensor, CORES)

    def z_of(self, step):
        return lax.rem(self.z + step + self.zs, self.zs)

    def x_of(self, step):
        return lax.rem(self.x + step + self.xs, self.xs)

    def z_peer(self, step):
        return (self.z_of(step) * self.xs + self.x, self.tensor)

    def x_peer(self, step):
        return (self.z * self.xs + self.x_of(step), self.tensor)

    def tensor_peer(self, step):
        return (self.dp, lax.rem(self.tensor + step, self.tensor_count))

    def core_peer(self):
        return (self.dp, self.y * CORES + 1 - self.core)

    def y_peer(self):
        return (self.dp, (1 - self.y) * CORES + self.core)

    def share_of(self, other_y, other_core):
        y = 1 - self.y if other_y else self.y
        core = 1 - self.core if other_core else self.core
        return y * CORES + core


def greet(peers):
    barrier = pltpu.get_barrier_semaphore()
    for peer in peers:
        pl.semaphore_signal(barrier, inc=1, device_id=peer, device_id_type=MESH)
    pl.semaphore_wait(barrier, len(peers))


def remote(src, dst, sends, recvs, peer):
    return pltpu.make_async_remote_copy(
        src_ref=src, dst_ref=dst, send_sem=sends, recv_sem=recvs, device_id=peer, device_id_type=MESH
    )


def rows_at(start, count):
    return pl.ds(pl.multiple_of(start, 16), count)


AHEAD = 3


def unit_rows(shard, most=48):
    return most if shard % most == 0 else shard


FIRST_UNIT, LAST_UNIT = 48, 48


class Gather:
    def __init__(self, place, pieces, z_sems, x_sems):
        self.place, self.pieces = place, pieces
        self.z_send, self.z_recv = z_sems
        self.x_send, self.x_recv = x_sems
        self.hops = place.zs - 1
        self.ticks = 0

    def slot(self, piece, z, x):
        full, shard, first, count = self.pieces[piece]
        return full.at[rows_at((z * self.place.xs + x) * shard + first, count)]

    def hop(self, piece, source, step, sem):
        at = self.place
        chunk = self.slot(piece, source, at.x)
        return remote(chunk, chunk, self.z_send.at[piece, sem], self.z_recv.at[piece, sem], at.z_peer(step))

    def x_copy(self, piece, source, step):
        at = self.place
        chunk = self.slot(piece, source, at.x)
        sems = self.x_send.at[piece, source, step - 1], self.x_recv.at[piece, source, step - 1]
        return remote(chunk, chunk, *sems, at.x_peer(step))

    def x_landing(self, piece, source, step):
        at = self.place
        chunk = self.slot(piece, source, at.x_of(-step))
        sems = self.x_send.at[piece, source, step - 1], self.x_recv.at[piece, source, step - 1]
        return remote(chunk, chunk, *sems, at.x_peer(step))

    def along_x(self, piece, source):
        for step in range(1, self.place.xs):
            self.x_copy(piece, source, step).start()

    def start(self, piece):
        at = self.place

        @pl.when(at.z < at.zs - 1)
        def _():
            self.hop(piece, at.z, 1, 0).start()

        @pl.when(at.z > 0)
        def _():
            self.hop(piece, at.z, -1, self.hops).start()

        self.along_x(piece, at.z)

    def pass_on(self, piece, away):
        at, hops = self.place, self.hops

        @pl.when(at.z >= away)
        def _():
            self.hop(piece, at.z - away, 1, away - 1).wait_recv()
            if away < hops:
                @pl.when(at.z < at.zs - 1)
                def _():
                    self.hop(piece, at.z - away, 1, away).start()
            self.along_x(piece, at.z - away)

        @pl.when(at.z + away < at.zs)
        def _():
            self.hop(piece, at.z + away, -1, hops + away - 1).wait_recv()
            if away < hops:
                @pl.when(at.z > 0)
                def _():
                    self.hop(piece, at.z + away, -1, hops + away).start()
            self.along_x(piece, at.z + away)

    def tick(self):
        now = self.ticks
        for away in range(1, self.hops + 1):
            if 0 <= now - away + 1 < len(self.pieces):
                self.pass_on(now - away + 1, away)
        if now + AHEAD < len(self.pieces):
            self.start(now + AHEAD)
        self.ticks += 1

    def tick_until(self, piece):
        while self.ticks < min(piece, len(self.pieces) - 1) + self.hops:
            self.tick()

    def arrive(self, piece):
        at = self.place
        for source in range(at.zs):
            for step in range(1, at.xs):
                self.x_landing(piece, source, step).wait_recv()

    def finish(self, piece):
        at, hops = self.place, self.hops
        for away in range(hops):
            @pl.when((at.z >= away) & (at.z < at.zs - 1))
            def _(away=away):
                self.hop(piece, at.z - away, 1, away).wait_send()

            @pl.when((at.z + away < at.zs) & (at.z > 0))
            def _(away=away):
                self.hop(piece, at.z + away, -1, hops + away).wait_send()
        for source in range(at.zs):
            for step in range(1, at.xs):
                self.x_copy(piece, source, step).wait_send()


def layer_norm(values):
    mean = jnp.mean(values, axis=-1, keepdims=True)
    centered = values - mean
    inv_std = lax.rsqrt(jnp.mean(centered * centered, axis=-1, keepdims=True) + NORM_EPSILON)
    return centered * inv_std, inv_std


def forward_kernel(
    sizes,
    x_ref, seg_col, seg_row, seg_cond, cond_ref, ada_ref, head_bias, inner_bias, shared_bias,
    proj_place, wq_raw, wp_raw, wi_raw, wo_raw,
    wq_out, wp_out, wi_out, wo_out, hid_a_out, heads_out, lse_out, att_out, hid_b_out, act_out,
    slope_out, far_out, own_out, branch_out, middle_out, modk_out,
    wq_full, wp_full, wp_tight, wi_full, wo_full, hid_a, heads, lse, lse_heads, att_heads, att, part, core_in,
    y_out, y_in, hid_b, act, slope, ff_part, ff_in, ff_far, ff_own, branch, middle, modk, mods, ada_tile,
    wp_wide,
    z_send, z_recv, x_send, x_recv, mod_send, mod_recv, sum_send, sum_recv, gat_send, gat_recv, ff_send, ff_recv,
    ada_sem, save_sem,
):
    at = Place(sizes[DP], sizes[TP])
    tokens, width, columns, share = sizes["tokens"], sizes["width"], sizes["columns"], sizes["share"]
    nheads, segs = columns // HD, seg_cond.shape[1]
    window = min(tokens, share + 2 * SEG_MOST)
    greet(
        [at.z_peer(s) for s in range(1, at.zs)]
        + [at.x_peer(s) for s in range(1, at.xs)]
        + [at.tensor_peer(s) for s in range(1, at.tensor_count)]
    )
    pieces, lists = [], []
    for full, shard in (
        (wq_full, wq_raw.shape[1]), (wp_full, wp_wide.shape[0]), (wi_full, wi_raw.shape[0]), (wo_full, wo_raw.shape[0])
    ):
        unit = unit_rows(shard, 48 if lists else FIRST_UNIT)
        lists.append(list(range(len(pieces), len(pieces) + shard // unit)))
        pieces += [(full, shard, first, unit) for first in range(0, shard, unit)]
    list_q, list_p, list_i, list_o = lists
    gather = Gather(at, pieces, (z_send, z_recv), (x_send, x_recv))
    last = len(pieces)

    def own_rows_of(full, shard):
        return rows_at(at.dp * shard, shard)

    wq_full[own_rows_of(wq_full, wq_raw.shape[1]), :] = jnp.concatenate(
        [wq_raw[part_index] for part_index in range(3)], axis=1
    ).astype(HALF)
    for piece in list_q[:AHEAD]:
        gather.start(piece)
    wp_wide[...] = jnp.zeros_like(wp_wide)
    wp_wide[0:wp_raw.shape[0], :] = wp_raw[...]
    for raw, full in ((wp_wide, wp_full), (wi_raw, wi_full), (wo_raw, wo_full)):
        full[own_rows_of(full, raw.shape[0]), :] = raw[...].astype(HALF)
    for piece in range(len(list_q[:AHEAD]), AHEAD):
        gather.start(piece)

    def ada_copy(group):
        return pltpu.make_async_copy(ada_ref.at[group], ada_tile.at[group % 2], ada_sem.at[group % 2])

    ada_copy(0).start()
    cond_high, cond_low = split_two(silu(pick_rows(cond_picks(seg_cond, cond_ref.shape[0]), cond_ref[...])))
    cond_both = jnp.concatenate([cond_high, cond_low], axis=0)
    for group in range(6):
        if group in (2, 4):
            gather.tick()
        if group < 5:
            ada_copy(group + 1).start()
        ada_copy(group).wait()
        weight_high, weight_low = split_two(ada_tile[group % 2])
        both = mm_nt(cond_both, weight_high)
        mods[at.tensor, group] = (
            both[:segs] + both[segs:] + mm_nt(cond_high, weight_low)
            + head_bias[3 + group:4 + group, :]
        )

    def mod_copy(step):
        own = mods.at[at.tensor]
        return remote(own, own, mod_send.at[step - 1], mod_recv.at[step - 1], at.tensor_peer(step))

    def mod_landing(step):
        landed = mods.at[lax.rem(at.tensor + at.tensor_count - step, at.tensor_count)]
        return remote(landed, landed, mod_send.at[step - 1], mod_recv.at[step - 1], at.tensor_peer(step))

    for step in range(1, at.tensor_count):
        mod_copy(step).start()
    gather.tick()
    for step in range(1, at.tensor_count):
        mod_landing(step).wait_recv()
    for group in range(6):
        whole = jnp.concatenate([mods[t, group] for t in range(at.tensor_count)], axis=1)
        high, low = split_two(whole)
        modk[group] = jnp.concatenate([high, low], axis=0)

    def pick(rows):
        ids = seg_col[rows, :]
        lanes = lax.broadcasted_iota(jnp.int32, (1, 2 * segs), 1)
        return (ids == lax.rem(lanes, segs)).astype(FLOAT).astype(HALF)

    gather.tick()

    def hidden_block(index, carry):
        rows = rows_at(index * share, share)
        normed, _ = layer_norm(x_ref[rows, :].astype(FLOAT))
        chosen = pick(rows)
        hid_a[rows, :] = (normed * (1.0 + mm(chosen, modk[1])) + mm(chosen, modk[0])).astype(HALF)
        return carry

    lax.fori_loop(0, tokens // share // 2, hidden_block, 0)
    gather.tick_until(list_q[-1] // 2)
    lax.fori_loop(tokens // share // 2, tokens // share, hidden_block, 0)
    gather.tick_until(list_q[-1])
    for piece in list_q:
        gather.arrive(piece)

    qkv_bias = jnp.concatenate([head_bias[i:i + 1, :] for i in range(3)], axis=1)

    def qkv_block(index, carry):
        rows = rows_at(index * share, share)
        values = mm(hid_a[rows, :], wq_full[...]) + qkv_bias
        for head in range(3 * nheads):
            heads[head, rows, :] = values[:, head * HD:(head + 1) * HD].astype(HALF)
        return carry

    lax.fori_loop(0, tokens // share, qkv_block, 0)

    def attend(block):
        start = block * share
        rows = rows_at(start, share)
        first = pl.multiple_of(jnp.clip(start - SEG_MOST, 0, tokens - window), 128)
        keys = pl.ds(first, window)

        def one_head(head, carry):
            same = seg_col[rows, :] == seg_row[:, keys]
            scores = mm_nt(heads[head, rows, :], heads[nheads + head, keys, :]) * (1.0 / math.sqrt(HD))
            scores = jnp.where(same, scores, -1e30)
            top = jnp.max(scores, axis=-1, keepdims=True)
            expo = jnp.exp(scores - top)
            total = jnp.sum(expo, axis=-1, keepdims=True)
            probs = (expo * (1.0 / total)).astype(HALF)
            att_heads[head, :, :] = mm(probs, heads[2 * nheads + head, keys, :])
            lse_heads[head] = top + jnp.log(total)
            return carry

        lax.fori_loop(0, nheads, one_head, 0)
        joined = jnp.concatenate([att_heads[head] for head in range(nheads)], axis=1).astype(HALF)
        att[rows, :] = joined
        lse[rows, :] = jnp.concatenate([lse_heads[head] for head in range(nheads)], axis=1)
        return joined

    def core_copy(slot, src):
        return remote(src, core_in.at[slot], sum_send.at[slot], sum_recv.at[slot], at.core_peer())

    y_copy = remote(y_out, y_in, sum_send.at[2], sum_recv.at[2], at.y_peer())

    gather.tick_until(list_p[0])
    joined = attend(at.share_of(True, True))
    gather.arrive(list_p[0])
    wp_tight[...] = mm(proj_place[...], wp_full[...]).astype(HALF)
    part[0] = mm(joined, wp_tight[...]).astype(HALF)
    core_copy(0, part.at[0]).start()
    joined = attend(at.share_of(False, True))
    part[1] = mm(joined, wp_tight[...]).astype(HALF)
    core_copy(1, part.at[1]).start()
    gather.tick_until(list_i[0])
    joined = attend(at.share_of(True, False))
    summed = mm(joined, wp_tight[...])
    core_copy(0, part.at[0]).wait_recv()
    y_out[...] = (summed + core_in[0].astype(FLOAT)).astype(HALF)
    y_copy.start()
    joined = attend(at.share_of(False, False))
    summed = mm(joined, wp_tight[...])
    core_copy(1, part.at[1]).wait_recv()
    summed = summed + core_in[1].astype(FLOAT)
    gather.tick_until(list_i[0] + 1)
    y_copy.wait_recv()
    branch[...] = summed + y_in[...].astype(FLOAT) + shared_bias[0:1, :]

    own_rows = rows_at(at.tensor * share, share)
    chosen = pick(own_rows)
    middle[...] = x_ref[own_rows, :].astype(FLOAT) + mm(chosen, modk[2]) * branch[...]
    normed, _ = layer_norm(middle[...])
    hid_b[own_rows, :] = (normed * (1.0 + mm(chosen, modk[4])) + mm(chosen, modk[3])).astype(HALF)

    def hid_rows(other_y, other_core):
        return hid_b.at[rows_at(at.share_of(other_y, other_core) * share, share)]

    own_hid = hid_rows(False, False)
    to_core = remote(own_hid, own_hid, gat_send.at[0], gat_recv.at[0], at.core_peer())
    to_y = remote(own_hid, own_hid, gat_send.at[1], gat_recv.at[1], at.y_peer())
    to_y.start()
    to_core.start()
    across = hid_rows(True, False)
    onward = remote(across, across, gat_send.at[2], gat_recv.at[2], at.core_peer())
    gather.tick_until(list_i[-1])
    gather.tick_until(list_o[0])
    remote(across, across, gat_send.at[1], gat_recv.at[1], at.y_peer()).wait_recv()
    onward.start()
    for piece in list_i:
        gather.arrive(piece)
    beside = hid_rows(False, True)
    remote(beside, beside, gat_send.at[0], gat_recv.at[0], at.core_peer()).wait_recv()
    far = hid_rows(True, True)
    remote(far, far, gat_send.at[2], gat_recv.at[2], at.core_peer()).wait_recv()

    def inner_block(index, carry):
        rows = rows_at(index * share, share)
        pre = mm(hid_b[rows, :], wi_full[...]) + inner_bias[...].reshape(1, -1)
        factor = math.sqrt(2.0 / math.pi)
        squared = pre * pre
        bend = jnp.tanh(factor * (pre + 0.044715 * squared * pre))
        act[rows, :] = (0.5 * pre * (1.0 + bend)).astype(HALF)
        slope[rows, :] = (
            0.5 * (1.0 + bend)
            + 0.5 * pre * (1.0 - bend * bend) * (factor * (1.0 + (3 * 0.044715) * squared))
        ).astype(HALF)
        return carry

    lax.fori_loop(0, tokens // share // 2, inner_block, 0)
    gather.tick_until(list_o[0] + 1)
    lax.fori_loop(tokens // share // 2, tokens // share, inner_block, 0)

    saves = []

    def save(src, dst):
        copy = pltpu.make_async_copy(src, dst, save_sem.at[len(saves)])
        copy.start()
        saves.append(copy)

    for src, dst in (
        (wq_full, wq_out), (wp_tight, wp_out), (wi_full, wi_out), (hid_a, hid_a_out), (heads, heads_out),
        (lse, lse_out), (att, att_out), (hid_b, hid_b_out), (act, act_out), (slope, slope_out),
        (branch, branch_out), (middle, middle_out), (modk, modk_out),
    ):
        save(src, dst)
    gather.tick_until(list_o[-1])
    for piece in list_o:
        gather.arrive(piece)
    save(wo_full, wo_out)

    def outer_block(other_y, other_core):
        rows = rows_at(at.share_of(other_y, other_core) * share, share)
        return mm(act[rows, :], wo_full[...])

    def ff_copy(slot):
        return remote(ff_part.at[slot], ff_in.at[slot], ff_send.at[slot], ff_recv.at[slot], at.core_peer())

    ff_part[0] = outer_block(True, True).astype(HALF)
    ff_copy(0).start()
    ff_part[1] = outer_block(False, True).astype(HALF)
    ff_copy(1).start()
    summed = outer_block(True, False)
    ff_copy(0).wait_recv()
    ff_far[...] = (summed + ff_in[0].astype(FLOAT)).astype(HALF)
    save(ff_far, far_out)
    summed = outer_block(False, False)
    ff_copy(1).wait_recv()
    ff_own[...] = summed + ff_in[1].astype(FLOAT)
    save(ff_own, own_out)
    ff_copy(0).wait_send()
    ff_copy(1).wait_send()

    for step in range(1, at.tensor_count):
        mod_copy(step).wait_send()
    core_copy(0, part.at[0]).wait_send()
    core_copy(1, part.at[1]).wait_send()
    y_copy.wait_send()
    to_core.wait_send()
    to_y.wait_send()
    onward.wait_send()
    for piece in range(last):
        gather.finish(piece)
    for copy in saves:
        copy.wait()


def any_spec():
    return pl.BlockSpec(memory_space=pl.ANY)


def vmem_spec():
    return pl.BlockSpec(memory_space=pltpu.VMEM)


def sizes_of(block_input, conditions, segment_ids, segment_cond, qkv_weight, inner_weight):
    dp_count, tensor_count = lax.axis_size(DP), lax.axis_size(TP)
    tokens, width = block_input.shape
    return {
        DP: dp_count,
        TP: tensor_count,
        "tokens": tokens,
        "rows": segment_ids.shape[0],
        "width": width,
        "columns": qkv_weight.shape[2],
        "hidden": inner_weight.shape[1],
        "shard": qkv_weight.shape[0],
        "share": tokens // tensor_count,
        "segs": segment_cond.shape[1],
        "conds": conditions.shape[0],
    }


def kernels_fit(sizes):
    return (
        sizes[TP] == 2 * CORES
        and sizes["rows"] == 1
        and sizes["share"] % 128 == 0
        and sizes["width"] % 128 == 0
        and sizes["hidden"] % 128 == 0
        and sizes["shard"] % 16 == 0
        and sizes["columns"] % 32 == 0
        and sizes["conds"] % (8 * sizes[TP]) == 0
    )


def placing(columns, own_rows, pad_rows, dp_count):
    tight = np.arange(columns)
    place = (tight // own_rows * pad_rows + tight % own_rows)[:, None] == np.arange(dp_count * pad_rows)
    return place.astype(np.float32)


def run_forward(sizes, block_input, seg_col, segment_ids, segment_cond, conditions, ada_weight, head_biases,
                inner_bias, shared_biases, wq, wp, wi, wo):
    tokens, width, columns, share = (sizes[k] for k in ("tokens", "width", "columns", "share"))
    hidden, dp_count, tensor_count = sizes["hidden"], sizes[DP], sizes[TP]
    nheads, segs = columns // HD, sizes["segs"]
    own_rows = columns // dp_count
    pad_rows = own_rows + -own_rows % 16
    shards = (sizes["shard"], pad_rows, sizes["shard"], hidden // dp_count)
    xs = line_length(dp_count)
    zs = dp_count // xs
    units = shards[0] // unit_rows(shards[0], FIRST_UNIT) + sum(shard // unit_rows(shard) for shard in shards[1:])
    place = jnp.asarray(placing(columns, own_rows, pad_rows, dp_count), HALF)
    shapes = [
        ((width, 3 * columns), HALF), ((columns, width), HALF), ((width, hidden), HALF),
        ((hidden, width), HALF), ((tokens, width), HALF), ((3 * nheads, tokens, HD), HALF),
        ((tokens, nheads), FLOAT), ((tokens, columns), HALF), ((tokens, width), HALF),
        ((tokens, hidden), HALF), ((tokens, hidden), HALF), ((share, width), HALF), ((share, width), FLOAT),
        ((share, width), FLOAT), ((share, width), FLOAT), ((6, 2 * segs, width), HALF),
    ]
    vmem = pltpu.VMEM
    dma = pltpu.SemaphoreType.DMA
    scratch = [
        vmem((width, 3 * columns), HALF), vmem((dp_count * pad_rows, width), HALF),
        vmem((columns, width), HALF), vmem((width, hidden), HALF), vmem((hidden, width), HALF),
        vmem((tokens, width), HALF), vmem((3 * nheads, tokens, HD), HALF),
        vmem((tokens, nheads), FLOAT), vmem((nheads, share, 1), FLOAT), vmem((nheads, share, HD), FLOAT),
        vmem((tokens, columns), HALF), vmem((2, share, width), HALF), vmem((2, share, width), HALF),
        vmem((share, width), HALF), vmem((share, width), HALF), vmem((tokens, width), HALF),
        vmem((tokens, hidden), HALF), vmem((tokens, hidden), HALF), vmem((2, share, width), HALF),
        vmem((2, share, width), HALF), vmem((share, width), HALF), vmem((share, width), FLOAT),
        vmem((share, width), FLOAT), vmem((share, width), FLOAT), vmem((6, 2 * segs, width), HALF),
        vmem((tensor_count, 6, segs, columns), FLOAT), vmem((2, columns, width), FLOAT),
        vmem((pad_rows, width), FLOAT),
        dma((units, 2 * (zs - 1))), dma((units, 2 * (zs - 1))), dma((units, zs, xs - 1)),
        dma((units, zs, xs - 1)),
        dma((tensor_count - 1,)), dma((tensor_count - 1,)), dma((3,)), dma((3,)), dma((3,)), dma((3,)), dma((2,)), dma((2,)),
        dma((2,)), dma((16,)),
    ]
    return pl.pallas_call(
        functools.partial(forward_kernel, sizes),
        out_shape=[jax.ShapeDtypeStruct(s, t) for s, t in shapes],
        in_specs=[vmem_spec()] * 5 + [any_spec()] + [vmem_spec()] * 8,
        out_specs=[any_spec()] * len(shapes),
        scratch_shapes=scratch,
        name="forward",
        compiler_params=pltpu.CompilerParams(
            collective_id=1, has_side_effects=True, vmem_limit_bytes=VMEM_BYTES
        ),
    )(
        block_input, seg_col, segment_ids, segment_cond, conditions, ada_weight, head_biases, inner_bias,
        shared_biases, place, wq, wp, wi, wo,
    )


class Scatter:
    def __init__(self, place, pieces, x_sems, z_sems):
        self.place, self.pieces = place, pieces
        self.x_send, self.x_recv = x_sems
        self.z_send, self.z_recv = z_sems

    def slot(self, piece, z, x):
        whole, x_in, z_in, shard, first, count = self.pieces[piece]
        return whole.at[rows_at((z * self.place.xs + x) * shard + first, count)]

    def x_copy(self, piece, step, z):
        at = self.place
        whole, x_in, z_in, shard, first, count = self.pieces[piece]
        return remote(
            self.slot(piece, z, at.x_of(step)), x_in.at[step - 1, z, pl.ds(first, count)],
            self.x_send.at[piece, step - 1, z], self.x_recv.at[piece, step - 1, z], at.x_peer(step),
        )

    def z_copy(self, piece, step):
        at = self.place
        whole, x_in, z_in, shard, first, count = self.pieces[piece]
        return remote(
            self.slot(piece, at.z_of(step), at.x), z_in.at[step - 1, pl.ds(first, count)],
            self.z_send.at[piece, step - 1], self.z_recv.at[piece, step - 1], at.z_peer(step),
        )

    def start(self, piece):
        at = self.place
        for step in range(1, at.xs):
            for z in range(at.zs):
                self.x_copy(piece, step, z).start()

    def pass_on(self, piece):
        at = self.place
        whole, x_in, z_in, shard, first, count = self.pieces[piece]
        for z in range(at.zs):
            rows = rows_at((z * at.xs + at.x) * shard + first, count)
            total = whole[rows, :].astype(FLOAT)
            for step in range(1, at.xs):
                self.x_copy(piece, step, z).wait_recv()
                total = total + x_in[step - 1, z, first:first + count, :].astype(FLOAT)
            whole[rows, :] = total.astype(HALF)
        for step in sorted(range(1, at.zs), key=lambda s: -min(s, at.zs - s)):
            self.z_copy(piece, step).start()

    def arrive(self, piece):
        for step in range(1, self.place.zs):
            self.z_copy(piece, step).wait_recv()

    def finish(self, piece):
        at = self.place
        for step in range(1, at.xs):
            for z in range(at.zs):
                self.x_copy(piece, step, z).wait_send()
        for step in range(1, at.zs):
            self.z_copy(piece, step).wait_send()


class Spread:
    def __init__(self, place, chunks, z_sems, x_sems):
        self.place, self.chunks = place, chunks
        self.z_send, self.z_recv = z_sems
        self.x_send, self.x_recv = x_sems

    def z_copy(self, part, step, source):
        at = self.place
        chunk = self.chunks[part](self.place.z_of(source) * at.xs + at.x)
        return remote(chunk, chunk, self.z_send.at[part, step - 1], self.z_recv.at[part, step - 1], at.z_peer(step))

    def x_copy(self, part, back, step, source):
        at = self.place
        chunk = self.chunks[part](at.z_of(-back) * at.xs + at.x_of(source))
        sems = self.x_send.at[part, back, step - 1], self.x_recv.at[part, back, step - 1]
        return remote(chunk, chunk, *sems, at.x_peer(step))

    def start(self, part):
        for step in range(1, self.place.zs):
            self.z_copy(part, step, 0).start()

    def pass_on(self, part):
        for back in range(self.place.zs):
            if back > 0:
                self.z_copy(part, back, -back).wait_recv()
            for step in range(1, self.place.xs):
                self.x_copy(part, back, step, 0).start()

    def finish(self, part):
        at = self.place
        for step in range(1, at.zs):
            self.z_copy(part, step, 0).wait_send()
        for back in range(at.zs):
            for step in range(1, at.xs):
                self.x_copy(part, back, step, -step).wait_recv()
                self.x_copy(part, back, step, 0).wait_send()


def image_sums(chosen, values):
    high, low = split_two(values)
    return mm_tn(chosen, high) + mm_tn(chosen, low)


def backward_kernel(
    sizes,
    seg_col, seg_row, seg_cond, shared_bias, place_back,
    x_in, cot_in, wq_in, wp_in, wi_in, wo_in, hid_a_in, heads_in, lse_in, att_in, hid_b_in, act_in, slope_in,
    far_in, own_in, branch_in, middle_in, modk_in,
    block_out, input_out, qkv_out, proj_out, inner_out, outer_out, mods_out, packs_out, picks_out,
    wq, wp, wi, wo, heads, lse, att, hid_b, act, slope, cot, modk, branch, middle, ff_own,
    cot_own, x_own, gatt, key_sum, value_sum, grad_a, part, core_in, y_out, y_in, ff_in, grad_mid,
    whole_o, whole_i, whole_p, whole_q, xin_o, xin_i, xin_p, xin_q, zin_o, zin_i, zin_p, zin_q,
    mod_send_buf, mod_in, mods, packs, picks,
    load_sem, save_sem, x_send, x_recv, z_send, z_recv, sum_send, sum_recv, gat_send, gat_recv,
    ff_send, ff_recv, mod_send, mod_recv, all_z_send, all_z_recv, all_x_send, all_x_recv,
):
    at = Place(sizes[DP], sizes[TP])
    tokens, width, columns, share = sizes["tokens"], sizes["width"], sizes["columns"], sizes["share"]
    hidden = sizes["hidden"]
    nheads, segs = columns // HD, sizes["segs"]
    blocks = tokens // share
    scale = 1.0 / math.sqrt(HD)

    own_rows = rows_at(at.tensor * share, share)
    loads = {}

    def load(name, src, dst):
        copy = pltpu.make_async_copy(src, dst, load_sem.at[len(loads)])
        copy.start()
        loads[name] = copy

    load("cot", cot_in, cot)
    load("modk", modk_in, modk)
    load("act", act_in, act)
    load("wo", wo_in, wo)
    load("slope", slope_in, slope)
    load("wi", wi_in, wi)
    load("hid_b", hid_b_in, hid_b)
    load("middle", middle_in, middle)
    load("branch", branch_in, branch)
    load("ff_own", own_in, ff_own)
    load("att", att_in, att)
    load("wp", wp_in, wp)
    load("heads", heads_in, heads)
    load("lse", lse_in, lse)
    load("wq", wq_in, wq)
    load("x", x_in.at[own_rows], x_own)
    greet(
        [at.z_peer(s) for s in range(1, at.zs)]
        + [at.x_peer(s) for s in range(1, at.xs)]
        + [at.tensor_peer(s) for s in range(1, at.tensor_count)]
    )
    ff_copy = remote(far_in, ff_in, ff_send, ff_recv, at.y_peer())
    ff_copy.start()

    pieces = []
    for whole, x_in, z_in in (
        (whole_o, xin_o, zin_o), (whole_i, xin_i, zin_i), (whole_p, xin_p, zin_p), (whole_q, xin_q, zin_q)
    ):
        shard = x_in.shape[2]
        unit = unit_rows(shard, LAST_UNIT if whole is whole_q else 48)
        pieces.append([(whole, x_in, z_in, shard, first, unit) for first in range(0, shard, unit)])
    flat = [piece for group in pieces for piece in group]
    scatter = Scatter(at, flat, (x_send, x_recv), (z_send, z_recv))
    bounds = [sum(len(g) for g in pieces[:i]) for i in range(len(pieces) + 1)]
    list_o, list_i, list_p, list_q = (list(range(bounds[i], bounds[i + 1])) for i in range(4))

    def one_hot(rows, count):
        lanes = lax.broadcasted_iota(jnp.int32, (1, count), 1)
        return (seg_col[rows, :] == lax.rem(lanes, segs)).astype(FLOAT).astype(HALF)

    loads["cot"].wait()
    loads["modk"].wait()
    cot_own[...] = cot[own_rows, :]
    packs[at.dp] = jnp.zeros_like(packs[at.dp])
    picks[at.dp] = jnp.zeros_like(picks[at.dp])

    def grad_b_block(index, total):
        rows = rows_at(index * share, share)
        gate = mm(one_hot(rows, 2 * segs), modk[5])
        value = (cot[rows, :].astype(FLOAT) * gate).astype(HALF)
        cot[rows, :] = value
        return total + jnp.sum(value.astype(FLOAT), axis=0, keepdims=True)

    packs[at.dp, 3:4, 0:width] = lax.fori_loop(0, blocks, grad_b_block, jnp.zeros((1, width), FLOAT))
    loads["act"].wait()

    def lanes_at(index):
        return pl.ds(pl.multiple_of(index * 128, 128), 128)

    def outer_grad_block(index, carry):
        whole_o[rows_at(index * 128, 128), :] = mm_tn(act[:, lanes_at(index)], cot[...]).astype(HALF)
        return carry

    lax.fori_loop(0, hidden // 128, outer_grad_block, 0)
    for piece in list_o:
        scatter.start(piece)
    load("hid_a", hid_a_in, act)
    loads["wo"].wait()
    loads["slope"].wait()
    loads["wi"].wait()

    def back_two(block):
        rows = rows_at(block * share, share)
        grad_act = mm_nt(cot[rows, :], wo[...])
        grad_pre = (grad_act * slope[rows, :].astype(FLOAT)).astype(HALF)
        slope[rows, :] = grad_pre
        return mm_nt(grad_pre, wi[...]), jnp.sum(grad_pre.astype(FLOAT), axis=0, keepdims=True)

    def core_copy(slot):
        return remote(part.at[slot], core_in.at[slot], sum_send.at[slot], sum_recv.at[slot], at.core_peer())

    y_copy = remote(y_out, y_in, sum_send.at[2], sum_recv.at[2], at.y_peer())

    def sum_shares(make, between, held):
        part[0] = make(at.share_of(True, True)).astype(HALF)
        core_copy(0).start()
        part[1] = make(at.share_of(False, True)).astype(HALF)
        core_copy(1).start()
        summed = make(at.share_of(True, False))
        core_copy(0).wait_recv()
        y_out[...] = (summed + core_in[0].astype(FLOAT)).astype(HALF)
        y_copy.start()
        summed = make(at.share_of(False, False))
        core_copy(1).wait_recv()
        held[...] = summed + core_in[1].astype(FLOAT)
        between()
        y_copy.wait_recv()
        core_copy(0).wait_send()
        core_copy(1).wait_send()
        y_copy.wait_send()
        return held[...] + y_in[...].astype(FLOAT)

    bias_total = [jnp.zeros((1, hidden), FLOAT)]

    def make_two(block):
        value, bias = back_two(block)
        bias_total[0] = bias_total[0] + bias
        return value

    def inner_grads():
        packs[at.dp, 1:2, 0:hidden] = bias_total[0]
        loads["hid_b"].wait()

        def inner_grad_block(index, carry):
            whole_i[rows_at(index * 128, 128), :] = mm_tn(hid_b[:, lanes_at(index)], slope[...]).astype(HALF)
            return carry

        lax.fori_loop(0, width // 128, inner_grad_block, 0)
        for piece in list_i:
            scatter.start(piece)
        for piece in list_o[:2]:
            scatter.pass_on(piece)

    grad_hid_b = sum_shares(make_two, inner_grads, grad_mid)

    loads["middle"].wait()
    loads["branch"].wait()
    loads["ff_own"].wait()
    chosen = one_hot(own_rows, 2 * segs)
    normed, inv_std = layer_norm(middle[...])
    grad_normed = grad_hid_b * (1.0 + mm(chosen, modk[4]))
    first_mean = jnp.mean(grad_normed, axis=-1, keepdims=True)
    second_mean = jnp.mean(grad_normed * normed, axis=-1, keepdims=True)
    grad_mid[...] = cot_own[...].astype(FLOAT) + inv_std * (grad_normed - first_mean - normed * second_mean)
    grad_a[own_rows, :] = (grad_mid[...] * mm(chosen, modk[2])).astype(HALF)

    def hid_rows(other_y, other_core):
        return grad_a.at[rows_at(at.share_of(other_y, other_core) * share, share)]

    own_hid = hid_rows(False, False)
    to_core = remote(own_hid, own_hid, gat_send.at[0], gat_recv.at[0], at.core_peer())
    to_y = remote(own_hid, own_hid, gat_send.at[1], gat_recv.at[1], at.y_peer())
    to_y.start()
    to_core.start()
    across, beside, far = hid_rows(True, False), hid_rows(False, True), hid_rows(True, True)
    onward = remote(across, across, gat_send.at[2], gat_recv.at[2], at.core_peer())

    images = one_hot(own_rows, segs)

    def keep_mod(group, values):
        sums = image_sums(images, values)
        for t in range(at.tensor_count):
            mod_send_buf[t, group] = sums[:, t * columns:(t + 1) * columns]

    keep_mod(2, grad_mid[...] * branch[...])
    keep_mod(3, grad_hid_b)
    keep_mod(4, grad_hid_b * normed)
    mod_parts = ((2, 4), (0, 2))
    spread = Spread(
        at,
        [
            lambda source: mods.at[source, pl.ds(2, 4)],
            lambda source: mods.at[source, pl.ds(0, 2)],
            lambda source: packs.at[source],
            lambda source: picks.at[source],
        ],
        (all_z_send, all_z_recv), (all_x_send, all_x_recv),
    )

    def mod_copy(part_index, step):
        first, count = mod_parts[part_index]
        to = lax.rem(at.tensor + step, at.tensor_count)
        return remote(
            mod_send_buf.at[to, pl.ds(first, count)], mod_in.at[step - 1, pl.ds(first, count)],
            mod_send.at[part_index, step - 1], mod_recv.at[part_index, step - 1], at.tensor_peer(step),
        )

    def mod_start(part_index):
        for step in range(1, at.tensor_count):
            mod_copy(part_index, step).start()

    def mod_spread(part_index):
        first, count = mod_parts[part_index]
        total = mod_send_buf[at.tensor, first:first + count]
        for step in range(1, at.tensor_count):
            mod_copy(part_index, step).wait_recv()
            total = total + mod_in[step - 1, first:first + count]
        mods[at.dp, first:first + count] = total
        spread.start(part_index)

    window = min(tokens, share + 2 * SEG_MOST)
    key_sum[...] = jnp.zeros_like(key_sum)
    value_sum[...] = jnp.zeros_like(value_sum)

    def grad_att(block):
        rows = rows_at(block * share, share)
        values = mm_nt(grad_a[rows, :], wp[...])
        for head in range(nheads):
            gatt[head] = values[:, head * HD:(head + 1) * HD].astype(HALF)
        return jnp.sum(grad_a[rows, :].astype(FLOAT), axis=0, keepdims=True)

    def attend_back(block):
        start = block * share
        rows = rows_at(start, share)
        keys_at = pl.ds(pl.multiple_of(jnp.clip(start - SEG_MOST, 0, tokens - window), 128), window)

        def one_head(head, carry):
            query = heads[head, rows, :]
            keys = heads[nheads + head, keys_at, :]
            values = heads[2 * nheads + head, keys_at, :]
            grad = gatt[head]
            same = seg_col[rows, :] == seg_row[:, keys_at]
            scores = jnp.where(same, mm_nt(query, keys) * scale, -1e30)
            lanes = lax.broadcasted_iota(jnp.int32, (1, nheads), 1)
            peak = jnp.sum(jnp.where(lanes == head, lse[rows, :], 0.0), axis=-1, keepdims=True)
            probs = jnp.exp(scores - peak)
            grad_probs = mm_nt(grad, values)
            center = jnp.sum(probs * grad_probs, axis=-1, keepdims=True)
            grad_scores = (probs * (grad_probs - center)).astype(HALF)
            heads[head, rows, :] = (mm(grad_scores, keys) * scale).astype(HALF)
            key_sum[head, keys_at, :] += mm_tn(grad_scores, query)
            value_sum[head, keys_at, :] += mm_tn(probs.astype(HALF), grad)
            return carry

        lax.fori_loop(0, nheads, one_head, 0)

    loads["wp"].wait()
    loads["heads"].wait()
    loads["lse"].wait()
    for piece in list_o[2:]:
        scatter.pass_on(piece)
    grad_a_sum = grad_att(at.share_of(False, False))
    attend_back(at.share_of(False, False))
    remote(beside, beside, gat_send.at[0], gat_recv.at[0], at.core_peer()).wait_recv()
    grad_a_sum = grad_a_sum + grad_att(at.share_of(False, True))
    remote(across, across, gat_send.at[1], gat_recv.at[1], at.y_peer()).wait_recv()
    onward.start()
    attend_back(at.share_of(False, True))
    grad_a_sum = grad_a_sum + grad_att(at.share_of(True, False))
    scatter.pass_on(list_i[0])
    attend_back(at.share_of(True, False))
    remote(far, far, gat_send.at[2], gat_recv.at[2], at.core_peer()).wait_recv()
    grad_a_sum = grad_a_sum + grad_att(at.share_of(True, True))
    attend_back(at.share_of(True, True))
    for piece in list_i[1:2]:
        scatter.pass_on(piece)
    packs[at.dp, 2:3, 0:width] = grad_a_sum
    loads["att"].wait()
    proj_grad = mm_tn(att[...], grad_a[...]).astype(HALF)
    whole_p[...] = mm(place_back[...], proj_grad).astype(HALF)
    for piece in list_p:
        scatter.start(piece)
    to_core.wait_send()
    to_y.wait_send()
    onward.wait_send()

    def join_block(index, total):
        rows = rows_at(index * share, share)
        parts = [heads[head, rows, :].astype(FLOAT) for head in range(nheads)]
        parts += [(key_sum[head, rows, :] * scale).astype(HALF).astype(FLOAT) for head in range(nheads)]
        parts += [value_sum[head, rows, :].astype(HALF).astype(FLOAT) for head in range(nheads)]
        values = jnp.concatenate(parts, axis=1)
        grad_a[rows, 0:3 * columns] = values.astype(HALF)
        return total + jnp.sum(values, axis=0, keepdims=True)

    packs[at.dp, 0:1, 0:3 * columns] = lax.fori_loop(0, blocks, join_block, jnp.zeros((1, 3 * columns), FLOAT))
    for piece in list_i[2:]:
        scatter.pass_on(piece)
    loads["hid_a"].wait()

    def qkv_grad_block(index, carry):
        whole_q[rows_at(index * 128, 128), :] = mm_tn(act[:, lanes_at(index)], grad_a[:, 0:3 * columns]).astype(HALF)
        return carry

    lax.fori_loop(0, width // 128, qkv_grad_block, 0)
    for piece in list_q:
        scatter.start(piece)
    loads["wq"].wait()

    saves = []

    def save(src, dst):
        copy = pltpu.make_async_copy(src, dst, save_sem.at[len(saves)])
        copy.start()
        saves.append(copy)

    def mod_sums():
        for piece in list_p:
            scatter.pass_on(piece)
        ff_copy.wait_recv()
        branch_b = ff_own[...] + ff_in[...].astype(FLOAT) + shared_bias[1:2, :]
        keep_mod(5, cot_own[...].astype(FLOAT) * branch_b)
        ff_in[...] = (middle[...] + mm(chosen, modk[5]) * branch_b).astype(HALF)
        save(ff_in, block_out)
        mod_start(0)
        for part_index in (2, 3):
            spread.start(part_index)
        for piece in list_q[:len(list_q) // 3]:
            scatter.pass_on(piece)

    unit = lax.broadcasted_iota(jnp.int32, (segs, 1), 0) == lax.broadcasted_iota(jnp.int32, (1, segs), 1)
    conds = sizes["conds"]
    picks[at.dp, 0:segs, 0:conds] = mm_nt(unit.astype(FLOAT).astype(HALF), cond_picks(seg_cond, conds))
    grad_hid_a = sum_shares(
        lambda block: mm_nt(grad_a[rows_at(block * share, share), 0:3 * columns], wq[...]), mod_sums, branch
    )
    loads["x"].wait()
    normed, inv_std = layer_norm(x_own[...].astype(FLOAT))
    grad_normed = grad_hid_a * (1.0 + mm(chosen, modk[1]))
    first_mean = jnp.mean(grad_normed, axis=-1, keepdims=True)
    second_mean = jnp.mean(grad_normed * normed, axis=-1, keepdims=True)
    grad_mid[...] = grad_mid[...] + inv_std * (grad_normed - first_mean - normed * second_mean)
    save(grad_mid, input_out)
    mod_spread(0)
    keep_mod(0, grad_hid_a)
    keep_mod(1, grad_hid_a * normed)
    mod_start(1)
    for piece in list_q[len(list_q) // 3:]:
        scatter.pass_on(piece)
    for part_index in (2, 3, 0):
        spread.pass_on(part_index)
    mod_spread(1)
    spread.pass_on(1)
    outs = ((list_o, outer_out), (list_i, inner_out), (list_p, proj_out), (list_q, qkv_out))
    for pieces_of, out in outs:
        whole, x_in, z_in, shard = flat[pieces_of[0]][:4]
        for piece in pieces_of:
            scatter.arrive(piece)
        save(whole.at[rows_at((at.z * at.xs + at.x) * shard, shard)], out.at[0])
        for step in range(1, at.zs):
            save(z_in.at[step - 1], out.at[step])
    for part_index in range(4):
        spread.finish(part_index)
    save(mods, mods_out)
    save(packs, packs_out)
    save(picks, picks_out)
    ff_copy.wait_send()
    for piece in range(len(flat)):
        scatter.finish(piece)
    for part_index in range(2):
        for step in range(1, at.tensor_count):
            mod_copy(part_index, step).wait_send()
    for copy in saves:
        copy.wait()


def run_backward(sizes, block_input, seg_col, segment_ids, segment_cond, shared_biases, cotangent, kept):
    (wq, wp, wi, wo, hid_a, heads, lse, att, hid_b, act, slope, far, own, branch, middle, modk) = kept
    tokens, width, columns, share = (sizes[k] for k in ("tokens", "width", "columns", "share"))
    hidden, dp_count, tensor_count, segs = sizes["hidden"], sizes[DP], sizes[TP], sizes["segs"]
    nheads = columns // HD
    own_rows = columns // dp_count
    pad_rows = own_rows + -own_rows % 16
    xs = line_length(dp_count)
    zs = dp_count // xs
    shards = (hidden // dp_count, width // dp_count, pad_rows, width // dp_count)
    wholes = ((hidden, width), (width, hidden), (dp_count * pad_rows, width), (width, 3 * columns))
    units = sum(shard // unit_rows(shard) for shard in shards[:3]) + shards[3] // unit_rows(shards[3], LAST_UNIT)
    place = jnp.asarray(placing(columns, own_rows, pad_rows, dp_count).T, HALF)
    pack_width = max(width, hidden, 3 * columns)
    shapes = [((share, width), HALF), ((share, width), FLOAT)]
    shapes += [((zs, shards[i], wholes[i][1]), HALF) for i in (3, 2, 1, 0)]
    shapes += [((dp_count, 6, segs, columns), FLOAT), ((dp_count, 4, pack_width), FLOAT)]
    shapes += [((dp_count, 8, 128), FLOAT)]
    vmem, dma = pltpu.VMEM, pltpu.SemaphoreType.DMA
    scratch = [
        vmem((width, 3 * columns), HALF), vmem((columns, width), HALF), vmem((width, hidden), HALF),
        vmem((hidden, width), HALF), vmem((3 * nheads, tokens, HD), HALF), vmem((tokens, nheads), FLOAT),
        vmem((tokens, columns), HALF), vmem((tokens, width), HALF), vmem((tokens, hidden), HALF),
        vmem((tokens, hidden), HALF), vmem((tokens, width), HALF), vmem((6, 2 * segs, width), HALF),
        vmem((share, width), FLOAT), vmem((share, width), FLOAT), vmem((share, width), FLOAT),
        vmem((share, width), HALF), vmem((share, width), HALF), vmem((nheads, share, HD), HALF),
        vmem((nheads, tokens, HD), FLOAT), vmem((nheads, tokens, HD), FLOAT), vmem((tokens, width), HALF),
        vmem((2, share, width), HALF), vmem((2, share, width), HALF), vmem((share, width), HALF),
        vmem((share, width), HALF), vmem((share, width), HALF), vmem((share, width), FLOAT),
    ]
    scratch += [vmem(shape, HALF) for shape in wholes]
    scratch += [vmem((xs - 1, zs, shards[i], wholes[i][1]), HALF) for i in range(4)]
    scratch += [vmem((zs - 1, shards[i], wholes[i][1]), HALF) for i in range(4)]
    scratch += [
        vmem((tensor_count, 6, segs, columns), FLOAT), vmem((tensor_count - 1, 6, segs, columns), FLOAT),
        vmem((dp_count, 6, segs, columns), FLOAT), vmem((dp_count, 4, pack_width), FLOAT),
        vmem((dp_count, 8, 128), FLOAT),
        dma((17,)), dma((5 + 4 * zs,)), dma((units, xs - 1, zs)), dma((units, xs - 1, zs)),
        dma((units, zs - 1)), dma((units, zs - 1)), dma((3,)), dma((3,)), dma((3,)), dma((3,)),
        dma(()), dma(()), dma((2, tensor_count - 1)), dma((2, tensor_count - 1)),
        dma((4, zs - 1)), dma((4, zs - 1)), dma((4, zs, xs - 1)), dma((4, zs, xs - 1)),
    ]
    return pl.pallas_call(
        functools.partial(backward_kernel, sizes),
        out_shape=[jax.ShapeDtypeStruct(s, t) for s, t in shapes],
        in_specs=[vmem_spec()] * 5 + [any_spec()] * 18,
        out_specs=[any_spec()] * len(shapes),
        scratch_shapes=scratch,
        name="backward",
        compiler_params=pltpu.CompilerParams(
            collective_id=2, has_side_effects=True, vmem_limit_bytes=VMEM_BYTES
        ),
    )(
        seg_col, segment_ids, segment_cond, shared_biases, place, block_input, cotangent, wq, wp, wi, wo, hid_a, heads, lse, att, hid_b, act, slope, far, own,
        branch, middle, modk,
    )


def on_device_general(
    block_input,
    conditions,
    segment_ids,
    segment_cond,
    cotangent,
    qkv_weight,
    proj_weight,
    inner_weight,
    outer_weight,
    ada_weight,
    head_biases,
    inner_bias,
    shared_biases,
    qkv_first,
    proj_first,
    inner_first,
    outer_first,
    ada_first,
    head_biases_first,
    inner_bias_first,
    shared_biases_first,
    qkv_second,
    proj_second,
    inner_second,
    outer_second,
    ada_second,
    head_biases_second,
    inner_bias_second,
    shared_biases_second,
):
    columns = qkv_weight.shape[2]
    heads_local = columns // HD
    rows_local = segment_ids.shape[0]
    row_length = segment_ids.shape[1]
    token_count = rows_local * row_length
    seg_count = segment_cond.shape[1]
    width = block_input.shape[1]
    share_count = token_count // lax.axis_size(TP)
    share_start = lax.axis_index(TP) * share_count

    def share(values):
        return lax.dynamic_slice_in_dim(values, share_start, share_count, 0)

    qkv_full, proj_full, inner_full, outer_full = (
        lax.all_gather(qkv_weight.astype(HALF), DP, axis=0, tiled=True),
        lax.all_gather(proj_weight.astype(HALF), DP, axis=0, tiled=True),
        lax.all_gather(inner_weight.astype(HALF), DP, axis=0, tiled=True),
        lax.all_gather(outer_weight.astype(HALF), DP, axis=0, tiled=True),
    )
    condition_select = (
        segment_cond[:, :, None] == jnp.arange(conditions.shape[0])[None, None, :]
    ).astype(FLOAT)
    condition_row_block = jnp.einsum(
        "btu,ua->bta", condition_select, conditions, precision=PRECISION_MAX
    )
    cond_act = silu(condition_row_block)
    local_mod = (
        jnp.einsum("rsd,kcd->rskc", cond_act, ada_weight, precision=PRECISION_MAX)
        + head_biases[3:][None, None]
    )
    full_mod = lax.all_gather(local_mod, TP, axis=3, tiled=True)
    seg_pick = (segment_ids[:, :, None] == jnp.arange(seg_count)[None, None, :]).astype(FLOAT)
    token_mod = jnp.einsum("rls,rskd->rlkd", seg_pick, full_mod, precision=PRECISION_MAX).reshape(
        token_count, 6, width
    )
    inputs = block_input.astype(FLOAT)
    normed_one, inv_one = normalize(inputs)
    hidden_one = (normed_one * (1.0 + token_mod[:, 1]) + token_mod[:, 0]).astype(HALF)
    qkv_values = (
        jnp.einsum("nd,dkc->nkc", hidden_one, qkv_full, preferred_element_type=FLOAT)
        + head_biases[:3][None]
    ).astype(HALF)
    row_qkv = qkv_values.reshape(rows_local, row_length, 3, heads_local, HD)
    row = 0
    attended_row, total_row = attend_forward(row_qkv[row], segment_ids[row])
    attended_rows = [attended_row]
    total_rows = [total_row]
    attended = jnp.stack(attended_rows).reshape(token_count, columns).astype(HALF)
    attn_partial = jnp.dot(attended, proj_full, preferred_element_type=FLOAT)
    share_mod = share(token_mod)
    branch_one = sum_to_shares(attn_partial) + shared_biases[0]
    middle = share(inputs) + share_mod[:, 2] * branch_one
    normed_two, inv_two = normalize(middle)
    hidden_two_share = (normed_two * (1.0 + share_mod[:, 4]) + share_mod[:, 3]).astype(HALF)
    hidden_two = lax.all_gather(hidden_two_share, TP, axis=0, tiled=True)
    pre_act = jnp.dot(hidden_two, inner_full, preferred_element_type=FLOAT) + inner_bias
    act_values, gelu_back = jax.vjp(gelu_tanh, pre_act)
    act_low = act_values.astype(HALF)
    ff_partial = jnp.dot(act_low, outer_full, preferred_element_type=FLOAT)
    branch_two = sum_to_shares(ff_partial) + shared_biases[1]
    output = middle + share_mod[:, 5] * branch_two
    grad_out = cotangent.astype(FLOAT)
    grad_two = (grad_out * token_mod[:, 5]).astype(HALF)
    outer_grad = jnp.einsum("nf,nd->fd", act_low, grad_two, preferred_element_type=FLOAT)
    grad_act = jnp.einsum("nd,fd->nf", grad_two, outer_full, preferred_element_type=FLOAT)
    grad_pre = gelu_back(grad_act)[0].astype(HALF)
    inner_grad = jnp.einsum("nd,nf->df", hidden_two, grad_pre, preferred_element_type=FLOAT)
    back_two_partial = jnp.einsum("nf,df->nd", grad_pre, inner_full, preferred_element_type=FLOAT)
    grad_hidden_two = sum_to_shares(back_two_partial)
    grad_out_share = share(grad_out)
    grad_middle = grad_out_share + norm_back(
        grad_hidden_two * (1.0 + share_mod[:, 4]), normed_two, inv_two
    )
    grad_one_share = (grad_middle * share_mod[:, 2]).astype(HALF)
    grad_one = lax.all_gather(grad_one_share, TP, axis=0, tiled=True)
    proj_grad = jnp.einsum("nc,nd->cd", attended, grad_one, preferred_element_type=FLOAT)
    grad_attended = jnp.einsum(
        "nd,cd->nc", grad_one, proj_full, preferred_element_type=FLOAT
    ).astype(HALF)
    grad_rows = grad_attended.reshape(rows_local, row_length, heads_local, HD)
    row = 0
    grad_qkv_rows = [
        attend_backward(row_qkv[row], segment_ids[row], grad_rows[row], total_rows[row])
    ]
    grad_qkv = jnp.stack(grad_qkv_rows).reshape(token_count, 3, columns).astype(HALF)
    qkv_grad = jnp.einsum("nd,nkc->dkc", hidden_one, grad_qkv, preferred_element_type=FLOAT)
    back_one_partial = jnp.einsum("nkc,dkc->nd", grad_qkv, qkv_full, preferred_element_type=FLOAT)
    grad_hidden_one = sum_to_shares(back_one_partial)
    normed_one_share, inv_one_share = share(normed_one), share(inv_one)
    input_out = grad_middle + norm_back(
        grad_hidden_one * (1.0 + share_mod[:, 1]), normed_one_share, inv_one_share
    )
    block_out = output.astype(HALF)
    contributions = jnp.concatenate(
        [
            grad_hidden_one,
            grad_hidden_one * normed_one_share,
            grad_middle * branch_one,
            grad_hidden_two,
            grad_hidden_two * normed_two,
            grad_out_share * branch_two,
        ],
        axis=1,
    )
    pick_share = share(seg_pick.reshape(token_count, seg_count))
    cond_pick = jnp.dot(pick_share, condition_select[0], precision=PRECISION_MAX)
    cond_sums = jnp.einsum("lq,lc->qc", cond_pick, contributions, precision=PRECISION_MAX)
    cond_sums = cond_sums.reshape(-1, 6, lax.axis_size(TP), columns)
    cond_sums = lax.psum_scatter(cond_sums, TP, scatter_dimension=2, tiled=True)[:, :, 0]
    cond_total = lax.psum(cond_sums, DP)
    all_act, all_silu_back = jax.vjp(silu, conditions)
    grad_all_act = jnp.einsum("qkc,kcd->qd", cond_total, ada_weight, precision=PRECISION_MAX)
    cond_grad = all_silu_back(lax.psum(grad_all_act, TP))[0]
    head_bias_grad = jnp.sum(grad_qkv.astype(FLOAT), axis=0)
    inner_bias_grad = jnp.sum(grad_pre.astype(FLOAT), axis=0)
    shared_bias_grad = jnp.stack(
        [jnp.sum(grad_one.astype(FLOAT), axis=0), jnp.sum(grad_two.astype(FLOAT), axis=0)]
    )
    ada_total = jnp.einsum("qd,qkc->kcd", all_act, cond_total, precision=PRECISION_MAX)
    head_total, inner_bias_total, shared_total = lax.psum(
        (head_bias_grad, inner_bias_grad, shared_bias_grad), DP
    )
    head_total = jnp.concatenate([head_total, jnp.sum(cond_total, axis=0)], axis=0)
    qkv_shard, proj_shard, inner_shard, outer_shard = (
        sum_to_owners(qkv_grad),
        sum_to_owners(proj_grad),
        sum_to_owners(inner_grad),
        sum_to_owners(outer_grad),
    )
    qkv_new = adam_update(qkv_weight, qkv_shard, qkv_first, qkv_second, RATES[0])
    proj_new = adam_update(proj_weight, proj_shard, proj_first, proj_second, RATES[1])
    inner_new = adam_update(inner_weight, inner_shard, inner_first, inner_second, RATES[2])
    outer_new = adam_update(outer_weight, outer_shard, outer_first, outer_second, RATES[3])
    ada_new = adam_update(ada_weight, ada_total, ada_first, ada_second, RATES[4])
    head_new = adam_update(head_biases, head_total, head_biases_first, head_biases_second, RATES[5])
    inner_bias_new = adam_update(
        inner_bias, inner_bias_total, inner_bias_first, inner_bias_second, RATES[6]
    )
    shared_new = adam_update(
        shared_biases, shared_total, shared_biases_first, shared_biases_second, RATES[7]
    )
    return (
        block_out,
        input_out,
        cond_grad,
        qkv_new[0],
        proj_new[0],
        inner_new[0],
        outer_new[0],
        ada_new[0],
        head_new[0],
        inner_bias_new[0],
        shared_new[0],
        qkv_new[1],
        proj_new[1],
        inner_new[1],
        outer_new[1],
        ada_new[1],
        head_new[1],
        inner_bias_new[1],
        shared_new[1],
        qkv_new[2],
        proj_new[2],
        inner_new[2],
        outer_new[2],
        ada_new[2],
        head_new[2],
        inner_bias_new[2],
        shared_new[2],
        qkv_new[0].astype(HALF),
        proj_new[0].astype(HALF),
        inner_new[0].astype(HALF),
        outer_new[0].astype(HALF),
    )


def update_kernel(
    sizes,
    cond_ref, mods, packs, picks, head_w, head_m, head_v, hidden_w, hidden_m, hidden_v, shared_w, shared_m, shared_v,
    *refs,
):
    width, columns, segs, hidden = sizes["width"], sizes["columns"], sizes["segs"], sizes["hidden"]
    big_in = [refs[i * 4:i * 4 + 4] for i in range(4)]
    ada_in = refs[16:19]
    part, *small_out = refs[19:29]
    ada_out = refs[29:32]
    big_out = [refs[32 + i * 4:36 + i * 4] for i in range(4)]
    refs = refs[48:]
    ada = refs[:3]
    big = [refs[3 + i * 5:8 + i * 5] for i in range(4)]
    gt, act_rows, head_grad = refs[23:26]
    ada_load, ada_save, big_load, big_save = refs[26:]
    conds, dp_count = cond_ref.shape[0], sizes[DP]

    def ada_copy(kind, group):
        return pltpu.make_async_copy(ada_in[kind].at[group], ada[kind].at[group], ada_load.at[kind, group])

    for group in range(6):
        ada_copy(0, group).start()
    for group in range(6):
        ada_copy(1, group).start()
        ada_copy(2, group).start()
    big_loads = []
    for index in range(4):
        copies = [
            pltpu.make_async_copy(big_in[index][kind], big[index][kind], big_load.at[index, kind])
            for kind in range(4)
        ]
        for copy in copies:
            copy.start()
        big_loads.append(copies)

    act = silu(cond_ref[...])
    act_high, act_low = split_two(act)
    act_rows[...] = jnp.concatenate([act_high, act_high, act_low], axis=0)
    picked = jnp.concatenate(
        [picks[row, 0:segs, 0:conds] for row in range(dp_count)], axis=0
    ).astype(HALF)
    for group in range(6):
        images = jnp.concatenate([mods[row, group] for row in range(dp_count)], axis=0)
        head_grad[3 + group:4 + group, :] = jnp.sum(images, axis=0, keepdims=True)
        high, low = split_two(images)
        sums_high, sums_low = split_two(mm_tn(high, picked) + mm_tn(low, picked))
        gt[group] = jnp.concatenate([sums_high, sums_low, sums_high], axis=1)

    part[...] = jnp.zeros_like(part)
    for group in range(6):
        ada_copy(0, group).wait()
        weight_high, weight_low = split_two(ada[0][group])
        both = mm_tn(gt[group, :, 0:2 * conds], weight_high)
        part[...] += both[:conds] + both[conds:] + mm_tn(gt[group, :, 0:conds], weight_low)

    def update(values, rate, grad):
        weight, first, second = values
        return adam_update(weight, grad, first, second, rate)

    tile = 96 if columns % 96 == 0 else columns
    saves = []

    def ada_group(group):
        for kind in (1, 2):
            ada_copy(kind, group).wait()

        def ada_tile(index, carry):
            rows = pl.ds(pl.multiple_of(index * tile, 8), tile)
            grad = mm(gt[group, rows, :], act_rows[...])
            new = update([ref[group, rows, :] for ref in ada], RATES[4], grad)
            for ref, value in zip(ada, new, strict=True):
                ref[group, rows, :] = value
            return carry

        lax.fori_loop(0, columns // tile, ada_tile, 0)
        for kind in range(3):
            copy = pltpu.make_async_copy(ada[kind].at[group], ada_out[kind].at[group], ada_save.at[kind, group])
            copy.start()
            saves.append(copy)

    for group in range(6):
        ada_group(group)

    pack = packs[0]
    for row in range(1, dp_count):
        pack = pack + packs[row]
    for part_index in range(3):
        head_grad[part_index:part_index + 1, :] = pack[0:1, part_index * columns:(part_index + 1) * columns]
    smalls = (
        ((head_w, head_m, head_v), RATES[5], head_grad[...]),
        ((hidden_w, hidden_m, hidden_v), RATES[6], pack[1:2, 0:hidden].reshape(hidden_w.shape)),
        ((shared_w, shared_m, shared_v), RATES[7], pack[2:4, 0:width]),
    )
    for index, (kinds, rate, grad) in enumerate(smalls):
        for kind, value in enumerate(update([ref[...] for ref in kinds], rate, grad)):
            small_out[index * 3 + kind][...] = value

    for index in range(4):
        for copy in big_loads[index]:
            copy.wait()
        weight, first, second, grad, low = big[index]
        planes = weight.shape[0] if len(weight.shape) == 3 else 0
        for plane in range(max(planes, 1)):
            where = (plane,) if planes else (slice(0, weight.shape[0]),)
            lanes = weight.shape[-1]
            gradient = grad[0, :, plane * lanes:(plane + 1) * lanes].astype(FLOAT)
            for source in range(1, grad.shape[0]):
                gradient = gradient + grad[source, :, plane * lanes:(plane + 1) * lanes].astype(FLOAT)
            gradient = gradient[0:weight.shape[-2], :]
            new = update([ref[where] for ref in (weight, first, second)], RATES[index], gradient)
            for ref, value in zip((weight, first, second), new, strict=True):
                ref[where] = value
            low[where] = new[0].astype(HALF)
        for kind, ref in enumerate((weight, first, second, low)):
            copy = pltpu.make_async_copy(ref, big_out[index][kind], big_save.at[index, kind])
            copy.start()
            saves.append(copy)

    for copy in saves:
        copy.wait()


def run_update(sizes, conditions, mods, packs, picks, smalls, bigs, ada):
    width, columns, segs = sizes["width"], sizes["columns"], sizes["segs"]
    conds = conditions.shape[0]
    vmem, dma = pltpu.VMEM, pltpu.SemaphoreType.DMA
    flat_small = [array for kinds in smalls for array in kinds]
    flat_big = [array for kinds in bigs for array in kinds]

    def like(array, dtype=FLOAT):
        return jax.ShapeDtypeStruct(array.shape, dtype)

    outs = [like(conditions)] + [like(a) for a in flat_small] + [like(a) for a in ada]
    for weight, first, second, grad in bigs:
        outs += [like(weight), like(first), like(second), like(weight, HALF)]
    scratch = [vmem(array.shape, FLOAT) for array in ada]
    for kinds in bigs:
        scratch += [vmem(array.shape, array.dtype) for array in kinds] + [vmem(kinds[0].shape, HALF)]
    scratch += [
        vmem((6, columns, 3 * conds), HALF), vmem((3 * conds, width), HALF), vmem((9, columns), FLOAT),
        dma((3, 6)), dma((3, 6)), dma((4, 4)), dma((4, 4)),
    ]
    return pl.pallas_call(
        functools.partial(update_kernel, sizes),
        out_shape=outs,
        in_specs=[vmem_spec()] * 13 + [any_spec()] * 19,
        out_specs=[vmem_spec()] * 10 + [any_spec()] * 19,
        scratch_shapes=scratch,
        name="update",
        compiler_params=pltpu.CompilerParams(vmem_limit_bytes=VMEM_BYTES),
    )(conditions, mods, packs, picks, *flat_small, *flat_big, *ada)


def cond_kernel(sizes, cond_ref, part_in, cond_out, part, landing, result, out_send, out_recv, back_send, back_recv):
    at = Place(sizes[DP], sizes[TP])
    slice_rows = cond_ref.shape[0] // at.tensor_count
    part[...] = part_in[...]
    greet([at.tensor_peer(s) for s in range(1, at.tensor_count)])

    def slice_at(index):
        return pl.ds(pl.multiple_of(index * slice_rows, 8), slice_rows)

    def out_copy(step):
        to = lax.rem(at.tensor + step, at.tensor_count)
        return remote(
            part.at[slice_at(to)], landing.at[step - 1], out_send.at[step - 1], out_recv.at[step - 1],
            at.tensor_peer(step),
        )

    def back_copy(step, owner):
        rows = result.at[slice_at(owner)]
        return remote(rows, rows, back_send.at[step - 1], back_recv.at[step - 1], at.tensor_peer(step))

    for step in range(1, at.tensor_count):
        out_copy(step).start()

    total = part[slice_at(at.tensor), :]
    for step in range(1, at.tensor_count):
        out_copy(step).wait_recv()
        total = total + landing[step - 1]
    own = cond_ref[slice_at(at.tensor), :]
    gate = 1.0 / (1.0 + jnp.exp(-own))
    result[slice_at(at.tensor), :] = total * (gate * (1.0 + own * (1.0 - gate)))
    for step in range(1, at.tensor_count):
        back_copy(step, at.tensor).start()
    for step in range(1, at.tensor_count):
        back_copy(step, lax.rem(at.tensor + at.tensor_count - step, at.tensor_count)).wait_recv()
    cond_out[...] = result[...]
    for step in range(1, at.tensor_count):
        out_copy(step).wait_send()
        back_copy(step, at.tensor).wait_send()


def run_cond(sizes, conditions, part):
    tensor_count, vmem, dma = sizes[TP], pltpu.VMEM, pltpu.SemaphoreType.DMA
    shape = conditions.shape
    return pl.pallas_call(
        functools.partial(cond_kernel, sizes),
        out_shape=jax.ShapeDtypeStruct(shape, FLOAT),
        in_specs=[vmem_spec()] * 2,
        out_specs=vmem_spec(),
        scratch_shapes=[
            vmem(shape, FLOAT), vmem((tensor_count - 1, shape[0] // tensor_count, shape[1]), FLOAT),
            vmem(shape, FLOAT), *[dma((tensor_count - 1,))] * 4,
        ],
        name="cond",
        compiler_params=pltpu.CompilerParams(collective_id=3, has_side_effects=True),
    )(conditions, part)


def on_device_kernels(
    block_input, conditions, segment_ids, segment_cond, cotangent, qkv_weight, proj_weight, inner_weight,
    outer_weight, ada_weight, head_biases, inner_bias, shared_biases, *moments,
):
    firsts, seconds = moments[:8], moments[8:]
    sizes = sizes_of(block_input, conditions, segment_ids, segment_cond, qkv_weight, inner_weight)
    seg_col = segment_ids.reshape(-1, 1)

    def planes(array):
        return array.transpose(1, 0, 2)

    kept = run_forward(
        sizes, block_input, seg_col, segment_ids, segment_cond, conditions, ada_weight, head_biases, inner_bias,
        shared_biases, planes(qkv_weight), proj_weight, inner_weight, outer_weight,
    )
    block_out, input_out, *grads, mods, packs, picks = run_backward(
        sizes, block_input, seg_col, segment_ids, segment_cond, shared_biases, cotangent, kept
    )
    weights = (qkv_weight, proj_weight, inner_weight, outer_weight)
    bigs = [[w, m, v, g] for w, m, v, g in zip(weights, firsts[:4], seconds[:4], grads, strict=True)]
    bigs[0][:3] = [planes(array) for array in bigs[0][:3]]
    smalls = list(zip((head_biases, inner_bias, shared_biases), firsts[5:], seconds[5:], strict=True))
    cond_part, *news = run_update(
        sizes, conditions, mods, packs, picks, smalls, bigs, (ada_weight, firsts[4], seconds[4])
    )
    small_new, ada_new, big_new = news[:9], news[9:12], news[12:]
    big_new[:4] = [planes(array) for array in big_new[:4]]
    outs = [block_out, input_out, run_cond(sizes, conditions, cond_part)]
    for kind in range(3):
        outs += [big_new[4 * i + kind] for i in range(4)]
        outs += [ada_new[kind]] + [small_new[3 * i + kind] for i in range(3)]
    return (*outs, *big_new[3::4])


def on_device(*args):
    sizes = sizes_of(args[0], args[1], args[2], args[3], args[5], args[7])
    return (on_device_kernels if kernels_fit(sizes) else on_device_general)(*args)


def solution(mesh):
    in_specs = (
        P(DP, None),
        P(),
        P(DP, None),
        P(DP, None),
        P(DP, None),
        P(DP, None, TP),
        P((TP, DP), None),
        P(DP, TP),
        P((TP, DP), None),
        P(None, TP, None),
        P(None, TP),
        P(TP),
        P(),
        P(DP, None, TP),
        P((TP, DP), None),
        P(DP, TP),
        P((TP, DP), None),
        P(None, TP, None),
        P(None, TP),
        P(TP),
        P(),
        P(DP, None, TP),
        P((TP, DP), None),
        P(DP, TP),
        P((TP, DP), None),
        P(None, TP, None),
        P(None, TP),
        P(TP),
        P(),
    )
    out_specs = (
        P((DP, TP), None),
        P((DP, TP), None),
        P(),
        P(DP, None, TP),
        P((TP, DP), None),
        P(DP, TP),
        P((TP, DP), None),
        P(None, TP, None),
        P(None, TP),
        P(TP),
        P(),
        P(DP, None, TP),
        P((TP, DP), None),
        P(DP, TP),
        P((TP, DP), None),
        P(None, TP, None),
        P(None, TP),
        P(TP),
        P(),
        P(DP, None, TP),
        P((TP, DP), None),
        P(DP, TP),
        P((TP, DP), None),
        P(None, TP, None),
        P(None, TP),
        P(TP),
        P(),
        P(DP, None, TP),
        P((TP, DP), None),
        P(DP, TP),
        P((TP, DP), None),
    )
    return jax.shard_map(
        on_device, mesh=mesh, in_specs=in_specs, out_specs=out_specs, check_vma=False
    )
```

```python
import functools
import math

import jax
import jax.numpy as jnp
import numpy as np
from jax import lax
from jax.experimental import pallas as pl
from jax.experimental.pallas import tpu as pltpu
from jax.sharding import PartitionSpec as P

HD = 72
STEP = 10


BETA_ONE = 0.5
BETA_TWO = 0.6
ADAM_EPS = 1e-08
DECAY = 0.01
NORM_EPSILON = 1e-06
RATES = (0.04, 0.3, 0.04, 0.04, 0.04, 0.4, 0.4, 0.4)
PRECISION_MAX = lax.Precision.HIGHEST
FLOAT = jnp.float32
HALF = jnp.bfloat16
DP, TP = "dp", "tensor"


def silu(values):
    return values / (1.0 + jnp.exp(-values))


def gelu_tanh(values):
    inner = math.sqrt(2.0 / math.pi) * (values + 0.044715 * values * values * values)
    return 0.5 * values * (1.0 + jnp.tanh(inner))


def normalize(values):
    centered = values - jnp.mean(values, axis=-1, keepdims=True)
    inv_std = lax.rsqrt(jnp.mean(centered * centered, axis=-1, keepdims=True) + NORM_EPSILON)
    return (centered * inv_std, inv_std)


def norm_back(grad_normed, normed, inv_std):
    first_mean = jnp.mean(grad_normed, axis=-1, keepdims=True)
    second_mean = jnp.mean(grad_normed * normed, axis=-1, keepdims=True)
    return inv_std * (grad_normed - first_mean - normed * second_mean)


def block_scores(query_block, keys, query_segs, key_segs):
    scores = jnp.einsum("qhe,khe->hqk", query_block, keys, preferred_element_type=FLOAT) * (
        1.0 / math.sqrt(HD)
    )
    same = query_segs[:, None] == key_segs[None, :]
    return jnp.where(same[None], scores, -1e30)


def attend_forward(row_qkv, row_segs):
    queries = row_qkv[:, 0]
    keys = row_qkv[:, 1]
    values = row_qkv[:, 2]
    length = queries.shape[0]
    heads_local = queries.shape[1]
    block = min(512, length)
    blocks = length // block

    def one_block(pieces):
        query_block, query_segs = pieces
        scores = block_scores(query_block, keys, query_segs, row_segs)
        top = jnp.max(scores, axis=-1, keepdims=True)
        expo = jnp.exp(scores - top)
        total = jnp.sum(expo, axis=-1, keepdims=True)
        probs = (expo / total).astype(HALF)
        attended = jnp.einsum("hqk,khe->qhe", probs, values, preferred_element_type=FLOAT)
        return (attended, (top + jnp.log(total))[:, :, 0])

    attended, log_totals = lax.map(
        one_block,
        (queries.reshape(blocks, block, heads_local, HD), row_segs.reshape(blocks, block)),
    )
    return (attended.reshape(length, heads_local, HD), log_totals)


def attend_backward(row_qkv, row_segs, grad_row, log_totals):
    queries = row_qkv[:, 0]
    keys = row_qkv[:, 1]
    values = row_qkv[:, 2]
    length = queries.shape[0]
    heads_local = queries.shape[1]
    block = min(512, length)
    blocks = length // block
    scale = 1.0 / math.sqrt(HD)

    def one_block(carry, pieces):
        key_sum, value_sum = carry
        query_block, query_segs, grad_block, block_total = pieces
        scores = block_scores(query_block, keys, query_segs, row_segs)
        probs = jnp.exp(scores - block_total[:, :, None])
        grad_probs = jnp.einsum("qhe,khe->hqk", grad_block, values, preferred_element_type=FLOAT)
        center = jnp.sum(probs * grad_probs, axis=-1, keepdims=True)
        grad_scores = (probs * (grad_probs - center)).astype(HALF)
        grad_query = (
            jnp.einsum("hqk,khe->qhe", grad_scores, keys, preferred_element_type=FLOAT) * scale
        )
        key_sum = (
            key_sum
            + jnp.einsum("hqk,qhe->khe", grad_scores, query_block, preferred_element_type=FLOAT)
            * scale
        )
        value_sum = value_sum + jnp.einsum(
            "hqk,qhe->khe", probs.astype(HALF), grad_block, preferred_element_type=FLOAT
        )
        return ((key_sum, value_sum), grad_query)

    zeros = jnp.zeros((length, heads_local, HD), FLOAT)
    sums, grad_queries = lax.scan(
        one_block,
        (zeros, zeros),
        (
            queries.reshape(blocks, block, heads_local, HD),
            row_segs.reshape(blocks, block),
            grad_row.reshape(blocks, block, heads_local, HD),
            log_totals,
        ),
    )
    return jnp.stack([grad_queries.reshape(length, heads_local, HD), sums[0], sums[1]], axis=1)


def adam_update(weight, grad, first, second, rate):
    first_new = BETA_ONE * first + (1.0 - BETA_ONE) * grad
    second_new = BETA_TWO * second + (1.0 - BETA_TWO) * grad * grad
    fix_one = 1.0 - BETA_ONE**STEP
    fix_two = 1.0 - BETA_TWO**STEP
    update = first_new / fix_one / (jnp.sqrt(second_new / fix_two) + ADAM_EPS)
    return (weight - rate * (update + DECAY * weight), first_new, second_new)


def sum_to_shares(partial):
    return lax.psum_scatter(
        partial.astype(HALF), TP, scatter_dimension=0, tiled=True
    ).astype(FLOAT)


def sum_to_owners(partial):
    return lax.psum_scatter(
        partial.astype(HALF), DP, scatter_dimension=0, tiled=True
    ).astype(FLOAT)


SEG_MOST = 256
CORES = 2
MESH = pl.DeviceIdType.MESH
NT_DIMS = (((1,), (1,)), ((), ()))
TN_DIMS = (((0,), (0,)), ((), ()))
VMEM_BYTES = 62 * 1024 * 1024


def line_length(count):
    length = 1
    while (2 * length) ** 2 <= count:
        length *= 2
    return length


def mm(left, right):
    return jnp.dot(left, right, preferred_element_type=FLOAT)


def mm_nt(left, right):
    return lax.dot_general(left, right, NT_DIMS, preferred_element_type=FLOAT)


def mm_tn(left, right):
    return lax.dot_general(left, right, TN_DIMS, preferred_element_type=FLOAT)


def split_two(values):
    high = values.astype(HALF)
    return high, (values - high.astype(FLOAT)).astype(HALF)


def cond_picks(seg_cond, conds):
    return (lax.broadcasted_iota(jnp.int32, (conds, 1), 0) == seg_cond[...]).astype(FLOAT).astype(HALF)


def pick_rows(picks, values):
    high, rest = split_two(values)
    middle, low = split_two(values - high.astype(FLOAT))
    return mm_tn(picks, high) + mm_tn(picks, middle) + mm_tn(picks, low)


class Place:
    def __init__(self, dp_count, tensor_count):
        self.dp_count, self.tensor_count = dp_count, tensor_count
        self.xs = line_length(dp_count)
        self.zs = dp_count // self.xs
        self.ys = tensor_count // CORES
        self.dp, self.tensor = lax.axis_index(DP), lax.axis_index(TP)
        self.z, self.x = lax.div(self.dp, self.xs), lax.rem(self.dp, self.xs)
        self.y, self.core = lax.div(self.tensor, CORES), lax.rem(self.tensor, CORES)

    def z_of(self, step):
        return lax.rem(self.z + step + self.zs, self.zs)

    def x_of(self, step):
        return lax.rem(self.x + step + self.xs, self.xs)

    def z_peer(self, step):
        return (self.z_of(step) * self.xs + self.x, self.tensor)

    def x_peer(self, step):
        return (self.z * self.xs + self.x_of(step), self.tensor)

    def tensor_peer(self, step):
        return (self.dp, lax.rem(self.tensor + step, self.tensor_count))

    def core_peer(self):
        return (self.dp, self.y * CORES + 1 - self.core)

    def y_peer(self):
        return (self.dp, (1 - self.y) * CORES + self.core)

    def share_of(self, other_y, other_core):
        y = 1 - self.y if other_y else self.y
        core = 1 - self.core if other_core else self.core
        return y * CORES + core


def greet(peers):
    barrier = pltpu.get_barrier_semaphore()
    for peer in peers:
        pl.semaphore_signal(barrier, inc=1, device_id=peer, device_id_type=MESH)
    pl.semaphore_wait(barrier, len(peers))


def remote(src, dst, sends, recvs, peer):
    return pltpu.make_async_remote_copy(
        src_ref=src, dst_ref=dst, send_sem=sends, recv_sem=recvs, device_id=peer, device_id_type=MESH
    )


def rows_at(start, count):
    return pl.ds(pl.multiple_of(start, 16), count)


AHEAD = 2


def unit_rows(shard, most=48):
    return most if shard % most == 0 else shard


FIRST_UNIT, LAST_UNIT = 48, 48


class Gather:
    def __init__(self, place, pieces, z_sems, x_sems):
        self.place, self.pieces = place, pieces
        self.z_send, self.z_recv = z_sems
        self.x_send, self.x_recv = x_sems
        self.hops = place.zs - 1
        self.ticks = 0

    def slot(self, piece, z, x):
        full, shard, first, count = self.pieces[piece]
        return full.at[rows_at((z * self.place.xs + x) * shard + first, count)]

    def hop(self, piece, source, step, sem):
        at = self.place
        chunk = self.slot(piece, source, at.x)
        return remote(chunk, chunk, self.z_send.at[piece, sem], self.z_recv.at[piece, sem], at.z_peer(step))

    def x_copy(self, piece, source, step):
        at = self.place
        chunk = self.slot(piece, source, at.x)
        sems = self.x_send.at[piece, source, step - 1], self.x_recv.at[piece, source, step - 1]
        return remote(chunk, chunk, *sems, at.x_peer(step))

    def x_landing(self, piece, source, step):
        at = self.place
        chunk = self.slot(piece, source, at.x_of(-step))
        sems = self.x_send.at[piece, source, step - 1], self.x_recv.at[piece, source, step - 1]
        return remote(chunk, chunk, *sems, at.x_peer(step))

    def along_x(self, piece, source):
        for step in range(1, self.place.xs):
            self.x_copy(piece, source, step).start()

    def start(self, piece):
        at = self.place

        @pl.when(at.z < at.zs - 1)
        def _():
            self.hop(piece, at.z, 1, 0).start()

        @pl.when(at.z > 0)
        def _():
            self.hop(piece, at.z, -1, self.hops).start()

        self.along_x(piece, at.z)

    def pass_on(self, piece, away):
        at, hops = self.place, self.hops

        @pl.when(at.z >= away)
        def _():
            self.hop(piece, at.z - away, 1, away - 1).wait_recv()
            if away < hops:
                @pl.when(at.z < at.zs - 1)
                def _():
                    self.hop(piece, at.z - away, 1, away).start()
            self.along_x(piece, at.z - away)

        @pl.when(at.z + away < at.zs)
        def _():
            self.hop(piece, at.z + away, -1, hops + away - 1).wait_recv()
            if away < hops:
                @pl.when(at.z > 0)
                def _():
                    self.hop(piece, at.z + away, -1, hops + away).start()
            self.along_x(piece, at.z + away)

    def tick(self):
        now = self.ticks
        for away in range(self.hops, 0, -1):
            if 0 <= now - away + 1 < len(self.pieces):
                self.pass_on(now - away + 1, away)
        if now + AHEAD < len(self.pieces):
            self.start(now + AHEAD)
        self.ticks += 1

    def tick_until(self, piece):
        while self.ticks < min(piece, len(self.pieces) - 1) + self.hops:
            self.tick()

    def arrive(self, piece):
        at = self.place
        for source in range(at.zs):
            for step in range(1, at.xs):
                self.x_landing(piece, source, step).wait_recv()

    def finish(self, piece):
        at, hops = self.place, self.hops
        for away in range(hops):
            @pl.when((at.z >= away) & (at.z < at.zs - 1))
            def _(away=away):
                self.hop(piece, at.z - away, 1, away).wait_send()

            @pl.when((at.z + away < at.zs) & (at.z > 0))
            def _(away=away):
                self.hop(piece, at.z + away, -1, hops + away).wait_send()
        for source in range(at.zs):
            for step in range(1, at.xs):
                self.x_copy(piece, source, step).wait_send()


def layer_norm(values):
    mean = jnp.mean(values, axis=-1, keepdims=True)
    centered = values - mean
    inv_std = lax.rsqrt(jnp.mean(centered * centered, axis=-1, keepdims=True) + NORM_EPSILON)
    return centered * inv_std, inv_std


def forward_kernel(
    sizes,
    x_ref, seg_col, seg_row, seg_cond, cond_ref, ada_ref, head_bias, inner_bias, shared_bias,
    proj_place, wq_raw, wp_raw, wi_raw, wo_raw,
    wq_out, wp_out, wi_out, wo_out, hid_a_out, heads_out, lse_out, att_out, hid_b_out, act_out,
    slope_out, far_out, own_out, branch_out, middle_out, modk_out,
    wq_full, wp_full, wp_tight, wi_full, wo_full, hid_a, heads, lse, lse_heads, att_heads, att, part, core_in,
    y_out, y_in, hid_b, act, slope, ff_part, ff_in, ff_far, ff_own, branch, middle, modk, mods, ada_tile,
    wp_wide,
    z_send, z_recv, x_send, x_recv, mod_send, mod_recv, sum_send, sum_recv, gat_send, gat_recv, ff_send, ff_recv,
    ada_sem, save_sem,
):
    at = Place(sizes[DP], sizes[TP])
    tokens, width, columns, share = sizes["tokens"], sizes["width"], sizes["columns"], sizes["share"]
    nheads, segs = columns // HD, seg_cond.shape[1]
    window = min(tokens, share + 2 * SEG_MOST)
    greet(
        [at.z_peer(s) for s in range(1, at.zs)]
        + [at.x_peer(s) for s in range(1, at.xs)]
        + [at.tensor_peer(s) for s in range(1, at.tensor_count)]
    )
    pieces, lists = [], []
    for full, shard in (
        (wq_full, wq_raw.shape[1]), (wp_full, wp_wide.shape[0]), (wi_full, wi_raw.shape[0]), (wo_full, wo_raw.shape[0])
    ):
        unit = unit_rows(shard, 48 if lists else FIRST_UNIT)
        lists.append(list(range(len(pieces), len(pieces) + shard // unit)))
        pieces += [(full, shard, first, unit) for first in range(0, shard, unit)]
    list_q, list_p, list_i, list_o = lists
    gather = Gather(at, pieces, (z_send, z_recv), (x_send, x_recv))
    last = len(pieces)

    def own_rows_of(full, shard):
        return rows_at(at.dp * shard, shard)

    wq_full[own_rows_of(wq_full, wq_raw.shape[1]), :] = jnp.concatenate(
        [wq_raw[part_index] for part_index in range(3)], axis=1
    ).astype(HALF)
    for piece in list_q[:AHEAD]:
        gather.start(piece)
    wp_wide[...] = jnp.zeros_like(wp_wide)
    wp_wide[0:wp_raw.shape[0], :] = wp_raw[...]
    for raw, full in ((wp_wide, wp_full), (wi_raw, wi_full), (wo_raw, wo_full)):
        full[own_rows_of(full, raw.shape[0]), :] = raw[...].astype(HALF)
    for piece in range(len(list_q[:AHEAD]), AHEAD):
        gather.start(piece)

    def ada_copy(group):
        return pltpu.make_async_copy(ada_ref.at[group], ada_tile.at[group % 2], ada_sem.at[group % 2])

    ada_copy(0).start()
    cond_high, cond_low = split_two(silu(pick_rows(cond_picks(seg_cond, cond_ref.shape[0]), cond_ref[...])))
    cond_both = jnp.concatenate([cond_high, cond_low], axis=0)
    for group in range(6):
        if group in (2, 4):
            gather.tick()
        if group < 5:
            ada_copy(group + 1).start()
        ada_copy(group).wait()
        weight_high, weight_low = split_two(ada_tile[group % 2])
        both = mm_nt(cond_both, weight_high)
        mods[at.tensor, group] = (
            both[:segs] + both[segs:] + mm_nt(cond_high, weight_low)
            + head_bias[3 + group:4 + group, :]
        )

    def mod_copy(step):
        own = mods.at[at.tensor]
        return remote(own, own, mod_send.at[step - 1], mod_recv.at[step - 1], at.tensor_peer(step))

    def mod_landing(step):
        landed = mods.at[lax.rem(at.tensor + at.tensor_count - step, at.tensor_count)]
        return remote(landed, landed, mod_send.at[step - 1], mod_recv.at[step - 1], at.tensor_peer(step))

    for step in range(1, at.tensor_count):
        mod_copy(step).start()
    gather.tick()
    for step in range(1, at.tensor_count):
        mod_landing(step).wait_recv()
    for group in range(6):
        whole = jnp.concatenate([mods[t, group] for t in range(at.tensor_count)], axis=1)
        high, low = split_two(whole)
        modk[group] = jnp.concatenate([high, low], axis=0)

    def pick(rows):
        ids = seg_col[rows, :]
        lanes = lax.broadcasted_iota(jnp.int32, (1, 2 * segs), 1)
        return (ids == lax.rem(lanes, segs)).astype(FLOAT).astype(HALF)

    gather.tick()

    def hidden_block(index, carry):
        rows = rows_at(index * share, share)
        normed, _ = layer_norm(x_ref[rows, :].astype(FLOAT))
        chosen = pick(rows)
        hid_a[rows, :] = (normed * (1.0 + mm(chosen, modk[1])) + mm(chosen, modk[0])).astype(HALF)
        return carry

    lax.fori_loop(0, tokens // share // 2, hidden_block, 0)
    gather.tick_until(list_q[-1] // 2)
    lax.fori_loop(tokens // share // 2, tokens // share, hidden_block, 0)
    gather.tick_until(list_q[-1])
    for piece in list_q:
        gather.arrive(piece)

    qkv_bias = jnp.concatenate([head_bias[i:i + 1, :] for i in range(3)], axis=1)

    def qkv_block(index, carry):
        rows = rows_at(index * share, share)
        values = mm(hid_a[rows, :], wq_full[...]) + qkv_bias
        for head in range(3 * nheads):
            heads[head, rows, :] = values[:, head * HD:(head + 1) * HD].astype(HALF)
        return carry

    lax.fori_loop(0, tokens // share, qkv_block, 0)

    def attend(block):
        start = block * share
        rows = rows_at(start, share)
        first = pl.multiple_of(jnp.clip(start - SEG_MOST, 0, tokens - window), 128)
        keys = pl.ds(first, window)

        def one_head(head, carry):
            same = seg_col[rows, :] == seg_row[:, keys]
            scores = mm_nt(heads[head, rows, :], heads[nheads + head, keys, :]) * (1.0 / math.sqrt(HD))
            scores = jnp.where(same, scores, -1e30)
            top = jnp.max(scores, axis=-1, keepdims=True)
            expo = jnp.exp(scores - top)
            total = jnp.sum(expo, axis=-1, keepdims=True)
            probs = (expo * (1.0 / total)).astype(HALF)
            att_heads[head, :, :] = mm(probs, heads[2 * nheads + head, keys, :])
            lse_heads[head] = top + jnp.log(total)
            return carry

        lax.fori_loop(0, nheads, one_head, 0)
        joined = jnp.concatenate([att_heads[head] for head in range(nheads)], axis=1).astype(HALF)
        att[rows, :] = joined
        lse[rows, :] = jnp.concatenate([lse_heads[head] for head in range(nheads)], axis=1)
        return joined

    def core_copy(slot, src):
        return remote(src, core_in.at[slot], sum_send.at[slot], sum_recv.at[slot], at.core_peer())

    y_copy = remote(y_out, y_in, sum_send.at[2], sum_recv.at[2], at.y_peer())

    gather.tick_until(list_p[0])
    joined = attend(at.share_of(True, True))
    gather.arrive(list_p[0])
    wp_tight[...] = mm(proj_place[...], wp_full[...]).astype(HALF)
    part[0] = mm(joined, wp_tight[...]).astype(HALF)
    core_copy(0, part.at[0]).start()
    joined = attend(at.share_of(False, True))
    part[1] = mm(joined, wp_tight[...]).astype(HALF)
    core_copy(1, part.at[1]).start()
    gather.tick_until(list_i[0])
    joined = attend(at.share_of(True, False))
    summed = mm(joined, wp_tight[...])
    core_copy(0, part.at[0]).wait_recv()
    y_out[...] = (summed + core_in[0].astype(FLOAT)).astype(HALF)
    y_copy.start()
    joined = attend(at.share_of(False, False))
    summed = mm(joined, wp_tight[...])
    core_copy(1, part.at[1]).wait_recv()
    summed = summed + core_in[1].astype(FLOAT)
    gather.tick_until(list_i[0] + 1)
    y_copy.wait_recv()
    branch[...] = summed + y_in[...].astype(FLOAT) + shared_bias[0:1, :]

    own_rows = rows_at(at.tensor * share, share)
    chosen = pick(own_rows)
    middle[...] = x_ref[own_rows, :].astype(FLOAT) + mm(chosen, modk[2]) * branch[...]
    normed, _ = layer_norm(middle[...])
    hid_b[own_rows, :] = (normed * (1.0 + mm(chosen, modk[4])) + mm(chosen, modk[3])).astype(HALF)

    def hid_rows(other_y, other_core):
        return hid_b.at[rows_at(at.share_of(other_y, other_core) * share, share)]

    own_hid = hid_rows(False, False)
    to_core = remote(own_hid, own_hid, gat_send.at[0], gat_recv.at[0], at.core_peer())
    to_y = remote(own_hid, own_hid, gat_send.at[1], gat_recv.at[1], at.y_peer())
    to_y.start()
    to_core.start()
    across = hid_rows(True, False)
    onward = remote(across, across, gat_send.at[2], gat_recv.at[2], at.core_peer())
    gather.tick_until(list_i[-1])
    gather.tick_until(list_o[0])
    remote(across, across, gat_send.at[1], gat_recv.at[1], at.y_peer()).wait_recv()
    onward.start()
    for piece in list_i:
        gather.arrive(piece)
    beside = hid_rows(False, True)
    remote(beside, beside, gat_send.at[0], gat_recv.at[0], at.core_peer()).wait_recv()
    far = hid_rows(True, True)
    remote(far, far, gat_send.at[2], gat_recv.at[2], at.core_peer()).wait_recv()

    def inner_block(index, carry):
        rows = rows_at(index * share, share)
        pre = mm(hid_b[rows, :], wi_full[...]) + inner_bias[...].reshape(1, -1)
        factor = math.sqrt(2.0 / math.pi)
        squared = pre * pre
        bend = jnp.tanh(factor * (pre + 0.044715 * squared * pre))
        act[rows, :] = (0.5 * pre * (1.0 + bend)).astype(HALF)
        slope[rows, :] = (
            0.5 * (1.0 + bend)
            + 0.5 * pre * (1.0 - bend * bend) * (factor * (1.0 + (3 * 0.044715) * squared))
        ).astype(HALF)
        return carry

    lax.fori_loop(0, tokens // share // 2, inner_block, 0)
    gather.tick_until(list_o[0] + 1)
    lax.fori_loop(tokens // share // 2, tokens // share, inner_block, 0)

    saves = []

    def save(src, dst):
        copy = pltpu.make_async_copy(src, dst, save_sem.at[len(saves)])
        copy.start()
        saves.append(copy)

    for src, dst in (
        (wq_full, wq_out), (wp_tight, wp_out), (wi_full, wi_out), (hid_a, hid_a_out), (heads, heads_out),
        (lse, lse_out), (att, att_out), (hid_b, hid_b_out), (act, act_out), (slope, slope_out),
        (branch, branch_out), (middle, middle_out), (modk, modk_out),
    ):
        save(src, dst)
    gather.tick_until(list_o[-1])
    for piece in list_o:
        gather.arrive(piece)
    save(wo_full, wo_out)

    def outer_block(other_y, other_core):
        rows = rows_at(at.share_of(other_y, other_core) * share, share)
        return mm(act[rows, :], wo_full[...])

    def ff_copy(slot):
        return remote(ff_part.at[slot], ff_in.at[slot], ff_send.at[slot], ff_recv.at[slot], at.core_peer())

    ff_part[0] = outer_block(True, True).astype(HALF)
    ff_copy(0).start()
    ff_part[1] = outer_block(False, True).astype(HALF)
    ff_copy(1).start()
    summed = outer_block(True, False)
    ff_copy(0).wait_recv()
    ff_far[...] = (summed + ff_in[0].astype(FLOAT)).astype(HALF)
    save(ff_far, far_out)
    summed = outer_block(False, False)
    ff_copy(1).wait_recv()
    ff_own[...] = summed + ff_in[1].astype(FLOAT)
    save(ff_own, own_out)
    ff_copy(0).wait_send()
    ff_copy(1).wait_send()

    for step in range(1, at.tensor_count):
        mod_copy(step).wait_send()
    core_copy(0, part.at[0]).wait_send()
    core_copy(1, part.at[1]).wait_send()
    y_copy.wait_send()
    to_core.wait_send()
    to_y.wait_send()
    onward.wait_send()
    for piece in range(last):
        gather.finish(piece)
    for copy in saves:
        copy.wait()


def any_spec():
    return pl.BlockSpec(memory_space=pl.ANY)


def vmem_spec():
    return pl.BlockSpec(memory_space=pltpu.VMEM)


def sizes_of(block_input, conditions, segment_ids, segment_cond, qkv_weight, inner_weight):
    dp_count, tensor_count = lax.axis_size(DP), lax.axis_size(TP)
    tokens, width = block_input.shape
    return {
        DP: dp_count,
        TP: tensor_count,
        "tokens": tokens,
        "rows": segment_ids.shape[0],
        "width": width,
        "columns": qkv_weight.shape[2],
        "hidden": inner_weight.shape[1],
        "shard": qkv_weight.shape[0],
        "share": tokens // tensor_count,
        "segs": segment_cond.shape[1],
        "conds": conditions.shape[0],
    }


def kernels_fit(sizes):
    return (
        sizes[TP] == 2 * CORES
        and sizes["rows"] == 1
        and sizes["share"] % 128 == 0
        and sizes["width"] % 128 == 0
        and sizes["hidden"] % 128 == 0
        and sizes["shard"] % 16 == 0
        and sizes["columns"] % 32 == 0
        and sizes["conds"] % (8 * sizes[TP]) == 0
    )


def placing(columns, own_rows, pad_rows, dp_count):
    tight = np.arange(columns)
    place = (tight // own_rows * pad_rows + tight % own_rows)[:, None] == np.arange(dp_count * pad_rows)
    return place.astype(np.float32)


def run_forward(sizes, block_input, seg_col, segment_ids, segment_cond, conditions, ada_weight, head_biases,
                inner_bias, shared_biases, wq, wp, wi, wo):
    tokens, width, columns, share = (sizes[k] for k in ("tokens", "width", "columns", "share"))
    hidden, dp_count, tensor_count = sizes["hidden"], sizes[DP], sizes[TP]
    nheads, segs = columns // HD, sizes["segs"]
    own_rows = columns // dp_count
    pad_rows = own_rows + -own_rows % 16
    shards = (sizes["shard"], pad_rows, sizes["shard"], hidden // dp_count)
    xs = line_length(dp_count)
    zs = dp_count // xs
    units = shards[0] // unit_rows(shards[0], FIRST_UNIT) + sum(shard // unit_rows(shard) for shard in shards[1:])
    place = jnp.asarray(placing(columns, own_rows, pad_rows, dp_count), HALF)
    shapes = [
        ((width, 3 * columns), HALF), ((columns, width), HALF), ((width, hidden), HALF),
        ((hidden, width), HALF), ((tokens, width), HALF), ((3 * nheads, tokens, HD), HALF),
        ((tokens, nheads), FLOAT), ((tokens, columns), HALF), ((tokens, width), HALF),
        ((tokens, hidden), HALF), ((tokens, hidden), HALF), ((share, width), HALF), ((share, width), FLOAT),
        ((share, width), FLOAT), ((share, width), FLOAT), ((6, 2 * segs, width), HALF),
    ]
    vmem = pltpu.VMEM
    dma = pltpu.SemaphoreType.DMA
    scratch = [
        vmem((width, 3 * columns), HALF), vmem((dp_count * pad_rows, width), HALF),
        vmem((columns, width), HALF), vmem((width, hidden), HALF), vmem((hidden, width), HALF),
        vmem((tokens, width), HALF), vmem((3 * nheads, tokens, HD), HALF),
        vmem((tokens, nheads), FLOAT), vmem((nheads, share, 1), FLOAT), vmem((nheads, share, HD), FLOAT),
        vmem((tokens, columns), HALF), vmem((2, share, width), HALF), vmem((2, share, width), HALF),
        vmem((share, width), HALF), vmem((share, width), HALF), vmem((tokens, width), HALF),
        vmem((tokens, hidden), HALF), vmem((tokens, hidden), HALF), vmem((2, share, width), HALF),
        vmem((2, share, width), HALF), vmem((share, width), HALF), vmem((share, width), FLOAT),
        vmem((share, width), FLOAT), vmem((share, width), FLOAT), vmem((6, 2 * segs, width), HALF),
        vmem((tensor_count, 6, segs, columns), FLOAT), vmem((2, columns, width), FLOAT),
        vmem((pad_rows, width), FLOAT),
        dma((units, 2 * (zs - 1))), dma((units, 2 * (zs - 1))), dma((units, zs, xs - 1)),
        dma((units, zs, xs - 1)),
        dma((tensor_count - 1,)), dma((tensor_count - 1,)), dma((3,)), dma((3,)), dma((3,)), dma((3,)), dma((2,)), dma((2,)),
        dma((2,)), dma((16,)),
    ]
    return pl.pallas_call(
        functools.partial(forward_kernel, sizes),
        out_shape=[jax.ShapeDtypeStruct(s, t) for s, t in shapes],
        in_specs=[vmem_spec()] * 5 + [any_spec()] + [vmem_spec()] * 8,
        out_specs=[any_spec()] * len(shapes),
        scratch_shapes=scratch,
        name="forward",
        compiler_params=pltpu.CompilerParams(
            collective_id=1, has_side_effects=True, vmem_limit_bytes=VMEM_BYTES
        ),
    )(
        block_input, seg_col, segment_ids, segment_cond, conditions, ada_weight, head_biases, inner_bias,
        shared_biases, place, wq, wp, wi, wo,
    )


class Scatter:
    def __init__(self, place, pieces, x_sems, z_sems):
        self.place, self.pieces = place, pieces
        self.x_send, self.x_recv = x_sems
        self.z_send, self.z_recv = z_sems

    def slot(self, piece, z, x):
        whole, x_in, z_in, shard, first, count = self.pieces[piece]
        return whole.at[rows_at((z * self.place.xs + x) * shard + first, count)]

    def x_copy(self, piece, step, z):
        at = self.place
        whole, x_in, z_in, shard, first, count = self.pieces[piece]
        return remote(
            self.slot(piece, z, at.x_of(step)), x_in.at[step - 1, z, pl.ds(first, count)],
            self.x_send.at[piece, step - 1, z], self.x_recv.at[piece, step - 1, z], at.x_peer(step),
        )

    def z_copy(self, piece, step):
        at = self.place
        whole, x_in, z_in, shard, first, count = self.pieces[piece]
        return remote(
            self.slot(piece, at.z_of(step), at.x), z_in.at[step - 1, pl.ds(first, count)],
            self.z_send.at[piece, step - 1], self.z_recv.at[piece, step - 1], at.z_peer(step),
        )

    def start(self, piece):
        at = self.place
        for step in range(1, at.xs):
            for z in range(at.zs):
                self.x_copy(piece, step, z).start()

    def pass_on(self, piece):
        at = self.place
        whole, x_in, z_in, shard, first, count = self.pieces[piece]
        for z in range(at.zs):
            rows = rows_at((z * at.xs + at.x) * shard + first, count)
            total = whole[rows, :].astype(FLOAT)
            for step in range(1, at.xs):
                self.x_copy(piece, step, z).wait_recv()
                total = total + x_in[step - 1, z, first:first + count, :].astype(FLOAT)
            whole[rows, :] = total.astype(HALF)
        for step in sorted(range(1, at.zs), key=lambda s: -min(s, at.zs - s)):
            self.z_copy(piece, step).start()

    def arrive(self, piece):
        for step in range(1, self.place.zs):
            self.z_copy(piece, step).wait_recv()

    def finish(self, piece):
        at = self.place
        for step in range(1, at.xs):
            for z in range(at.zs):
                self.x_copy(piece, step, z).wait_send()
        for step in range(1, at.zs):
            self.z_copy(piece, step).wait_send()


class Spread:
    def __init__(self, place, chunks, z_sems, x_sems):
        self.place, self.chunks = place, chunks
        self.z_send, self.z_recv = z_sems
        self.x_send, self.x_recv = x_sems

    def z_copy(self, part, step, source):
        at = self.place
        chunk = self.chunks[part](self.place.z_of(source) * at.xs + at.x)
        return remote(chunk, chunk, self.z_send.at[part, step - 1], self.z_recv.at[part, step - 1], at.z_peer(step))

    def x_copy(self, part, back, step, source):
        at = self.place
        chunk = self.chunks[part](at.z_of(-back) * at.xs + at.x_of(source))
        sems = self.x_send.at[part, back, step - 1], self.x_recv.at[part, back, step - 1]
        return remote(chunk, chunk, *sems, at.x_peer(step))

    def start(self, part):
        for step in range(1, self.place.zs):
            self.z_copy(part, step, 0).start()

    def pass_on(self, part):
        for back in range(self.place.zs):
            if back > 0:
                self.z_copy(part, back, -back).wait_recv()
            for step in range(1, self.place.xs):
                self.x_copy(part, back, step, 0).start()

    def finish(self, part):
        at = self.place
        for step in range(1, at.zs):
            self.z_copy(part, step, 0).wait_send()
        for back in range(at.zs):
            for step in range(1, at.xs):
                self.x_copy(part, back, step, -step).wait_recv()
                self.x_copy(part, back, step, 0).wait_send()


def image_sums(chosen, values):
    high, low = split_two(values)
    return mm_tn(chosen, high) + mm_tn(chosen, low)


def backward_kernel(
    sizes,
    seg_col, seg_row, seg_cond, shared_bias, place_back,
    x_in, cot_in, wq_in, wp_in, wi_in, wo_in, hid_a_in, heads_in, lse_in, att_in, hid_b_in, act_in, slope_in,
    far_in, own_in, branch_in, middle_in, modk_in,
    block_out, input_out, qkv_out, proj_out, inner_out, outer_out, mods_out, packs_out, picks_out,
    wq, wp, wi, wo, heads, lse, att, hid_b, act, slope, cot, modk, branch, middle, ff_own,
    cot_own, x_own, gatt, key_sum, value_sum, grad_a, part, core_in, y_out, y_in, ff_in, grad_mid,
    whole_o, whole_i, whole_p, whole_q, xin_o, xin_i, xin_p, xin_q, zin_o, zin_i, zin_p, zin_q,
    mod_send_buf, mod_in, mods, packs, picks,
    load_sem, save_sem, x_send, x_recv, z_send, z_recv, sum_send, sum_recv, gat_send, gat_recv,
    ff_send, ff_recv, mod_send, mod_recv, all_z_send, all_z_recv, all_x_send, all_x_recv,
):
    at = Place(sizes[DP], sizes[TP])
    tokens, width, columns, share = sizes["tokens"], sizes["width"], sizes["columns"], sizes["share"]
    hidden = sizes["hidden"]
    nheads, segs = columns // HD, sizes["segs"]
    blocks = tokens // share
    scale = 1.0 / math.sqrt(HD)

    own_rows = rows_at(at.tensor * share, share)
    loads = {}

    def load(name, src, dst):
        copy = pltpu.make_async_copy(src, dst, load_sem.at[len(loads)])
        copy.start()
        loads[name] = copy

    load("cot", cot_in, cot)
    load("modk", modk_in, modk)
    load("act", act_in, act)
    load("wo", wo_in, wo)
    load("slope", slope_in, slope)
    load("wi", wi_in, wi)
    load("hid_b", hid_b_in, hid_b)
    load("middle", middle_in, middle)
    load("branch", branch_in, branch)
    load("ff_own", own_in, ff_own)
    load("att", att_in, att)
    load("wp", wp_in, wp)
    load("heads", heads_in, heads)
    load("lse", lse_in, lse)
    load("wq", wq_in, wq)
    load("x", x_in.at[own_rows], x_own)
    greet(
        [at.z_peer(s) for s in range(1, at.zs)]
        + [at.x_peer(s) for s in range(1, at.xs)]
        + [at.tensor_peer(s) for s in range(1, at.tensor_count)]
    )
    ff_copy = remote(far_in, ff_in, ff_send, ff_recv, at.y_peer())
    ff_copy.start()

    pieces = []
    for whole, x_in, z_in in (
        (whole_o, xin_o, zin_o), (whole_i, xin_i, zin_i), (whole_p, xin_p, zin_p), (whole_q, xin_q, zin_q)
    ):
        shard = x_in.shape[2]
        unit = unit_rows(shard, LAST_UNIT if whole is whole_q else 48)
        pieces.append([(whole, x_in, z_in, shard, first, unit) for first in range(0, shard, unit)])
    flat = [piece for group in pieces for piece in group]
    scatter = Scatter(at, flat, (x_send, x_recv), (z_send, z_recv))
    bounds = [sum(len(g) for g in pieces[:i]) for i in range(len(pieces) + 1)]
    list_o, list_i, list_p, list_q = (list(range(bounds[i], bounds[i + 1])) for i in range(4))

    def one_hot(rows, count):
        lanes = lax.broadcasted_iota(jnp.int32, (1, count), 1)
        return (seg_col[rows, :] == lax.rem(lanes, segs)).astype(FLOAT).astype(HALF)

    loads["cot"].wait()
    loads["modk"].wait()
    cot_own[...] = cot[own_rows, :]
    packs[at.dp] = jnp.zeros_like(packs[at.dp])
    picks[at.dp] = jnp.zeros_like(picks[at.dp])

    def grad_b_block(index, total):
        rows = rows_at(index * share, share)
        gate = mm(one_hot(rows, 2 * segs), modk[5])
        value = (cot[rows, :].astype(FLOAT) * gate).astype(HALF)
        cot[rows, :] = value
        return total + jnp.sum(value.astype(FLOAT), axis=0, keepdims=True)

    packs[at.dp, 3:4, 0:width] = lax.fori_loop(0, blocks, grad_b_block, jnp.zeros((1, width), FLOAT))
    loads["act"].wait()

    def lanes_at(index):
        return pl.ds(pl.multiple_of(index * 128, 128), 128)

    def outer_grad_block(index, carry):
        whole_o[rows_at(index * 128, 128), :] = mm_tn(act[:, lanes_at(index)], cot[...]).astype(HALF)
        return carry

    lax.fori_loop(0, hidden // 128, outer_grad_block, 0)
    for piece in list_o:
        scatter.start(piece)
    load("hid_a", hid_a_in, act)
    loads["wo"].wait()
    loads["slope"].wait()
    loads["wi"].wait()

    def back_two(block):
        rows = rows_at(block * share, share)
        grad_act = mm_nt(cot[rows, :], wo[...])
        grad_pre = (grad_act * slope[rows, :].astype(FLOAT)).astype(HALF)
        slope[rows, :] = grad_pre
        return mm_nt(grad_pre, wi[...]), jnp.sum(grad_pre.astype(FLOAT), axis=0, keepdims=True)

    def core_copy(slot):
        return remote(part.at[slot], core_in.at[slot], sum_send.at[slot], sum_recv.at[slot], at.core_peer())

    y_copy = remote(y_out, y_in, sum_send.at[2], sum_recv.at[2], at.y_peer())

    def sum_shares(make, between, held):
        part[0] = make(at.share_of(True, True)).astype(HALF)
        core_copy(0).start()
        part[1] = make(at.share_of(False, True)).astype(HALF)
        core_copy(1).start()
        summed = make(at.share_of(True, False))
        core_copy(0).wait_recv()
        y_out[...] = (summed + core_in[0].astype(FLOAT)).astype(HALF)
        y_copy.start()
        summed = make(at.share_of(False, False))
        core_copy(1).wait_recv()
        held[...] = summed + core_in[1].astype(FLOAT)
        between()
        y_copy.wait_recv()
        core_copy(0).wait_send()
        core_copy(1).wait_send()
        y_copy.wait_send()
        return held[...] + y_in[...].astype(FLOAT)

    bias_total = [jnp.zeros((1, hidden), FLOAT)]

    def make_two(block):
        value, bias = back_two(block)
        bias_total[0] = bias_total[0] + bias
        return value

    def inner_grads():
        packs[at.dp, 1:2, 0:hidden] = bias_total[0]
        loads["hid_b"].wait()

        def inner_grad_block(index, carry):
            whole_i[rows_at(index * 128, 128), :] = mm_tn(hid_b[:, lanes_at(index)], slope[...]).astype(HALF)
            return carry

        lax.fori_loop(0, width // 128, inner_grad_block, 0)
        for piece in list_i:
            scatter.start(piece)
        for piece in list_o[:2]:
            scatter.pass_on(piece)

    grad_hid_b = sum_shares(make_two, inner_grads, grad_mid)

    loads["middle"].wait()
    loads["branch"].wait()
    loads["ff_own"].wait()
    chosen = one_hot(own_rows, 2 * segs)
    normed, inv_std = layer_norm(middle[...])
    grad_normed = grad_hid_b * (1.0 + mm(chosen, modk[4]))
    first_mean = jnp.mean(grad_normed, axis=-1, keepdims=True)
    second_mean = jnp.mean(grad_normed * normed, axis=-1, keepdims=True)
    grad_mid[...] = cot_own[...].astype(FLOAT) + inv_std * (grad_normed - first_mean - normed * second_mean)
    grad_a[own_rows, :] = (grad_mid[...] * mm(chosen, modk[2])).astype(HALF)

    def hid_rows(other_y, other_core):
        return grad_a.at[rows_at(at.share_of(other_y, other_core) * share, share)]

    own_hid = hid_rows(False, False)
    to_core = remote(own_hid, own_hid, gat_send.at[0], gat_recv.at[0], at.core_peer())
    to_y = remote(own_hid, own_hid, gat_send.at[1], gat_recv.at[1], at.y_peer())
    to_y.start()
    to_core.start()
    across, beside, far = hid_rows(True, False), hid_rows(False, True), hid_rows(True, True)
    onward = remote(across, across, gat_send.at[2], gat_recv.at[2], at.core_peer())

    images = one_hot(own_rows, segs)

    def keep_mod(group, values):
        sums = image_sums(images, values)
        for t in range(at.tensor_count):
            mod_send_buf[t, group] = sums[:, t * columns:(t + 1) * columns]

    keep_mod(2, grad_mid[...] * branch[...])
    keep_mod(3, grad_hid_b)
    keep_mod(4, grad_hid_b * normed)
    mod_parts = ((2, 4), (0, 2))
    spread = Spread(
        at,
        [
            lambda source: mods.at[source, pl.ds(2, 4)],
            lambda source: mods.at[source, pl.ds(0, 2)],
            lambda source: packs.at[source],
            lambda source: picks.at[source],
        ],
        (all_z_send, all_z_recv), (all_x_send, all_x_recv),
    )

    def mod_copy(part_index, step):
        first, count = mod_parts[part_index]
        to = lax.rem(at.tensor + step, at.tensor_count)
        return remote(
            mod_send_buf.at[to, pl.ds(first, count)], mod_in.at[step - 1, pl.ds(first, count)],
            mod_send.at[part_index, step - 1], mod_recv.at[part_index, step - 1], at.tensor_peer(step),
        )

    def mod_start(part_index):
        for step in range(1, at.tensor_count):
            mod_copy(part_index, step).start()

    def mod_spread(part_index):
        first, count = mod_parts[part_index]
        total = mod_send_buf[at.tensor, first:first + count]
        for step in range(1, at.tensor_count):
            mod_copy(part_index, step).wait_recv()
            total = total + mod_in[step - 1, first:first + count]
        mods[at.dp, first:first + count] = total
        spread.start(part_index)

    window = min(tokens, share + 2 * SEG_MOST)
    key_sum[...] = jnp.zeros_like(key_sum)
    value_sum[...] = jnp.zeros_like(value_sum)

    def grad_att(block):
        rows = rows_at(block * share, share)
        values = mm_nt(grad_a[rows, :], wp[...])
        for head in range(nheads):
            gatt[head] = values[:, head * HD:(head + 1) * HD].astype(HALF)
        return jnp.sum(grad_a[rows, :].astype(FLOAT), axis=0, keepdims=True)

    def attend_back(block):
        start = block * share
        rows = rows_at(start, share)
        keys_at = pl.ds(pl.multiple_of(jnp.clip(start - SEG_MOST, 0, tokens - window), 128), window)

        def one_head(head, carry):
            query = heads[head, rows, :]
            keys = heads[nheads + head, keys_at, :]
            values = heads[2 * nheads + head, keys_at, :]
            grad = gatt[head]
            same = seg_col[rows, :] == seg_row[:, keys_at]
            scores = jnp.where(same, mm_nt(query, keys) * scale, -1e30)
            lanes = lax.broadcasted_iota(jnp.int32, (1, nheads), 1)
            peak = jnp.sum(jnp.where(lanes == head, lse[rows, :], 0.0), axis=-1, keepdims=True)
            probs = jnp.exp(scores - peak)
            grad_probs = mm_nt(grad, values)
            center = jnp.sum(probs * grad_probs, axis=-1, keepdims=True)
            grad_scores = (probs * (grad_probs - center)).astype(HALF)
            heads[head, rows, :] = (mm(grad_scores, keys) * scale).astype(HALF)
            key_sum[head, keys_at, :] += mm_tn(grad_scores, query)
            value_sum[head, keys_at, :] += mm_tn(probs.astype(HALF), grad)
            return carry

        lax.fori_loop(0, nheads, one_head, 0)

    loads["wp"].wait()
    loads["heads"].wait()
    loads["lse"].wait()
    for piece in list_o[2:]:
        scatter.pass_on(piece)
    grad_a_sum = grad_att(at.share_of(False, False))
    attend_back(at.share_of(False, False))
    remote(beside, beside, gat_send.at[0], gat_recv.at[0], at.core_peer()).wait_recv()
    grad_a_sum = grad_a_sum + grad_att(at.share_of(False, True))
    remote(across, across, gat_send.at[1], gat_recv.at[1], at.y_peer()).wait_recv()
    onward.start()
    attend_back(at.share_of(False, True))
    grad_a_sum = grad_a_sum + grad_att(at.share_of(True, False))
    scatter.pass_on(list_i[0])
    attend_back(at.share_of(True, False))
    remote(far, far, gat_send.at[2], gat_recv.at[2], at.core_peer()).wait_recv()
    grad_a_sum = grad_a_sum + grad_att(at.share_of(True, True))
    attend_back(at.share_of(True, True))
    for piece in list_i[1:2]:
        scatter.pass_on(piece)
    packs[at.dp, 2:3, 0:width] = grad_a_sum
    loads["att"].wait()
    proj_grad = mm_tn(att[...], grad_a[...]).astype(HALF)
    whole_p[...] = mm(place_back[...], proj_grad).astype(HALF)
    for piece in list_p:
        scatter.start(piece)
    to_core.wait_send()
    to_y.wait_send()
    onward.wait_send()

    def join_block(index, total):
        rows = rows_at(index * share, share)
        parts = [heads[head, rows, :].astype(FLOAT) for head in range(nheads)]
        parts += [(key_sum[head, rows, :] * scale).astype(HALF).astype(FLOAT) for head in range(nheads)]
        parts += [value_sum[head, rows, :].astype(HALF).astype(FLOAT) for head in range(nheads)]
        values = jnp.concatenate(parts, axis=1)
        grad_a[rows, 0:3 * columns] = values.astype(HALF)
        return total + jnp.sum(values, axis=0, keepdims=True)

    packs[at.dp, 0:1, 0:3 * columns] = lax.fori_loop(0, blocks, join_block, jnp.zeros((1, 3 * columns), FLOAT))
    for piece in list_i[2:]:
        scatter.pass_on(piece)
    loads["hid_a"].wait()

    def qkv_grad_block(index, carry):
        whole_q[rows_at(index * 128, 128), :] = mm_tn(act[:, lanes_at(index)], grad_a[:, 0:3 * columns]).astype(HALF)
        return carry

    lax.fori_loop(0, width // 128, qkv_grad_block, 0)
    for piece in list_q:
        scatter.start(piece)
    loads["wq"].wait()

    saves = []

    def save(src, dst):
        copy = pltpu.make_async_copy(src, dst, save_sem.at[len(saves)])
        copy.start()
        saves.append(copy)

    def mod_sums():
        for piece in list_p:
            scatter.pass_on(piece)
        ff_copy.wait_recv()
        branch_b = ff_own[...] + ff_in[...].astype(FLOAT) + shared_bias[1:2, :]
        keep_mod(5, cot_own[...].astype(FLOAT) * branch_b)
        ff_in[...] = (middle[...] + mm(chosen, modk[5]) * branch_b).astype(HALF)
        save(ff_in, block_out)
        mod_start(0)
        for part_index in (2, 3):
            spread.start(part_index)
        for piece in list_q[:len(list_q) // 3]:
            scatter.pass_on(piece)

    unit = lax.broadcasted_iota(jnp.int32, (segs, 1), 0) == lax.broadcasted_iota(jnp.int32, (1, segs), 1)
    conds = sizes["conds"]
    picks[at.dp, 0:segs, 0:conds] = mm_nt(unit.astype(FLOAT).astype(HALF), cond_picks(seg_cond, conds))
    grad_hid_a = sum_shares(
        lambda block: mm_nt(grad_a[rows_at(block * share, share), 0:3 * columns], wq[...]), mod_sums, branch
    )
    loads["x"].wait()
    normed, inv_std = layer_norm(x_own[...].astype(FLOAT))
    grad_normed = grad_hid_a * (1.0 + mm(chosen, modk[1]))
    first_mean = jnp.mean(grad_normed, axis=-1, keepdims=True)
    second_mean = jnp.mean(grad_normed * normed, axis=-1, keepdims=True)
    grad_mid[...] = grad_mid[...] + inv_std * (grad_normed - first_mean - normed * second_mean)
    save(grad_mid, input_out)
    mod_spread(0)
    keep_mod(0, grad_hid_a)
    keep_mod(1, grad_hid_a * normed)
    mod_start(1)
    for piece in list_q[len(list_q) // 3:]:
        scatter.pass_on(piece)
    for part_index in (2, 3, 0):
        spread.pass_on(part_index)
    mod_spread(1)
    spread.pass_on(1)
    outs = ((list_o, outer_out), (list_i, inner_out), (list_p, proj_out), (list_q, qkv_out))
    for pieces_of, out in outs:
        whole, x_in, z_in, shard = flat[pieces_of[0]][:4]
        for piece in pieces_of:
            scatter.arrive(piece)
        save(whole.at[rows_at((at.z * at.xs + at.x) * shard, shard)], out.at[0])
        for step in range(1, at.zs):
            save(z_in.at[step - 1], out.at[step])
    for part_index in range(4):
        spread.finish(part_index)
    save(mods, mods_out)
    save(packs, packs_out)
    save(picks, picks_out)
    ff_copy.wait_send()
    for piece in range(len(flat)):
        scatter.finish(piece)
    for part_index in range(2):
        for step in range(1, at.tensor_count):
            mod_copy(part_index, step).wait_send()
    for copy in saves:
        copy.wait()


def run_backward(sizes, block_input, seg_col, segment_ids, segment_cond, shared_biases, cotangent, kept):
    (wq, wp, wi, wo, hid_a, heads, lse, att, hid_b, act, slope, far, own, branch, middle, modk) = kept
    tokens, width, columns, share = (sizes[k] for k in ("tokens", "width", "columns", "share"))
    hidden, dp_count, tensor_count, segs = sizes["hidden"], sizes[DP], sizes[TP], sizes["segs"]
    nheads = columns // HD
    own_rows = columns // dp_count
    pad_rows = own_rows + -own_rows % 16
    xs = line_length(dp_count)
    zs = dp_count // xs
    shards = (hidden // dp_count, width // dp_count, pad_rows, width // dp_count)
    wholes = ((hidden, width), (width, hidden), (dp_count * pad_rows, width), (width, 3 * columns))
    units = sum(shard // unit_rows(shard) for shard in shards[:3]) + shards[3] // unit_rows(shards[3], LAST_UNIT)
    place = jnp.asarray(placing(columns, own_rows, pad_rows, dp_count).T, HALF)
    pack_width = max(width, hidden, 3 * columns)
    shapes = [((share, width), HALF), ((share, width), FLOAT)]
    shapes += [((zs, shards[i], wholes[i][1]), HALF) for i in (3, 2, 1, 0)]
    shapes += [((dp_count, 6, segs, columns), FLOAT), ((dp_count, 4, pack_width), FLOAT)]
    shapes += [((dp_count, 8, 128), FLOAT)]
    vmem, dma = pltpu.VMEM, pltpu.SemaphoreType.DMA
    scratch = [
        vmem((width, 3 * columns), HALF), vmem((columns, width), HALF), vmem((width, hidden), HALF),
        vmem((hidden, width), HALF), vmem((3 * nheads, tokens, HD), HALF), vmem((tokens, nheads), FLOAT),
        vmem((tokens, columns), HALF), vmem((tokens, width), HALF), vmem((tokens, hidden), HALF),
        vmem((tokens, hidden), HALF), vmem((tokens, width), HALF), vmem((6, 2 * segs, width), HALF),
        vmem((share, width), FLOAT), vmem((share, width), FLOAT), vmem((share, width), FLOAT),
        vmem((share, width), HALF), vmem((share, width), HALF), vmem((nheads, share, HD), HALF),
        vmem((nheads, tokens, HD), FLOAT), vmem((nheads, tokens, HD), FLOAT), vmem((tokens, width), HALF),
        vmem((2, share, width), HALF), vmem((2, share, width), HALF), vmem((share, width), HALF),
        vmem((share, width), HALF), vmem((share, width), HALF), vmem((share, width), FLOAT),
    ]
    scratch += [vmem(shape, HALF) for shape in wholes]
    scratch += [vmem((xs - 1, zs, shards[i], wholes[i][1]), HALF) for i in range(4)]
    scratch += [vmem((zs - 1, shards[i], wholes[i][1]), HALF) for i in range(4)]
    scratch += [
        vmem((tensor_count, 6, segs, columns), FLOAT), vmem((tensor_count - 1, 6, segs, columns), FLOAT),
        vmem((dp_count, 6, segs, columns), FLOAT), vmem((dp_count, 4, pack_width), FLOAT),
        vmem((dp_count, 8, 128), FLOAT),
        dma((17,)), dma((5 + 4 * zs,)), dma((units, xs - 1, zs)), dma((units, xs - 1, zs)),
        dma((units, zs - 1)), dma((units, zs - 1)), dma((3,)), dma((3,)), dma((3,)), dma((3,)),
        dma(()), dma(()), dma((2, tensor_count - 1)), dma((2, tensor_count - 1)),
        dma((4, zs - 1)), dma((4, zs - 1)), dma((4, zs, xs - 1)), dma((4, zs, xs - 1)),
    ]
    return pl.pallas_call(
        functools.partial(backward_kernel, sizes),
        out_shape=[jax.ShapeDtypeStruct(s, t) for s, t in shapes],
        in_specs=[vmem_spec()] * 5 + [any_spec()] * 18,
        out_specs=[any_spec()] * len(shapes),
        scratch_shapes=scratch,
        name="backward",
        compiler_params=pltpu.CompilerParams(
            collective_id=2, has_side_effects=True, vmem_limit_bytes=VMEM_BYTES
        ),
    )(
        seg_col, segment_ids, segment_cond, shared_biases, place, block_input, cotangent, wq, wp, wi, wo, hid_a, heads, lse, att, hid_b, act, slope, far, own,
        branch, middle, modk,
    )


def on_device_general(
    block_input,
    conditions,
    segment_ids,
    segment_cond,
    cotangent,
    qkv_weight,
    proj_weight,
    inner_weight,
    outer_weight,
    ada_weight,
    head_biases,
    inner_bias,
    shared_biases,
    qkv_first,
    proj_first,
    inner_first,
    outer_first,
    ada_first,
    head_biases_first,
    inner_bias_first,
    shared_biases_first,
    qkv_second,
    proj_second,
    inner_second,
    outer_second,
    ada_second,
    head_biases_second,
    inner_bias_second,
    shared_biases_second,
):
    columns = qkv_weight.shape[2]
    heads_local = columns // HD
    rows_local = segment_ids.shape[0]
    row_length = segment_ids.shape[1]
    token_count = rows_local * row_length
    seg_count = segment_cond.shape[1]
    width = block_input.shape[1]
    share_count = token_count // lax.axis_size(TP)
    share_start = lax.axis_index(TP) * share_count

    def share(values):
        return lax.dynamic_slice_in_dim(values, share_start, share_count, 0)

    qkv_full, proj_full, inner_full, outer_full = (
        lax.all_gather(qkv_weight.astype(HALF), DP, axis=0, tiled=True),
        lax.all_gather(proj_weight.astype(HALF), DP, axis=0, tiled=True),
        lax.all_gather(inner_weight.astype(HALF), DP, axis=0, tiled=True),
        lax.all_gather(outer_weight.astype(HALF), DP, axis=0, tiled=True),
    )
    condition_select = (
        segment_cond[:, :, None] == jnp.arange(conditions.shape[0])[None, None, :]
    ).astype(FLOAT)
    condition_row_block = jnp.einsum(
        "btu,ua->bta", condition_select, conditions, precision=PRECISION_MAX
    )
    cond_act = silu(condition_row_block)
    local_mod = (
        jnp.einsum("rsd,kcd->rskc", cond_act, ada_weight, precision=PRECISION_MAX)
        + head_biases[3:][None, None]
    )
    full_mod = lax.all_gather(local_mod, TP, axis=3, tiled=True)
    seg_pick = (segment_ids[:, :, None] == jnp.arange(seg_count)[None, None, :]).astype(FLOAT)
    token_mod = jnp.einsum("rls,rskd->rlkd", seg_pick, full_mod, precision=PRECISION_MAX).reshape(
        token_count, 6, width
    )
    inputs = block_input.astype(FLOAT)
    normed_one, inv_one = normalize(inputs)
    hidden_one = (normed_one * (1.0 + token_mod[:, 1]) + token_mod[:, 0]).astype(HALF)
    qkv_values = (
        jnp.einsum("nd,dkc->nkc", hidden_one, qkv_full, preferred_element_type=FLOAT)
        + head_biases[:3][None]
    ).astype(HALF)
    row_qkv = qkv_values.reshape(rows_local, row_length, 3, heads_local, HD)
    row = 0
    attended_row, total_row = attend_forward(row_qkv[row], segment_ids[row])
    attended_rows = [attended_row]
    total_rows = [total_row]
    attended = jnp.stack(attended_rows).reshape(token_count, columns).astype(HALF)
    attn_partial = jnp.dot(attended, proj_full, preferred_element_type=FLOAT)
    share_mod = share(token_mod)
    branch_one = sum_to_shares(attn_partial) + shared_biases[0]
    middle = share(inputs) + share_mod[:, 2] * branch_one
    normed_two, inv_two = normalize(middle)
    hidden_two_share = (normed_two * (1.0 + share_mod[:, 4]) + share_mod[:, 3]).astype(HALF)
    hidden_two = lax.all_gather(hidden_two_share, TP, axis=0, tiled=True)
    pre_act = jnp.dot(hidden_two, inner_full, preferred_element_type=FLOAT) + inner_bias
    act_values, gelu_back = jax.vjp(gelu_tanh, pre_act)
    act_low = act_values.astype(HALF)
    ff_partial = jnp.dot(act_low, outer_full, preferred_element_type=FLOAT)
    branch_two = sum_to_shares(ff_partial) + shared_biases[1]
    output = middle + share_mod[:, 5] * branch_two
    grad_out = cotangent.astype(FLOAT)
    grad_two = (grad_out * token_mod[:, 5]).astype(HALF)
    outer_grad = jnp.einsum("nf,nd->fd", act_low, grad_two, preferred_element_type=FLOAT)
    grad_act = jnp.einsum("nd,fd->nf", grad_two, outer_full, preferred_element_type=FLOAT)
    grad_pre = gelu_back(grad_act)[0].astype(HALF)
    inner_grad = jnp.einsum("nd,nf->df", hidden_two, grad_pre, preferred_element_type=FLOAT)
    back_two_partial = jnp.einsum("nf,df->nd", grad_pre, inner_full, preferred_element_type=FLOAT)
    grad_hidden_two = sum_to_shares(back_two_partial)
    grad_out_share = share(grad_out)
    grad_middle = grad_out_share + norm_back(
        grad_hidden_two * (1.0 + share_mod[:, 4]), normed_two, inv_two
    )
    grad_one_share = (grad_middle * share_mod[:, 2]).astype(HALF)
    grad_one = lax.all_gather(grad_one_share, TP, axis=0, tiled=True)
    proj_grad = jnp.einsum("nc,nd->cd", attended, grad_one, preferred_element_type=FLOAT)
    grad_attended = jnp.einsum(
        "nd,cd->nc", grad_one, proj_full, preferred_element_type=FLOAT
    ).astype(HALF)
    grad_rows = grad_attended.reshape(rows_local, row_length, heads_local, HD)
    row = 0
    grad_qkv_rows = [
        attend_backward(row_qkv[row], segment_ids[row], grad_rows[row], total_rows[row])
    ]
    grad_qkv = jnp.stack(grad_qkv_rows).reshape(token_count, 3, columns).astype(HALF)
    qkv_grad = jnp.einsum("nd,nkc->dkc", hidden_one, grad_qkv, preferred_element_type=FLOAT)
    back_one_partial = jnp.einsum("nkc,dkc->nd", grad_qkv, qkv_full, preferred_element_type=FLOAT)
    grad_hidden_one = sum_to_shares(back_one_partial)
    normed_one_share, inv_one_share = share(normed_one), share(inv_one)
    input_out = grad_middle + norm_back(
        grad_hidden_one * (1.0 + share_mod[:, 1]), normed_one_share, inv_one_share
    )
    block_out = output.astype(HALF)
    contributions = jnp.concatenate(
        [
            grad_hidden_one,
            grad_hidden_one * normed_one_share,
            grad_middle * branch_one,
            grad_hidden_two,
            grad_hidden_two * normed_two,
            grad_out_share * branch_two,
        ],
        axis=1,
    )
    pick_share = share(seg_pick.reshape(token_count, seg_count))
    cond_pick = jnp.dot(pick_share, condition_select[0], precision=PRECISION_MAX)
    cond_sums = jnp.einsum("lq,lc->qc", cond_pick, contributions, precision=PRECISION_MAX)
    cond_sums = cond_sums.reshape(-1, 6, lax.axis_size(TP), columns)
    cond_sums = lax.psum_scatter(cond_sums, TP, scatter_dimension=2, tiled=True)[:, :, 0]
    cond_total = lax.psum(cond_sums, DP)
    all_act, all_silu_back = jax.vjp(silu, conditions)
    grad_all_act = jnp.einsum("qkc,kcd->qd", cond_total, ada_weight, precision=PRECISION_MAX)
    cond_grad = all_silu_back(lax.psum(grad_all_act, TP))[0]
    head_bias_grad = jnp.sum(grad_qkv.astype(FLOAT), axis=0)
    inner_bias_grad = jnp.sum(grad_pre.astype(FLOAT), axis=0)
    shared_bias_grad = jnp.stack(
        [jnp.sum(grad_one.astype(FLOAT), axis=0), jnp.sum(grad_two.astype(FLOAT), axis=0)]
    )
    ada_total = jnp.einsum("qd,qkc->kcd", all_act, cond_total, precision=PRECISION_MAX)
    head_total, inner_bias_total, shared_total = lax.psum(
        (head_bias_grad, inner_bias_grad, shared_bias_grad), DP
    )
    head_total = jnp.concatenate([head_total, jnp.sum(cond_total, axis=0)], axis=0)
    qkv_shard, proj_shard, inner_shard, outer_shard = (
        sum_to_owners(qkv_grad),
        sum_to_owners(proj_grad),
        sum_to_owners(inner_grad),
        sum_to_owners(outer_grad),
    )
    qkv_new = adam_update(qkv_weight, qkv_shard, qkv_first, qkv_second, RATES[0])
    proj_new = adam_update(proj_weight, proj_shard, proj_first, proj_second, RATES[1])
    inner_new = adam_update(inner_weight, inner_shard, inner_first, inner_second, RATES[2])
    outer_new = adam_update(outer_weight, outer_shard, outer_first, outer_second, RATES[3])
    ada_new = adam_update(ada_weight, ada_total, ada_first, ada_second, RATES[4])
    head_new = adam_update(head_biases, head_total, head_biases_first, head_biases_second, RATES[5])
    inner_bias_new = adam_update(
        inner_bias, inner_bias_total, inner_bias_first, inner_bias_second, RATES[6]
    )
    shared_new = adam_update(
        shared_biases, shared_total, shared_biases_first, shared_biases_second, RATES[7]
    )
    return (
        block_out,
        input_out,
        cond_grad,
        qkv_new[0],
        proj_new[0],
        inner_new[0],
        outer_new[0],
        ada_new[0],
        head_new[0],
        inner_bias_new[0],
        shared_new[0],
        qkv_new[1],
        proj_new[1],
        inner_new[1],
        outer_new[1],
        ada_new[1],
        head_new[1],
        inner_bias_new[1],
        shared_new[1],
        qkv_new[2],
        proj_new[2],
        inner_new[2],
        outer_new[2],
        ada_new[2],
        head_new[2],
        inner_bias_new[2],
        shared_new[2],
        qkv_new[0].astype(HALF),
        proj_new[0].astype(HALF),
        inner_new[0].astype(HALF),
        outer_new[0].astype(HALF),
    )


def update_kernel(
    sizes,
    cond_ref, mods, packs, picks, head_w, head_m, head_v, hidden_w, hidden_m, hidden_v, shared_w, shared_m, shared_v,
    *refs,
):
    width, columns, segs, hidden = sizes["width"], sizes["columns"], sizes["segs"], sizes["hidden"]
    big_in = [refs[i * 4:i * 4 + 4] for i in range(4)]
    ada_in = refs[16:19]
    part, *small_out = refs[19:29]
    ada_out = refs[29:32]
    big_out = [refs[32 + i * 4:36 + i * 4] for i in range(4)]
    refs = refs[48:]
    ada = refs[:3]
    big = [refs[3 + i * 5:8 + i * 5] for i in range(4)]
    gt, act_rows, head_grad = refs[23:26]
    ada_load, ada_save, big_load, big_save = refs[26:]
    conds, dp_count = cond_ref.shape[0], sizes[DP]

    def ada_copy(kind, group):
        return pltpu.make_async_copy(ada_in[kind].at[group], ada[kind].at[group], ada_load.at[kind, group])

    for group in range(6):
        ada_copy(0, group).start()
    for group in range(6):
        ada_copy(1, group).start()
        ada_copy(2, group).start()
    big_loads = []
    for index in range(4):
        copies = [
            pltpu.make_async_copy(big_in[index][kind], big[index][kind], big_load.at[index, kind])
            for kind in range(4)
        ]
        for copy in copies:
            copy.start()
        big_loads.append(copies)

    act = silu(cond_ref[...])
    act_high, act_low = split_two(act)
    act_rows[...] = jnp.concatenate([act_high, act_high, act_low], axis=0)
    picked = jnp.concatenate(
        [picks[row, 0:segs, 0:conds] for row in range(dp_count)], axis=0
    ).astype(HALF)
    for group in range(6):
        images = jnp.concatenate([mods[row, group] for row in range(dp_count)], axis=0)
        head_grad[3 + group:4 + group, :] = jnp.sum(images, axis=0, keepdims=True)
        high, low = split_two(images)
        sums_high, sums_low = split_two(mm_tn(high, picked) + mm_tn(low, picked))
        gt[group] = jnp.concatenate([sums_high, sums_low, sums_high], axis=1)

    part[...] = jnp.zeros_like(part)
    for group in range(6):
        ada_copy(0, group).wait()
        weight_high, weight_low = split_two(ada[0][group])
        both = mm_tn(gt[group, :, 0:2 * conds], weight_high)
        part[...] += both[:conds] + both[conds:] + mm_tn(gt[group, :, 0:conds], weight_low)

    def update(values, rate, grad):
        weight, first, second = values
        return adam_update(weight, grad, first, second, rate)

    tile = 96 if columns % 96 == 0 else columns
    saves = []

    def ada_group(group):
        for kind in (1, 2):
            ada_copy(kind, group).wait()

        def ada_tile(index, carry):
            rows = pl.ds(pl.multiple_of(index * tile, 8), tile)
            grad = mm(gt[group, rows, :], act_rows[...])
            new = update([ref[group, rows, :] for ref in ada], RATES[4], grad)
            for ref, value in zip(ada, new, strict=True):
                ref[group, rows, :] = value
            return carry

        lax.fori_loop(0, columns // tile, ada_tile, 0)
        for kind in range(3):
            copy = pltpu.make_async_copy(ada[kind].at[group], ada_out[kind].at[group], ada_save.at[kind, group])
            copy.start()
            saves.append(copy)

    for group in range(6):
        ada_group(group)

    pack = packs[0]
    for row in range(1, dp_count):
        pack = pack + packs[row]
    for part_index in range(3):
        head_grad[part_index:part_index + 1, :] = pack[0:1, part_index * columns:(part_index + 1) * columns]
    smalls = (
        ((head_w, head_m, head_v), RATES[5], head_grad[...]),
        ((hidden_w, hidden_m, hidden_v), RATES[6], pack[1:2, 0:hidden].reshape(hidden_w.shape)),
        ((shared_w, shared_m, shared_v), RATES[7], pack[2:4, 0:width]),
    )
    for index, (kinds, rate, grad) in enumerate(smalls):
        for kind, value in enumerate(update([ref[...] for ref in kinds], rate, grad)):
            small_out[index * 3 + kind][...] = value

    for index in range(4):
        for copy in big_loads[index]:
            copy.wait()
        weight, first, second, grad, low = big[index]
        planes = weight.shape[0] if len(weight.shape) == 3 else 0
        for plane in range(max(planes, 1)):
            where = (plane,) if planes else (slice(0, weight.shape[0]),)
            lanes = weight.shape[-1]
            gradient = grad[0, :, plane * lanes:(plane + 1) * lanes].astype(FLOAT)
            for source in range(1, grad.shape[0]):
                gradient = gradient + grad[source, :, plane * lanes:(plane + 1) * lanes].astype(FLOAT)
            gradient = gradient[0:weight.shape[-2], :]
            new = update([ref[where] for ref in (weight, first, second)], RATES[index], gradient)
            for ref, value in zip((weight, first, second), new, strict=True):
                ref[where] = value
            low[where] = new[0].astype(HALF)
        for kind, ref in enumerate((weight, first, second, low)):
            copy = pltpu.make_async_copy(ref, big_out[index][kind], big_save.at[index, kind])
            copy.start()
            saves.append(copy)

    for copy in saves:
        copy.wait()


def run_update(sizes, conditions, mods, packs, picks, smalls, bigs, ada):
    width, columns, segs = sizes["width"], sizes["columns"], sizes["segs"]
    conds = conditions.shape[0]
    vmem, dma = pltpu.VMEM, pltpu.SemaphoreType.DMA
    flat_small = [array for kinds in smalls for array in kinds]
    flat_big = [array for kinds in bigs for array in kinds]

    def like(array, dtype=FLOAT):
        return jax.ShapeDtypeStruct(array.shape, dtype)

    outs = [like(conditions)] + [like(a) for a in flat_small] + [like(a) for a in ada]
    for weight, first, second, grad in bigs:
        outs += [like(weight), like(first), like(second), like(weight, HALF)]
    scratch = [vmem(array.shape, FLOAT) for array in ada]
    for kinds in bigs:
        scratch += [vmem(array.shape, array.dtype) for array in kinds] + [vmem(kinds[0].shape, HALF)]
    scratch += [
        vmem((6, columns, 3 * conds), HALF), vmem((3 * conds, width), HALF), vmem((9, columns), FLOAT),
        dma((3, 6)), dma((3, 6)), dma((4, 4)), dma((4, 4)),
    ]
    return pl.pallas_call(
        functools.partial(update_kernel, sizes),
        out_shape=outs,
        in_specs=[vmem_spec()] * 13 + [any_spec()] * 19,
        out_specs=[vmem_spec()] * 10 + [any_spec()] * 19,
        scratch_shapes=scratch,
        name="update",
        compiler_params=pltpu.CompilerParams(vmem_limit_bytes=VMEM_BYTES),
    )(conditions, mods, packs, picks, *flat_small, *flat_big, *ada)


def cond_kernel(sizes, cond_ref, part_in, cond_out, part, landing, result, out_send, out_recv, back_send, back_recv):
    at = Place(sizes[DP], sizes[TP])
    slice_rows = cond_ref.shape[0] // at.tensor_count
    part[...] = part_in[...]
    greet([at.tensor_peer(s) for s in range(1, at.tensor_count)])

    def slice_at(index):
        return pl.ds(pl.multiple_of(index * slice_rows, 8), slice_rows)

    def out_copy(step):
        to = lax.rem(at.tensor + step, at.tensor_count)
        return remote(
            part.at[slice_at(to)], landing.at[step - 1], out_send.at[step - 1], out_recv.at[step - 1],
            at.tensor_peer(step),
        )

    def back_copy(step, owner):
        rows = result.at[slice_at(owner)]
        return remote(rows, rows, back_send.at[step - 1], back_recv.at[step - 1], at.tensor_peer(step))

    for step in range(1, at.tensor_count):
        out_copy(step).start()

    total = part[slice_at(at.tensor), :]
    for step in range(1, at.tensor_count):
        out_copy(step).wait_recv()
        total = total + landing[step - 1]
    own = cond_ref[slice_at(at.tensor), :]
    gate = 1.0 / (1.0 + jnp.exp(-own))
    result[slice_at(at.tensor), :] = total * (gate * (1.0 + own * (1.0 - gate)))
    for step in range(1, at.tensor_count):
        back_copy(step, at.tensor).start()
    for step in range(1, at.tensor_count):
        back_copy(step, lax.rem(at.tensor + at.tensor_count - step, at.tensor_count)).wait_recv()
    cond_out[...] = result[...]
    for step in range(1, at.tensor_count):
        out_copy(step).wait_send()
        back_copy(step, at.tensor).wait_send()


def run_cond(sizes, conditions, part):
    tensor_count, vmem, dma = sizes[TP], pltpu.VMEM, pltpu.SemaphoreType.DMA
    shape = conditions.shape
    return pl.pallas_call(
        functools.partial(cond_kernel, sizes),
        out_shape=jax.ShapeDtypeStruct(shape, FLOAT),
        in_specs=[vmem_spec()] * 2,
        out_specs=vmem_spec(),
        scratch_shapes=[
            vmem(shape, FLOAT), vmem((tensor_count - 1, shape[0] // tensor_count, shape[1]), FLOAT),
            vmem(shape, FLOAT), *[dma((tensor_count - 1,))] * 4,
        ],
        name="cond",
        compiler_params=pltpu.CompilerParams(collective_id=3, has_side_effects=True),
    )(conditions, part)


def on_device_kernels(
    block_input, conditions, segment_ids, segment_cond, cotangent, qkv_weight, proj_weight, inner_weight,
    outer_weight, ada_weight, head_biases, inner_bias, shared_biases, *moments,
):
    firsts, seconds = moments[:8], moments[8:]
    sizes = sizes_of(block_input, conditions, segment_ids, segment_cond, qkv_weight, inner_weight)
    seg_col = segment_ids.reshape(-1, 1)

    def planes(array):
        return array.transpose(1, 0, 2)

    kept = run_forward(
        sizes, block_input, seg_col, segment_ids, segment_cond, conditions, ada_weight, head_biases, inner_bias,
        shared_biases, planes(qkv_weight), proj_weight, inner_weight, outer_weight,
    )
    block_out, input_out, *grads, mods, packs, picks = run_backward(
        sizes, block_input, seg_col, segment_ids, segment_cond, shared_biases, cotangent, kept
    )
    weights = (qkv_weight, proj_weight, inner_weight, outer_weight)
    bigs = [[w, m, v, g] for w, m, v, g in zip(weights, firsts[:4], seconds[:4], grads, strict=True)]
    bigs[0][:3] = [planes(array) for array in bigs[0][:3]]
    smalls = list(zip((head_biases, inner_bias, shared_biases), firsts[5:], seconds[5:], strict=True))
    cond_part, *news = run_update(
        sizes, conditions, mods, packs, picks, smalls, bigs, (ada_weight, firsts[4], seconds[4])
    )
    small_new, ada_new, big_new = news[:9], news[9:12], news[12:]
    big_new[:4] = [planes(array) for array in big_new[:4]]
    outs = [block_out, input_out, run_cond(sizes, conditions, cond_part)]
    for kind in range(3):
        outs += [big_new[4 * i + kind] for i in range(4)]
        outs += [ada_new[kind]] + [small_new[3 * i + kind] for i in range(3)]
    return (*outs, *big_new[3::4])


def on_device(*args):
    sizes = sizes_of(args[0], args[1], args[2], args[3], args[5], args[7])
    return (on_device_kernels if kernels_fit(sizes) else on_device_general)(*args)


def solution(mesh):
    in_specs = (
        P(DP, None),
        P(),
        P(DP, None),
        P(DP, None),
        P(DP, None),
        P(DP, None, TP),
        P((TP, DP), None),
        P(DP, TP),
        P((TP, DP), None),
        P(None, TP, None),
        P(None, TP),
        P(TP),
        P(),
        P(DP, None, TP),
        P((TP, DP), None),
        P(DP, TP),
        P((TP, DP), None),
        P(None, TP, None),
        P(None, TP),
        P(TP),
        P(),
        P(DP, None, TP),
        P((TP, DP), None),
        P(DP, TP),
        P((TP, DP), None),
        P(None, TP, None),
        P(None, TP),
        P(TP),
        P(),
    )
    out_specs = (
        P((DP, TP), None),
        P((DP, TP), None),
        P(),
        P(DP, None, TP),
        P((TP, DP), None),
        P(DP, TP),
        P((TP, DP), None),
        P(None, TP, None),
        P(None, TP),
        P(TP),
        P(),
        P(DP, None, TP),
        P((TP, DP), None),
        P(DP, TP),
        P((TP, DP), None),
        P(None, TP, None),
        P(None, TP),
        P(TP),
        P(),
        P(DP, None, TP),
        P((TP, DP), None),
        P(DP, TP),
        P((TP, DP), None),
        P(None, TP, None),
        P(None, TP),
        P(TP),
        P(),
        P(DP, None, TP),
        P((TP, DP), None),
        P(DP, TP),
        P((TP, DP), None),
    )
    return jax.shard_map(
        on_device, mesh=mesh, in_specs=in_specs, out_specs=out_specs, check_vma=False
    )
```
